32 devices in a mesh: clip: 2 (over core), ctx: 4 (over z), head: 4 (over y, x).
Axes of the slice: x: 2, y: 2, z: 4, core: 2. Of those that a mesh axis runs over, the one named last changes fastest.
Arguments:
- queries: bfloat16 [1792, 5120], P(('clip', 'ctx', 'head')), parts along dimension 0, may hold values from -6 to 6
- keys_in: bfloat16 [1792, 5120], P(('clip', 'ctx', 'head')), parts along dimension 0, may hold values from -6 to 6
- values_in: bfloat16 [1792, 5120], P(('clip', 'ctx', 'head')), parts along dimension 0, may hold values from -6 to 6
- attn_out: bfloat16 [1792, 5120], P(('clip', 'ctx', 'head')), parts along dimension 0, may hold values from -6 to 6
- out_grad: bfloat16 [1792, 5120], P(('clip', 'ctx', 'head')), parts along dimension 0, may hold values from -192 to 192
- log_norm: float32 [1792, 40], P(('clip', 'ctx'), 'head'), parts along dimension 0, may hold values from -1 to 12
- span_id: int32 [1792], P(('clip', 'ctx', 'head')), parts along dimension 0, may hold values from 0 to 11, as said below
Outputs:
- query_grad: bfloat16 [1792, 5120], P(('clip', 'ctx', 'head')), parts along dimension 0
- key_grad: bfloat16 [1792, 5120], P(('clip', 'ctx', 'head')), parts along dimension 0
- value_grad: bfloat16 [1792, 5120], P(('clip', 'ctx', 'head')), parts along dimension 0
The draws below stay inside these ranges and needn't reach their ends.
There are 2 independent parts, one for each index of `clip`. The reference program is written for one: setup_inputs(seed, part) draws one part's arguments, and reference() takes and returns one part's arrays. A program takes and returns all parts, laid end to end along the dimension named above; each array names one. Nothing has to cross between parts.
Inputs may be any that keep to these rules, and one draw needn't show every extreme that they name: span_id[i] = (i + o) // 75 for one offset o per clip, 0 <= o <= 4: spans of 75 tokens, the first one entered partway.
All inputs are finite; a program needn't handle non-finite values.
Results may differ from the reference program's by a relative error of at most 0.007.
Values may be sent and summed in bfloat16 or wider, within the bound.
No kernel may reach another device: no remote copies, remote signals or barrier semaphores. Data moves between devices by JAX's collectives and lax.ppermute only.
A program may use at most 128 MiB of HBM per device.

```python
import jax
import jax.numpy as jnp
from jax import lax

H = 40
DH = 128
SEG = 224
SPANS = 12
TOKENS = 896
SPAN_LEN = 75
N_CTX = 4


def span_helper(key):
    offset_key = jax.random.fold_in(key, 7)
    slack = SPANS * SPAN_LEN - TOKENS
    offset = jax.random.randint(offset_key, (), 0, slack + 1, dtype=jnp.int32)
    positions = jnp.arange(TOKENS, dtype=jnp.int32)
    return ((positions + offset) // SPAN_LEN).astype(jnp.int32)


def draw_span_id(key, part):
    return span_helper(key)


def draw_log_norm(key, part):
    span_of = span_helper(key)
    onehot = (span_of[:, None] == jnp.arange(SPANS, dtype=jnp.int32)[None, :]).astype(jnp.int32)
    counts = jnp.sum(onehot, axis=0)
    ends = jnp.cumsum(counts)
    visible = jnp.sum(onehot * ends[None, :], axis=1)
    noise_key = jax.random.fold_in(key, 11)
    noise = jax.random.uniform(noise_key, (TOKENS, H), jnp.float32, -0.4, 0.4)
    return jnp.log(visible.astype(jnp.float32))[:, None] + 0.5 + noise


def block_scale(stream_key, shape, pieces, smallest, top_value):
    gain = 1.0
    for dim, shards_of in pieces:
        draws = jax.random.uniform(jax.random.fold_in(jax.random.fold_in(stream_key, 6), dim), (shards_of,), jnp.float32, smallest / len(pieces), top_value / len(pieces))
        gain = gain * jnp.repeat(jnp.exp(draws), shape[dim] // shards_of).reshape((-1,) + (1,) * (len(shape) - 1 - dim))
    return gain


def scatter_about(key, dims, spread, bound, pieces=(), held_as=jnp.bfloat16):
    values = jax.random.normal(key, dims, jnp.float32) * spread
    if len(pieces) > 0:
        values = block_scale(key, dims, pieces, -0.22, 0.18) * values
    return jnp.clip(values, min=-bound, max=bound).astype(held_as)


def setup_inputs(seed: int = 0, part: int = 0) -> dict:
    key_list = jax.random.split(jax.random.key(seed), 8)
    own_keys = jax.random.split(jax.random.fold_in(key_list[7], part), 8)
    queries = scatter_about(own_keys[0], (TOKENS, H * DH), 1.0, 6.0, ((0, 16),))
    keys_in = scatter_about(own_keys[1], (TOKENS, H * DH), 1.0, 6.0, ((0, 16),))
    values_in = scatter_about(own_keys[2], (TOKENS, H * DH), 1.0, 6.0, ((0, 16),))
    attn_out = scatter_about(own_keys[3], (TOKENS, H * DH), 1.0, 6.0, ((0, 16),))
    out_grad = scatter_about(own_keys[4], (TOKENS, H * DH), 32.0, 192.0, ((0, 16),))
    log_norm = draw_log_norm(jax.random.fold_in(jax.random.fold_in(key_list[7], part), 71), part)
    span_id = draw_span_id(jax.random.fold_in(jax.random.fold_in(key_list[7], part), 71), part)
    return dict(queries=queries, keys_in=keys_in, values_in=values_in, attn_out=attn_out, out_grad=out_grad, log_norm=log_norm, span_id=span_id)


def pair_terms(query_blk, grad_blk, norm_blk, delta_blk, query_ids, key_blk, value_blk, key_ids):
    scale = 1.0 / (DH ** 0.5)
    scores = jnp.einsum('rhd,khd->hrk', query_blk, key_blk)
    visible = key_ids[None, :] <= query_ids[:, None]
    weight = jnp.where(visible[None], jnp.exp(scores * scale - norm_blk.T[:, :, None]), 0.0)
    weight_low = weight.astype(jnp.bfloat16).astype(jnp.float32)
    dweight = jnp.einsum('rhd,khd->hrk', grad_blk, value_blk)
    dscore = (weight * (dweight - delta_blk.T[:, :, None]) * scale).astype(jnp.bfloat16).astype(jnp.float32)
    query_term = jnp.einsum('hrk,khd->rhd', dscore, key_blk)
    key_term = jnp.einsum('hrk,rhd->khd', dscore, query_blk)
    value_term = jnp.einsum('hrk,rhd->khd', weight_low, grad_blk)
    return query_term, key_term, value_term


def reference(queries, keys_in, values_in, attn_out, out_grad, log_norm, span_id):
    def blocks(array):
        return array.astype(jnp.float32).reshape(N_CTX, SEG, H, DH)

    query_all = blocks(queries)
    key_all = blocks(keys_in)
    value_all = blocks(values_in)
    grad_all = blocks(out_grad)
    delta = jnp.sum(grad_all * blocks(attn_out), axis=3)
    norm_all = log_norm.reshape(N_CTX, SEG, H)
    id_all = span_id.reshape(N_CTX, SEG)

    def outer(carry, query_side):
        key_total, value_total = carry
        query_blk, grad_blk, norm_blk, delta_blk, query_ids = query_side

        def inner(dq_total, key_side):
            key_blk, value_blk, key_ids = key_side
            query_term, key_term, value_term = pair_terms(query_blk, grad_blk, norm_blk, delta_blk, query_ids, key_blk, value_blk, key_ids)
            dq_total = dq_total + lax.optimization_barrier(query_term.astype(jnp.bfloat16)).astype(jnp.float32)
            return dq_total, (key_term.astype(jnp.bfloat16), value_term.astype(jnp.bfloat16))

        dq_total, (key_terms, value_terms) = lax.scan(inner, jnp.zeros((SEG, H, DH), jnp.float32), (key_all, value_all, id_all))
        key_total = key_total + key_terms.astype(jnp.float32)
        value_total = value_total + value_terms.astype(jnp.float32)
        return (key_total, value_total), dq_total.astype(jnp.bfloat16)

    start = jnp.zeros((N_CTX, SEG, H, DH), jnp.float32)
    (key_total, value_total), dq_blocks = lax.scan(outer, (start, start), (query_all, grad_all, norm_all, delta, id_all))
    query_grad = dq_blocks.reshape(N_CTX * SEG, H * DH)
    key_grad = key_total.reshape(N_CTX * SEG, H * DH).astype(jnp.bfloat16)
    value_grad = value_total.reshape(N_CTX * SEG, H * DH).astype(jnp.bfloat16)
    return (query_grad, key_grad, value_grad)
```

```python
import math

import jax
import jax.numpy as jnp
from jax import lax
from jax.experimental import pallas as pl
from jax.experimental.pallas import tpu as pltpu
from jax.sharding import PartitionSpec as P

SPANS = 12
EDGE = 16
LANES = 128
BF16 = jnp.bfloat16
F32 = jnp.float32

INWARD = ((0, 1), (3, 2))
SWAP = ((1, 2), (2, 1))
OUTWARD = ((1, 0), (2, 3))
DOWN = ((1, 0), (2, 1), (3, 2))
UP = ((0, 1), (1, 2), (2, 3))


def tile_terms(query_blk, grad_blk, norm_blk, delta_blk, query_ids, key_blk, value_blk, key_ids):
    row_count = query_blk.shape[0]
    key_count = key_blk.shape[0]
    head_count = norm_blk.shape[1]
    head_width = query_blk.shape[1] // head_count
    scale = 1.0 / math.sqrt(head_width)
    query3 = query_blk.reshape(row_count, head_count, head_width)
    grad3 = grad_blk.reshape(row_count, head_count, head_width)
    key3 = key_blk.reshape(key_count, head_count, head_width)
    value3 = value_blk.reshape(key_count, head_count, head_width)
    scores = jnp.einsum("rhd,khd->hrk", query3, key3, preferred_element_type=jnp.float32)
    visible = key_ids[None, :] <= query_ids[:, None]
    weight = jnp.where(visible[None], jnp.exp(scores * scale - norm_blk.T[:, :, None]), 0.0)
    weight_low = weight.astype(jnp.bfloat16)
    dweight = jnp.einsum("rhd,khd->hrk", grad3, value3, preferred_element_type=jnp.float32)
    dscore = (weight * (dweight - delta_blk.T[:, :, None]) * scale).astype(jnp.bfloat16)
    query_term = jnp.einsum("hrk,khd->rhd", dscore, key3, preferred_element_type=jnp.float32)
    key_term = jnp.einsum("hrk,rhd->khd", dscore, query3, preferred_element_type=jnp.float32)
    value_term = jnp.einsum("hrk,rhd->khd", weight_low, grad3, preferred_element_type=jnp.float32)
    return (
        query_term.reshape(row_count, -1),
        key_term.reshape(key_count, -1),
        value_term.reshape(key_count, -1),
    )


def rounded(term):
    return lax.optimization_barrier(term.astype(jnp.bfloat16)).astype(jnp.float32)


def local_plain(queries, keys_in, values_in, attn_out, out_grad, log_norm, span_id):
    local_q, local_k, local_v, local_out, local_grad = (
        lax.all_to_all(queries, "head", split_axis=1, concat_axis=0, tiled=True),
        lax.all_to_all(keys_in, "head", split_axis=1, concat_axis=0, tiled=True),
        lax.all_to_all(values_in, "head", split_axis=1, concat_axis=0, tiled=True),
        lax.all_to_all(attn_out, "head", split_axis=1, concat_axis=0, tiled=True),
        lax.all_to_all(out_grad, "head", split_axis=1, concat_axis=0, tiled=True),
    )
    all_ids = lax.all_gather(span_id, ("ctx", "head"), axis=0, tiled=True)
    seg_rows = local_q.shape[0]
    block_count = lax.axis_size("ctx")
    head_count = log_norm.shape[1]
    head_width = local_q.shape[1] // head_count
    my_block = lax.axis_index("ctx")
    own_ids = lax.dynamic_slice_in_dim(all_ids, my_block * seg_rows, seg_rows)
    id_blocks = all_ids.reshape(block_count, seg_rows)
    deltas = jnp.sum(
        (local_grad.astype(jnp.float32) * local_out.astype(jnp.float32)).reshape(
            seg_rows, head_count, head_width
        ),
        axis=2,
    )
    far_queries, far_grads = (
        lax.all_gather(local_q, "ctx", axis=0, tiled=True),
        lax.all_gather(local_grad, "ctx", axis=0, tiled=True),
    )
    far_norms, far_deltas = (
        lax.all_gather(log_norm, "ctx", axis=0, tiled=True),
        lax.all_gather(deltas, "ctx", axis=0, tiled=True),
    )

    def query_step(totals, piece):
        query_blk, grad_blk, norm_blk, delta_blk, query_ids = piece
        query_term, key_term, value_term = tile_terms(
            query_blk, grad_blk, norm_blk, delta_blk, query_ids, local_k, local_v, own_ids
        )
        return ((totals[0] + rounded(key_term), totals[1] + rounded(value_term)), query_term)

    zero_block = jnp.zeros(local_k.shape, jnp.float32)
    (dk_total, dv_total), query_terms = lax.scan(
        query_step,
        (zero_block, zero_block),
        (
            far_queries.reshape(block_count, seg_rows, -1),
            far_grads.reshape(block_count, seg_rows, -1),
            far_norms.reshape(block_count, seg_rows, -1),
            far_deltas.reshape(block_count, seg_rows, -1),
            id_blocks,
        ),
    )
    query_sum = lax.psum_scatter(
        query_terms.reshape(block_count * seg_rows, -1).astype(jnp.bfloat16),
        "ctx",
        scatter_dimension=0,
        tiled=True,
    )
    dk_local = dk_total.astype(jnp.bfloat16)
    dv_local = dv_total.astype(jnp.bfloat16)
    query_grad, key_grad, value_grad = (
        lax.all_to_all(query_sum, "head", split_axis=0, concat_axis=1, tiled=True),
        lax.all_to_all(dk_local, "head", split_axis=0, concat_axis=1, tiled=True),
        lax.all_to_all(dv_local, "head", split_axis=0, concat_axis=1, tiled=True),
    )
    return (query_grad, key_grad, value_grad)


def nt(a, b):
    return lax.dot_general(a, b, (((1,), (1,)), ((), ())), preferred_element_type=F32)


def tn(a, b):
    return lax.dot_general(a, b, (((0,), (0,)), ((), ())), preferred_element_type=F32)


def pieces(value):
    high = value.astype(BF16)
    rest = value - high.astype(F32)
    middle = rest.astype(BF16)
    low = (rest - middle.astype(F32)).astype(BF16)
    return high, middle, low


def run_copies(pairs, sems, first=0):
    made = [pltpu.make_async_copy(src, dst, sems.at[first + i]) for i, (src, dst) in enumerate(pairs)]
    for copy in made:
        copy.start()
    return made


def wait_all(made):
    for copy in made:
        copy.wait()


def anywhere(count):
    return [pl.BlockSpec(memory_space=pl.ANY)] * count


def pack(queries, keys_in, values_in, attn_out, out_grad, span_row, groups, width):
    rows = queries.shape[0]
    heads = width // LANES
    half = width // 2

    def body(q, k, v, o, g, ids, x1, x2, x3, o_v, g_v, meta, sems):
        low = lax.axis_index("ctx") < 2
        loads = run_copies([(o, o_v), (g, g_v)], sems)

        def moves(first, second, third, fourth, near, far):
            todo = []
            for h in range(groups):
                base = h * width
                todo.append((first.at[:, pl.ds(base + near, half)], x1.at[h, :, pl.ds(0, half)]))
                todo.append((second.at[:, pl.ds(base + near, half)], x1.at[h, :, pl.ds(half, half)]))
                todo.append((first.at[:, pl.ds(base + far, half)], x2.at[h, :, pl.ds(0, half)]))
                todo.append((second.at[:, pl.ds(base + far, half)], x2.at[h, :, pl.ds(half, half)]))
                todo.append((third.at[:, pl.ds(base, width)], x3.at[h, :, pl.ds(0, width)]))
                todo.append((fourth.at[:, pl.ds(base, width)], x3.at[h, :, pl.ds(width, width)]))
            return todo

        count = 6 * groups

        @pl.when(low)
        def _():
            run_copies(moves(k, v, q, g, half, 0), sems, 2)

        @pl.when(jnp.logical_not(low))
        def _():
            run_copies(moves(q, g, k, v, 0, half), sems, 2)

        wait_all(loads)
        lane = lax.broadcasted_iota(jnp.int32, (rows, LANES), 1)
        slot = jnp.where(lane < 3 * heads, lane % heads, -1)
        at_row = lax.broadcasted_iota(jnp.int32, (rows, rows), 0)
        at_col = lax.broadcasted_iota(jnp.int32, (rows, rows), 1)
        own = jnp.sum(jnp.where(at_row == at_col, ids[...].astype(F32), 0.0), axis=1, keepdims=True)
        for h in range(groups):
            total = jnp.zeros((rows, LANES), F32)
            for c in range(heads):
                cols = pl.ds(h * width + c * LANES, LANES)
                delta = jnp.sum(o_v[:, cols].astype(F32) * g_v[:, cols].astype(F32), axis=1, keepdims=True)
                total = jnp.where(slot == c, delta, total)
            high, middle, lowest = pieces(total)
            kept = jnp.where(lane < heads, high, jnp.where(lane < 2 * heads, middle, lowest))
            meta[h] = jnp.where(lane < 3 * heads, kept, jnp.where(lane == 3 * heads, own.astype(BF16), 0.0).astype(BF16))
        last = run_copies([(meta, x1.at[:, :, pl.ds(width, LANES)])], sems, 2 + count)

        @pl.when(low)
        def _():
            wait_all(
                [
                    pltpu.make_async_copy(src, dst, sems.at[2 + i])
                    for i, (src, dst) in enumerate(moves(k, v, q, g, half, 0))
                ]
            )

        @pl.when(jnp.logical_not(low))
        def _():
            wait_all(
                [
                    pltpu.make_async_copy(src, dst, sems.at[2 + i])
                    for i, (src, dst) in enumerate(moves(q, g, k, v, 0, half))
                ]
            )

        wait_all(last)

    return pl.pallas_call(
        body,
        out_shape=[
            jax.ShapeDtypeStruct((groups, rows, width + LANES), BF16),
            jax.ShapeDtypeStruct((groups, rows, width), BF16),
            jax.ShapeDtypeStruct((groups, rows, 2 * width), BF16),
        ],
        in_specs=anywhere(5) + [pl.BlockSpec(memory_space=pltpu.VMEM)],
        out_specs=anywhere(3),
        scratch_shapes=[
            pltpu.VMEM((rows, groups * width), BF16),
            pltpu.VMEM((rows, groups * width), BF16),
            pltpu.VMEM((groups, rows, LANES), BF16),
            pltpu.SemaphoreType.DMA((3 + 6 * groups,)),
        ],
        cost_estimate=pl.CostEstimate(flops=0, bytes_accessed=10 * rows * groups * width * 2, transcendentals=0),
        name="pack",
    )(queries, keys_in, values_in, attn_out, out_grad, span_row)


def add_norm(payload, norm_rows):
    rows, width = payload.shape
    heads = norm_rows.shape[0]
    block = pl.BlockSpec((rows, LANES), lambda i: (0, width // LANES - 1))

    def body(x, norm, y):
        at_row = lax.broadcasted_iota(jnp.int32, (heads, LANES), 0)
        at_lane = lax.broadcasted_iota(jnp.int32, (heads, LANES), 1)
        total = x[...].astype(F32)
        for i, piece in enumerate(pieces(norm[...])):
            place = jnp.where(at_lane == at_row + (3 * heads + 1 + i * heads), 1.0, 0.0).astype(BF16)
            total += tn(piece, place)
        y[...] = total.astype(BF16)

    return pl.pallas_call(
        body,
        grid=(1,),
        out_shape=jax.ShapeDtypeStruct(payload.shape, BF16),
        in_specs=[block, pl.BlockSpec((heads, rows), lambda i: (0, 0))],
        out_specs=block,
        input_output_aliases={0: 0},
        cost_estimate=pl.CostEstimate(flops=0, bytes_accessed=4 * rows * LANES, transcendentals=0),
        name="add_norm",
    )(payload, norm_rows)


def token_rows(meta, heads):
    at_row = lax.broadcasted_iota(jnp.int32, (32, LANES), 0)
    at_lane = lax.broadcasted_iota(jnp.int32, (32, LANES), 1)
    norm_lane = at_lane - (3 * heads + 1)
    is_norm = (norm_lane >= 0) & (norm_lane < 3 * heads) & (norm_lane % heads == at_row) & (at_row < heads)
    is_delta = (at_lane < 3 * heads) & (at_lane % heads == at_row - heads) & (at_row >= heads)
    is_id = (at_lane == 3 * heads) & (at_row == 2 * heads)
    chosen = jnp.where(is_norm | is_delta | is_id, 1.0, 0.0).astype(BF16)
    return nt(chosen, meta)


def pair_terms(query, grad, key, value, norm, delta, visible=None):
    scale = 1.0 / math.sqrt(query.shape[1])
    weight = jnp.exp(nt(key, query) * scale - norm)
    if visible is not None:
        weight = jnp.where(visible, weight, 0.0)
    dscore = (weight * (nt(value, grad) - delta) * scale).astype(BF16)
    value_term = jnp.dot(weight.astype(BF16), grad, preferred_element_type=F32)
    key_term = jnp.dot(dscore, query, preferred_element_type=F32)
    query_term = tn(dscore, key)
    return query_term, key_term, value_term


def far_pairs(y1, y2, w, r1, r2, s1, s2):
    rows, width = y2.shape
    half = width // 2
    count = half // LANES
    heads = 2 * count

    def body(y1, y2, w, r1, r2, s1, s2, swap1, out1, swap2, l1, l2, l3, buf, grads, meta, info, sems):
        z = lax.axis_index("ctx")
        one = z == 1

        def pick(a, b):
            return jnp.where(one, a, b)

        @pl.when((z == 1) | (z == 2))
        def _():
            near = pl.multiple_of(pick(0, half), LANES)
            other = pl.multiple_of(pick(half, 0), LANES)
            main = pl.ds(0, width)
            tail = pl.ds(width, LANES)
            left, right = pl.ds(0, half), pl.ds(half, half)
            made = run_copies(
                [
                    (y1.at[:, tail], meta.at[pick(2, 0)]),
                    (s1.at[:, tail], meta.at[pick(0, 3)]),
                    (s2.at[:, tail], meta.at[pick(1, 4)]),
                    (r1.at[:, tail], meta.at[pick(3, 1)]),
                    (s1.at[:, main], buf.at[pick(0, 3)]),
                    (s2.at[:, main], buf.at[pick(1, 2)]),
                    (r2, buf.at[pick(2, 1)]),
                    (y2, buf.at[pick(3, 0)]),
                    (w.at[:, pl.ds(near, half)], buf.at[4, :, left]),
                    (w.at[:, pl.ds(width + near, half)], buf.at[4, :, right]),
                    (w.at[:, pl.ds(other, half)], buf.at[5, :, left]),
                    (w.at[:, pl.ds(width + other, half)], buf.at[5, :, right]),
                    (r1.at[:, main], buf.at[6]),
                ],
                sems,
            )
            wait_all(made)
            for i in range(3):
                info[i] = token_rows(meta[i], heads)
            first_active = pick(0, count)
            first_other = pick(count, 0)
            zero = jnp.zeros((rows, LANES), BF16)

            def single(q_slot, k_slot, c, head):
                a = pl.ds(pl.multiple_of(c * LANES, LANES), LANES)
                b = pl.ds(pl.multiple_of(half + c * LANES, LANES), LANES)
                own = pick(2, 1)
                return pair_terms(
                    buf[q_slot, :, a],
                    buf[q_slot, :, b],
                    buf[k_slot, :, a],
                    buf[k_slot, :, b],
                    info[own, pl.ds(head, 1), :],
                    info[own, pl.ds(heads + head, 1), :],
                )

            def step(c, carry):
                a = pl.ds(pl.multiple_of(c * LANES, LANES), LANES)
                b = pl.ds(pl.multiple_of(half + c * LANES, LANES), LANES)
                head = first_active + c
                extra_q, extra_k, extra_v = single(pick(4, 1), pick(2, 4), c, head)
                key = buf[2:4, :, a].reshape(2 * rows, LANES)
                value = buf[2:4, :, b].reshape(2 * rows, LANES)
                key_sum, value_sum = None, None
                for i in range(2):
                    query_term, key_term, value_term = pair_terms(
                        buf[i, :, a],
                        buf[i, :, b],
                        key,
                        value,
                        info[i, pl.ds(head, 1), :],
                        info[i, pl.ds(heads + head, 1), :],
                    )
                    if i == 1:
                        query_term += jnp.where(one, 0.0, extra_q)
                    grads[i, :, a] = query_term.astype(BF16)
                    grads[i, :, b] = zero
                    key_sum = key_term if i == 0 else key_sum + key_term
                    value_sum = value_term if i == 0 else value_sum + value_term
                grads[2, :, a] = (key_sum[:rows] + jnp.where(one, extra_k, 0.0)).astype(BF16)
                grads[2, :, b] = (value_sum[:rows] + jnp.where(one, extra_v, 0.0)).astype(BF16)
                grads[3, :, a] = key_sum[rows:].astype(BF16)
                grads[3, :, b] = value_sum[rows:].astype(BF16)
                grads[4, :, a] = jnp.where(one, extra_q, extra_k).astype(BF16)
                grads[4, :, b] = jnp.where(one, 0.0, extra_v).astype(BF16)
                extra_q, extra_k, extra_v = single(pick(5, 6), pick(6, 5), c, first_other + c)
                grads[5, :, a] = jnp.where(one, extra_q, extra_k).astype(BF16)
                grads[5, :, b] = jnp.where(one, 0.0, extra_v).astype(BF16)
                grads[6, :, a] = jnp.where(one, extra_k, extra_q).astype(BF16)
                grads[6, :, b] = jnp.where(one, extra_v, 0.0).astype(BF16)
                return carry

            lax.fori_loop(0, count, step, 0)
            made = run_copies(
                [
                    (grads.at[pick(1, 2)], swap1),
                    (grads.at[pick(2, 1)], out1),
                    (grads.at[pick(0, 3)], swap2),
                    (grads.at[pick(3, 0)], l2),
                    (grads.at[6], l3),
                    (grads.at[4, :, left], l1.at[:, pl.ds(near, half)]),
                    (grads.at[4, :, right], l1.at[:, pl.ds(width + near, half)]),
                    (grads.at[5, :, left], l1.at[:, pl.ds(other, half)]),
                    (grads.at[5, :, right], l1.at[:, pl.ds(width + other, half)]),
                ],
                sems,
            )
            wait_all(made)

    single_shape = jax.ShapeDtypeStruct((rows, width), BF16)
    return pl.pallas_call(
        body,
        out_shape=[
            single_shape,
            single_shape,
            single_shape,
            jax.ShapeDtypeStruct((rows, 2 * width), BF16),
            single_shape,
            single_shape,
        ],
        in_specs=anywhere(7),
        out_specs=anywhere(6),
        scratch_shapes=[
            pltpu.VMEM((7, rows, width), BF16),
            pltpu.VMEM((7, rows, width), BF16),
            pltpu.VMEM((5, rows, LANES), BF16),
            pltpu.VMEM((3, 32, rows), F32),
            pltpu.SemaphoreType.DMA((13,)),
        ],
        compiler_params=pltpu.CompilerParams(vmem_limit_bytes=40 * 2**20),
        cost_estimate=pl.CostEstimate(
            flops=30 * 10 * rows * rows * LANES, bytes_accessed=30 * rows * width, transcendentals=30 * rows * rows
        ),
        name="far_pairs",
    )(y1, y2, w, r1, r2, s1, s2)


def near_pairs(y1, y2, w, key_edge, query_edge):
    rows, width = y2.shape
    half = width // 2
    count = half // LANES
    heads = 2 * count
    total = rows + EDGE

    def body(y1, y2, w, kedge, qedge, dw, dy1, dy2, dkedge, dqedge, qbuf, kbuf, dq, dk, kmeta, qmeta, info, sems):
        low = lax.axis_index("ctx") < 2
        left, right = pl.ds(0, half), pl.ds(half, half)
        own, past = pl.ds(0, rows), pl.ds(rows, EDGE)
        main = pl.ds(0, width)

        def halves(array, there, back=False):
            todo = []
            for i in range(2):
                for j in range(array.shape[1] // width):
                    wide = array.at[:, pl.ds(j * width + i * half, half)]
                    narrow = there(i, right if j else left)
                    todo.append((narrow, wide) if back else (wide, narrow))
            return todo

        shared = run_copies(
            [
                (y1.at[:, pl.ds(width, LANES)], kmeta.at[own]),
                (y1.at[:, pl.ds(width, LANES)], qmeta.at[own]),
                (kedge.at[:, pl.ds(2 * width, LANES)], kmeta.at[past]),
                (qedge.at[:, pl.ds(2 * width, LANES)], qmeta.at[past]),
            ]
            + halves(kedge, lambda i, cols: kbuf.at[i, past, cols])
            + halves(qedge, lambda i, cols: qbuf.at[i, past, cols]),
            sems,
        )

        @pl.when(low)
        def _():
            todo = halves(w, lambda i, cols: qbuf.at[i, own, cols])
            todo += [(y2, kbuf.at[0, own]), (y1.at[:, main], kbuf.at[1, own])]
            wait_all(run_copies(todo, sems, 12))

        @pl.when(jnp.logical_not(low))
        def _():
            todo = halves(w, lambda i, cols: kbuf.at[i, own, cols])
            todo += [(y1.at[:, main], qbuf.at[0, own]), (y2, qbuf.at[1, own])]
            wait_all(run_copies(todo, sems, 12))

        wait_all(shared)
        info[...] = token_rows(qmeta[...], heads)
        id_lane = lax.broadcasted_iota(jnp.int32, (total, LANES), 1) == 3 * heads
        key_ids = jnp.sum(jnp.where(id_lane, kmeta[...].astype(F32), 0.0), axis=1, keepdims=True)
        at_key = lax.broadcasted_iota(jnp.int32, (total, total), 0)
        at_query = lax.broadcasted_iota(jnp.int32, (total, total), 1)
        visible = (key_ids <= info[2 * heads : 2 * heads + 1, :]) & ((at_key < rows) | (at_query < rows - EDGE))
        for i in range(2):

            def step(c, carry, i=i):
                a = pl.ds(pl.multiple_of(c * LANES, LANES), LANES)
                b = pl.ds(pl.multiple_of(half + c * LANES, LANES), LANES)
                head = i * count + c
                query_term, key_term, value_term = pair_terms(
                    qbuf[i, :, a],
                    qbuf[i, :, b],
                    kbuf[i, :, a],
                    kbuf[i, :, b],
                    info[pl.ds(head, 1), :],
                    info[pl.ds(heads + head, 1), :],
                    visible,
                )
                dq[i, :, a] = query_term.astype(BF16)
                dk[i, :, a] = key_term.astype(BF16)
                dk[i, :, b] = value_term.astype(BF16)
                return carry

            lax.fori_loop(0, count, step, 0)

        made = run_copies(
            halves(dkedge, lambda i, cols: dk.at[i, past, cols], back=True)
            + halves(dqedge, lambda i, cols: dq.at[i, past, cols], back=True),
            sems,
        )

        @pl.when(low)
        def _():
            todo = [(dq.at[0, own], dw.at[:, left]), (dq.at[1, own], dw.at[:, right])]
            todo += [(dk.at[0, own], dy2), (dk.at[1, own], dy1)]
            wait_all(run_copies(todo, sems, 12))

        @pl.when(jnp.logical_not(low))
        def _():
            todo = halves(dw, lambda i, cols: dk.at[i, own, cols], back=True)
            todo += [(dq.at[0, own], dy1.at[:, left]), (dq.at[1, own], dy2.at[:, left])]
            wait_all(run_copies(todo, sems, 12))

        wait_all(made)

    return pl.pallas_call(
        body,
        out_shape=[
            jax.ShapeDtypeStruct((rows, 2 * width), BF16),
            jax.ShapeDtypeStruct((rows, width), BF16),
            jax.ShapeDtypeStruct((rows, width), BF16),
            jax.ShapeDtypeStruct((EDGE, 2 * width), BF16),
            jax.ShapeDtypeStruct((EDGE, width), BF16),
        ],
        in_specs=anywhere(5),
        out_specs=anywhere(5),
        scratch_shapes=[
            pltpu.VMEM((2, total, width), BF16),
            pltpu.VMEM((2, total, width), BF16),
            pltpu.VMEM((2, total, half), BF16),
            pltpu.VMEM((2, total, width), BF16),
            pltpu.VMEM((total, LANES), BF16),
            pltpu.VMEM((total, LANES), BF16),
            pltpu.VMEM((32, total), F32),
            pltpu.SemaphoreType.DMA((18,)),
        ],
        compiler_params=pltpu.CompilerParams(vmem_limit_bytes=32 * 2**20),
        cost_estimate=pl.CostEstimate(
            flops=10 * 10 * rows * rows * LANES, bytes_accessed=16 * rows * width, transcendentals=10 * rows * rows
        ),
        name="near_pairs",
    )(y1, y2, w, key_edge, query_edge)


def unpack(e1, e2, e3):
    groups, rows, width = e1.shape
    half = width // 2

    def body(e1, e2, e3, dq, dk, dv, sems):
        low = lax.axis_index("ctx") < 2
        left, right = pl.ds(0, half), pl.ds(half, half)

        def moves(first, far_dst, second_dst, near):
            todo = []
            far = half - near
            for h in range(groups):
                base = h * width
                todo.append((e1.at[h], first.at[:, pl.ds(base, width)]))
                todo.append((e2.at[h, :, left], far_dst.at[:, pl.ds(base + far, half)]))
                todo.append((e3.at[h, :, left], far_dst.at[:, pl.ds(base + near, half)]))
                spot = 0 if second_dst is None else 1
                if spot:
                    todo.append((e2.at[h, :, right], second_dst[0].at[:, pl.ds(base + second_dst[1], half)]))
                    todo.append((e3.at[h, :, right], second_dst[0].at[:, pl.ds(base + second_dst[2], half)]))
            return todo

        @pl.when(low)
        def _():
            wait_all(run_copies(moves(dq, dk, (dv, 0, half), half), sems))

        @pl.when(jnp.logical_not(low))
        def _():
            wait_all(run_copies(moves(dk, dq, (dv, 0, half), 0), sems))

    shape = jax.ShapeDtypeStruct((rows, groups * width), BF16)
    return pl.pallas_call(
        body,
        out_shape=[shape] * 3,
        in_specs=anywhere(3),
        out_specs=anywhere(3),
        scratch_shapes=[pltpu.SemaphoreType.DMA((5 * groups,))],
        cost_estimate=pl.CostEstimate(flops=0, bytes_accessed=6 * rows * groups * width * 2, transcendentals=0),
        name="unpack",
    )(e1, e2, e3)


def local_split(queries, keys_in, values_in, attn_out, out_grad, log_norm, span_id):
    groups = lax.axis_size("head")
    width = queries.shape[1] // groups
    half = width // 2
    z = lax.axis_index("ctx")
    low = z < 2
    middle = (z == 1) | (z == 2)

    def to_heads(x):
        y = lax.all_to_all(x, "head", split_axis=0, concat_axis=0, tiled=True)
        return y.reshape(-1, y.shape[2])

    def to_tokens(x):
        x = x.reshape(groups, -1, x.shape[1])
        return lax.all_to_all(x, "head", split_axis=0, concat_axis=0, tiled=True)

    x1, x2, x3 = pack(queries, keys_in, values_in, attn_out, out_grad, span_id.reshape(1, -1), groups, width)
    y1 = add_norm(to_heads(x1), log_norm.T)
    r1 = lax.ppermute(y1, "ctx", INWARD)
    s1 = lax.ppermute(y1, "ctx", SWAP)
    y2 = to_heads(x2)
    r2 = lax.ppermute(y2, "ctx", INWARD)
    s2 = lax.ppermute(r1, "ctx", SWAP)
    w = to_heads(x3)

    def joined(first, second, at):
        return jnp.concatenate([first[at, :half], second[at, :half], first[at, half:width], second[at, half:width]], axis=1)

    top, bottom = slice(0, EDGE), slice(y2.shape[0] - EDGE, None)
    key_edge = jnp.where(low, joined(y2, y1, top), w[top])
    query_edge = jnp.where(low, w[bottom], joined(y1, y2, bottom))
    key_edge = lax.ppermute(jnp.concatenate([key_edge, y1[top, width:]], axis=1), "ctx", DOWN)
    query_edge = lax.ppermute(jnp.concatenate([query_edge, y1[bottom, width:]], axis=1), "ctx", UP)

    swap1, out1, swap2, l1, l2, l3 = far_pairs(y1, y2, w, r1, r2, s1, s2)
    swap1 = lax.ppermute(swap1, "ctx", SWAP)
    out1 = lax.ppermute(out1, "ctx", OUTWARD)
    swap2 = lax.ppermute(swap2, "ctx", SWAP)
    dw, dy1, dy2, dkedge, dqedge = near_pairs(y1, y2, w, key_edge, query_edge)
    dkedge = lax.ppermute(dkedge, "ctx", UP)
    dqedge = lax.ppermute(dqedge, "ctx", DOWN)
    out2 = (swap1.astype(F32) + l3.astype(F32)).astype(BF16)
    out2 = lax.ppermute(out2, "ctx", OUTWARD)

    def wide(x):
        return x.astype(F32)

    def kept(x):
        return jnp.where(middle, x.astype(F32), 0.0)

    def edged(total, first, last):
        return jnp.concatenate([total[:EDGE] + first, total[EDGE:-EDGE], total[-EDGE:] + last], axis=0).astype(BF16)

    def sides(x):
        parts = jnp.split(x, x.shape[1] // half, axis=1)
        return jnp.concatenate(parts[0::2], axis=1), jnp.concatenate(parts[1::2], axis=1)

    dk_low, dk_high = jnp.where(low, wide(dkedge), 0.0), jnp.where(low, 0.0, wide(dkedge))
    dq_low, dq_high = jnp.where(low, wide(dqedge), 0.0), jnp.where(low, 0.0, wide(dqedge))
    dq_low, dq_high = (jnp.concatenate([x, jnp.zeros_like(x)], axis=1) for x in (dq_low, dq_high))
    gw = edged(wide(dw) + kept(l1), dk_high, dq_low)
    first_k, second_k = sides(dk_low)
    first_q, second_q = sides(dq_high)
    g2 = edged(wide(dy2) + kept(l2) + wide(out1), first_k, second_q)
    g1 = edged(wide(dy1) + wide(swap2) + wide(out2), second_k, first_q)
    e1 = to_tokens(gw[:, :width])
    e2 = to_tokens(
        jnp.concatenate([g2[:, :half], jnp.where(low, g2[:, half:], gw[:, width : width + half])], axis=1)
    )
    e3 = to_tokens(jnp.concatenate([g1[:, :half], jnp.where(low, g1[:, half:], gw[:, width + half :])], axis=1))
    return tuple(unpack(e1, e2, e3))


def splits(tokens, blocks, head_width, heads):
    if blocks != 4 or heads % 2 or head_width != LANES or 6 * heads + 1 > LANES:
        return False
    block = tokens // blocks
    span = -(-tokens // SPANS)
    for offset in range(SPANS * span - tokens + 1):
        for end in range(block, tokens, block):
            start = (end - 1 + offset) // span * span - offset
            if min(end - start, start + span - end) > EDGE or max(end - start, span) > block:
                return False
    return block % EDGE == 0


def local(queries, keys_in, values_in, attn_out, out_grad, log_norm, span_id):
    blocks, groups = lax.axis_size("ctx"), lax.axis_size("head")
    heads = log_norm.shape[1]
    tokens = queries.shape[0] * blocks * groups
    plan = local_plain
    if splits(tokens, blocks, queries.shape[1] // (heads * groups), heads):
        plan = local_split
    return plan(queries, keys_in, values_in, attn_out, out_grad, log_norm, span_id)


def solution(mesh):
    placed = (
        P(("clip", "ctx", "head"), None),
        P(("clip", "ctx", "head"), None),
        P(("clip", "ctx", "head"), None),
        P(("clip", "ctx", "head"), None),
        P(("clip", "ctx", "head"), None),
        P(("clip", "ctx"), "head"),
        P(("clip", "ctx", "head")),
    )
    return jax.shard_map(
        local,
        mesh=mesh,
        in_specs=placed,
        out_specs=(
            P(("clip", "ctx", "head"), None),
            P(("clip", "ctx", "head"), None),
            P(("clip", "ctx", "head"), None),
        ),
        check_vma=False,
    )
```

```python
import math

import jax
import jax.numpy as jnp
from jax import lax
from jax.experimental import pallas as pl
from jax.experimental.pallas import tpu as pltpu
from jax.sharding import PartitionSpec as P

SPANS = 12
EDGE = 16
LANES = 128
BF16 = jnp.bfloat16
F32 = jnp.float32

INWARD = ((0, 1), (3, 2))
SWAP = ((1, 2), (2, 1))
OUTWARD = ((1, 0), (2, 3))
DOWN = ((1, 0), (2, 1), (3, 2))
UP = ((0, 1), (1, 2), (2, 3))


def tile_terms(query_blk, grad_blk, norm_blk, delta_blk, query_ids, key_blk, value_blk, key_ids):
    row_count = query_blk.shape[0]
    key_count = key_blk.shape[0]
    head_count = norm_blk.shape[1]
    head_width = query_blk.shape[1] // head_count
    scale = 1.0 / math.sqrt(head_width)
    query3 = query_blk.reshape(row_count, head_count, head_width)
    grad3 = grad_blk.reshape(row_count, head_count, head_width)
    key3 = key_blk.reshape(key_count, head_count, head_width)
    value3 = value_blk.reshape(key_count, head_count, head_width)
    scores = jnp.einsum("rhd,khd->hrk", query3, key3, preferred_element_type=jnp.float32)
    visible = key_ids[None, :] <= query_ids[:, None]
    weight = jnp.where(visible[None], jnp.exp(scores * scale - norm_blk.T[:, :, None]), 0.0)
    weight_low = weight.astype(jnp.bfloat16)
    dweight = jnp.einsum("rhd,khd->hrk", grad3, value3, preferred_element_type=jnp.float32)
    dscore = (weight * (dweight - delta_blk.T[:, :, None]) * scale).astype(jnp.bfloat16)
    query_term = jnp.einsum("hrk,khd->rhd", dscore, key3, preferred_element_type=jnp.float32)
    key_term = jnp.einsum("hrk,rhd->khd", dscore, query3, preferred_element_type=jnp.float32)
    value_term = jnp.einsum("hrk,rhd->khd", weight_low, grad3, preferred_element_type=jnp.float32)
    return (
        query_term.reshape(row_count, -1),
        key_term.reshape(key_count, -1),
        value_term.reshape(key_count, -1),
    )


def rounded(term):
    return lax.optimization_barrier(term.astype(jnp.bfloat16)).astype(jnp.float32)


def local_plain(queries, keys_in, values_in, attn_out, out_grad, log_norm, span_id):
    local_q, local_k, local_v, local_out, local_grad = (
        lax.all_to_all(queries, "head", split_axis=1, concat_axis=0, tiled=True),
        lax.all_to_all(keys_in, "head", split_axis=1, concat_axis=0, tiled=True),
        lax.all_to_all(values_in, "head", split_axis=1, concat_axis=0, tiled=True),
        lax.all_to_all(attn_out, "head", split_axis=1, concat_axis=0, tiled=True),
        lax.all_to_all(out_grad, "head", split_axis=1, concat_axis=0, tiled=True),
    )
    all_ids = lax.all_gather(span_id, ("ctx", "head"), axis=0, tiled=True)
    seg_rows = local_q.shape[0]
    block_count = lax.axis_size("ctx")
    head_count = log_norm.shape[1]
    head_width = local_q.shape[1] // head_count
    my_block = lax.axis_index("ctx")
    own_ids = lax.dynamic_slice_in_dim(all_ids, my_block * seg_rows, seg_rows)
    id_blocks = all_ids.reshape(block_count, seg_rows)
    deltas = jnp.sum(
        (local_grad.astype(jnp.float32) * local_out.astype(jnp.float32)).reshape(
            seg_rows, head_count, head_width
        ),
        axis=2,
    )
    far_queries, far_grads = (
        lax.all_gather(local_q, "ctx", axis=0, tiled=True),
        lax.all_gather(local_grad, "ctx", axis=0, tiled=True),
    )
    far_norms, far_deltas = (
        lax.all_gather(log_norm, "ctx", axis=0, tiled=True),
        lax.all_gather(deltas, "ctx", axis=0, tiled=True),
    )

    def query_step(totals, piece):
        query_blk, grad_blk, norm_blk, delta_blk, query_ids = piece
        query_term, key_term, value_term = tile_terms(
            query_blk, grad_blk, norm_blk, delta_blk, query_ids, local_k, local_v, own_ids
        )
        return ((totals[0] + rounded(key_term), totals[1] + rounded(value_term)), query_term)

    zero_block = jnp.zeros(local_k.shape, jnp.float32)
    (dk_total, dv_total), query_terms = lax.scan(
        query_step,
        (zero_block, zero_block),
        (
            far_queries.reshape(block_count, seg_rows, -1),
            far_grads.reshape(block_count, seg_rows, -1),
            far_norms.reshape(block_count, seg_rows, -1),
            far_deltas.reshape(block_count, seg_rows, -1),
            id_blocks,
        ),
    )
    query_sum = lax.psum_scatter(
        query_terms.reshape(block_count * seg_rows, -1).astype(jnp.bfloat16),
        "ctx",
        scatter_dimension=0,
        tiled=True,
    )
    dk_local = dk_total.astype(jnp.bfloat16)
    dv_local = dv_total.astype(jnp.bfloat16)
    query_grad, key_grad, value_grad = (
        lax.all_to_all(query_sum, "head", split_axis=0, concat_axis=1, tiled=True),
        lax.all_to_all(dk_local, "head", split_axis=0, concat_axis=1, tiled=True),
        lax.all_to_all(dv_local, "head", split_axis=0, concat_axis=1, tiled=True),
    )
    return (query_grad, key_grad, value_grad)


def nt(a, b):
    return lax.dot_general(a, b, (((1,), (1,)), ((), ())), preferred_element_type=F32)


def tn(a, b):
    return lax.dot_general(a, b, (((0,), (0,)), ((), ())), preferred_element_type=F32)


def pieces(value):
    high = value.astype(BF16)
    rest = value - high.astype(F32)
    middle = rest.astype(BF16)
    low = (rest - middle.astype(F32)).astype(BF16)
    return high, middle, low


def run_copies(pairs, sems, first=0):
    made = [pltpu.make_async_copy(src, dst, sems.at[first + i]) for i, (src, dst) in enumerate(pairs)]
    for copy in made:
        copy.start()
    return made


def wait_all(made):
    for copy in made:
        copy.wait()


def anywhere(count):
    return [pl.BlockSpec(memory_space=pl.ANY)] * count


def pack(queries, keys_in, values_in, attn_out, out_grad, span_row, groups, width):
    rows = queries.shape[0]
    heads = width // LANES
    half = width // 2

    def body(q, k, v, o, g, ids, x1, x2, x3, q_v, k_v, v_v, o_v, g_v, meta, sems):
        low = lax.axis_index("ctx") < 2
        loads = run_copies([(k, k_v), (v, v_v), (q, q_v), (g, g_v), (o, o_v)], sems)

        def moves(first, second, third, fourth, near, far):
            todo = []
            for h in range(groups):
                base = h * width
                todo.append((first.at[:, pl.ds(base + near, half)], x1.at[h, :, pl.ds(0, half)]))
                todo.append((second.at[:, pl.ds(base + near, half)], x1.at[h, :, pl.ds(half, half)]))
            for h in range(groups):
                base = h * width
                todo.append((first.at[:, pl.ds(base + far, half)], x2.at[h, :, pl.ds(0, half)]))
                todo.append((second.at[:, pl.ds(base + far, half)], x2.at[h, :, pl.ds(half, half)]))
                todo.append((third.at[:, pl.ds(base, width)], x3.at[h, :, pl.ds(0, width)]))
                todo.append((fourth.at[:, pl.ds(base, width)], x3.at[h, :, pl.ds(width, width)]))
            return [pltpu.make_async_copy(src, dst, sems.at[5 + i]) for i, (src, dst) in enumerate(todo)]

        low_moves = (k_v, v_v, q_v, g_v, half, 0)
        high_moves = (q_v, g_v, k_v, v_v, 0, half)
        wait_all(loads[:4])

        @pl.when(low)
        def _():
            for copy in moves(*low_moves):
                copy.start()

        @pl.when(jnp.logical_not(low))
        def _():
            for copy in moves(*high_moves):
                copy.start()

        wait_all(loads[4:])
        lane = lax.broadcasted_iota(jnp.int32, (rows, LANES), 1)
        slot = jnp.where(lane < 3 * heads, lane % heads, -1)
        at_row = lax.broadcasted_iota(jnp.int32, (rows, rows), 0)
        at_col = lax.broadcasted_iota(jnp.int32, (rows, rows), 1)
        own = jnp.sum(jnp.where(at_row == at_col, ids[...].astype(F32), 0.0), axis=1, keepdims=True)
        for h in range(groups):
            total = jnp.zeros((rows, LANES), F32)
            for c in range(heads):
                cols = pl.ds(h * width + c * LANES, LANES)
                delta = jnp.sum(o_v[:, cols].astype(F32) * g_v[:, cols].astype(F32), axis=1, keepdims=True)
                total = jnp.where(slot == c, delta, total)
            high, middle, lowest = pieces(total)
            kept = jnp.where(lane < heads, high, jnp.where(lane < 2 * heads, middle, lowest))
            meta[h] = jnp.where(lane < 3 * heads, kept, jnp.where(lane == 3 * heads, own.astype(BF16), 0.0).astype(BF16))
        last = run_copies([(meta, x1.at[:, :, pl.ds(width, LANES)])], sems, 5 + 6 * groups)

        @pl.when(low)
        def _():
            wait_all(moves(*low_moves))

        @pl.when(jnp.logical_not(low))
        def _():
            wait_all(moves(*high_moves))

        wait_all(last)

    whole = pltpu.VMEM((rows, groups * width), BF16)
    return pl.pallas_call(
        body,
        out_shape=[
            jax.ShapeDtypeStruct((groups, rows, width + LANES), BF16),
            jax.ShapeDtypeStruct((groups, rows, width), BF16),
            jax.ShapeDtypeStruct((groups, rows, 2 * width), BF16),
        ],
        in_specs=anywhere(5) + [pl.BlockSpec(memory_space=pltpu.VMEM)],
        out_specs=anywhere(3),
        scratch_shapes=[whole] * 5
        + [pltpu.VMEM((groups, rows, LANES), BF16), pltpu.SemaphoreType.DMA((6 + 6 * groups,))],
        cost_estimate=pl.CostEstimate(flops=0, bytes_accessed=10 * rows * groups * width * 2, transcendentals=0),
        name="pack",
    )(queries, keys_in, values_in, attn_out, out_grad, span_row)


def add_norm(payload, norm_rows):
    rows, width = payload.shape
    heads = norm_rows.shape[0]
    block = pl.BlockSpec((rows, LANES), lambda i: (0, width // LANES - 1))

    def body(x, norm, y):
        at_row = lax.broadcasted_iota(jnp.int32, (heads, LANES), 0)
        at_lane = lax.broadcasted_iota(jnp.int32, (heads, LANES), 1)
        total = x[...].astype(F32)
        for i, piece in enumerate(pieces(norm[...])):
            place = jnp.where(at_lane == at_row + (3 * heads + 1 + i * heads), 1.0, 0.0).astype(BF16)
            total += tn(piece, place)
        y[...] = total.astype(BF16)

    return pl.pallas_call(
        body,
        grid=(1,),
        out_shape=jax.ShapeDtypeStruct(payload.shape, BF16),
        in_specs=[block, pl.BlockSpec((heads, rows), lambda i: (0, 0))],
        out_specs=block,
        input_output_aliases={0: 0},
        cost_estimate=pl.CostEstimate(flops=0, bytes_accessed=4 * rows * LANES, transcendentals=0),
        name="add_norm",
    )(payload, norm_rows)


def token_rows(meta, heads):
    at_row = lax.broadcasted_iota(jnp.int32, (32, LANES), 0)
    at_lane = lax.broadcasted_iota(jnp.int32, (32, LANES), 1)
    norm_lane = at_lane - (3 * heads + 1)
    is_norm = (norm_lane >= 0) & (norm_lane < 3 * heads) & (norm_lane % heads == at_row) & (at_row < heads)
    is_delta = (at_lane < 3 * heads) & (at_lane % heads == at_row - heads) & (at_row >= heads)
    is_id = (at_lane == 3 * heads) & (at_row == 2 * heads)
    chosen = jnp.where(is_norm | is_delta | is_id, 1.0, 0.0).astype(BF16)
    return nt(chosen, meta)


def pair_terms(query, grad, key, value, norm, delta, visible=None):
    scale = 1.0 / math.sqrt(query.shape[1])
    weight = jnp.exp(nt(key, query) * scale - norm)
    if visible is not None:
        weight = jnp.where(visible, weight, 0.0)
    dscore = (weight * (nt(value, grad) - delta) * scale).astype(BF16)
    value_term = jnp.dot(weight.astype(BF16), grad, preferred_element_type=F32)
    key_term = jnp.dot(dscore, query, preferred_element_type=F32)
    query_term = tn(dscore, key)
    return query_term, key_term, value_term


def far_pairs(y1, y2, w, r1, r2, s1, s2):
    rows, width = y2.shape
    half = width // 2
    count = half // LANES
    heads = 2 * count

    def body(y1, y2, w, r1, r2, s1, s2, swap1, out1, swap2, l1, l2, l3, buf, grads, meta, info, sems):
        z = lax.axis_index("ctx")
        one = z == 1

        def pick(a, b):
            return jnp.where(one, a, b)

        @pl.when((z == 1) | (z == 2))
        def _():
            near = pl.multiple_of(pick(0, half), LANES)
            other = pl.multiple_of(pick(half, 0), LANES)
            main = pl.ds(0, width)
            tail = pl.ds(width, LANES)
            left, right = pl.ds(0, half), pl.ds(half, half)
            made = run_copies(
                [
                    (y1.at[:, tail], meta.at[pick(2, 0)]),
                    (s1.at[:, tail], meta.at[pick(0, 3)]),
                    (s2.at[:, tail], meta.at[pick(1, 4)]),
                    (r1.at[:, tail], meta.at[pick(3, 1)]),
                    (s1.at[:, main], buf.at[pick(0, 3)]),
                    (s2.at[:, main], buf.at[pick(1, 2)]),
                    (r2, buf.at[pick(2, 1)]),
                    (y2, buf.at[pick(3, 0)]),
                    (w.at[:, pl.ds(near, half)], buf.at[4, :, left]),
                    (w.at[:, pl.ds(width + near, half)], buf.at[4, :, right]),
                    (w.at[:, pl.ds(other, half)], buf.at[5, :, left]),
                    (w.at[:, pl.ds(width + other, half)], buf.at[5, :, right]),
                    (r1.at[:, main], buf.at[6]),
                ],
                sems,
            )
            wait_all(made)
            for i in range(3):
                info[i] = token_rows(meta[i], heads)
            first_active = pick(0, count)
            first_other = pick(count, 0)
            zero = jnp.zeros((rows, LANES), BF16)

            def single(q_slot, k_slot, c, head):
                a = pl.ds(pl.multiple_of(c * LANES, LANES), LANES)
                b = pl.ds(pl.multiple_of(half + c * LANES, LANES), LANES)
                own = pick(2, 1)
                return pair_terms(
                    buf[q_slot, :, a],
                    buf[q_slot, :, b],
                    buf[k_slot, :, a],
                    buf[k_slot, :, b],
                    info[own, pl.ds(head, 1), :],
                    info[own, pl.ds(heads + head, 1), :],
                )

            def step(c, carry):
                a = pl.ds(pl.multiple_of(c * LANES, LANES), LANES)
                b = pl.ds(pl.multiple_of(half + c * LANES, LANES), LANES)
                head = first_active + c
                extra_q, extra_k, extra_v = single(pick(4, 1), pick(2, 4), c, head)
                key = buf[2:4, :, a].reshape(2 * rows, LANES)
                value = buf[2:4, :, b].reshape(2 * rows, LANES)
                key_sum, value_sum = None, None
                for i in range(2):
                    query_term, key_term, value_term = pair_terms(
                        buf[i, :, a],
                        buf[i, :, b],
                        key,
                        value,
                        info[i, pl.ds(head, 1), :],
                        info[i, pl.ds(heads + head, 1), :],
                    )
                    if i == 1:
                        query_term += jnp.where(one, 0.0, extra_q)
                    grads[i, :, a] = query_term.astype(BF16)
                    grads[i, :, b] = zero
                    key_sum = key_term if i == 0 else key_sum + key_term
                    value_sum = value_term if i == 0 else value_sum + value_term
                grads[2, :, a] = (key_sum[:rows] + jnp.where(one, extra_k, 0.0)).astype(BF16)
                grads[2, :, b] = (value_sum[:rows] + jnp.where(one, extra_v, 0.0)).astype(BF16)
                grads[3, :, a] = key_sum[rows:].astype(BF16)
                grads[3, :, b] = value_sum[rows:].astype(BF16)
                grads[4, :, a] = jnp.where(one, extra_q, extra_k).astype(BF16)
                grads[4, :, b] = jnp.where(one, 0.0, extra_v).astype(BF16)
                extra_q, extra_k, extra_v = single(pick(5, 6), pick(6, 5), c, first_other + c)
                grads[5, :, a] = jnp.where(one, extra_q, extra_k).astype(BF16)
                grads[5, :, b] = jnp.where(one, 0.0, extra_v).astype(BF16)
                grads[6, :, a] = jnp.where(one, extra_k, extra_q).astype(BF16)
                grads[6, :, b] = jnp.where(one, extra_v, 0.0).astype(BF16)
                return carry

            lax.fori_loop(0, count, step, 0)
            made = run_copies(
                [
                    (grads.at[pick(1, 2)], swap1),
                    (grads.at[pick(2, 1)], out1),
                    (grads.at[pick(0, 3)], swap2),
                    (grads.at[pick(3, 0)], l2),
                    (grads.at[6], l3),
                    (grads.at[4, :, left], l1.at[:, pl.ds(near, half)]),
                    (grads.at[4, :, right], l1.at[:, pl.ds(width + near, half)]),
                    (grads.at[5, :, left], l1.at[:, pl.ds(other, half)]),
                    (grads.at[5, :, right], l1.at[:, pl.ds(width + other, half)]),
                ],
                sems,
            )
            wait_all(made)

    single_shape = jax.ShapeDtypeStruct((rows, width), BF16)
    return pl.pallas_call(
        body,
        out_shape=[
            single_shape,
            single_shape,
            single_shape,
            jax.ShapeDtypeStruct((rows, 2 * width), BF16),
            single_shape,
            single_shape,
        ],
        in_specs=anywhere(7),
        out_specs=anywhere(6),
        scratch_shapes=[
            pltpu.VMEM((7, rows, width), BF16),
            pltpu.VMEM((7, rows, width), BF16),
            pltpu.VMEM((5, rows, LANES), BF16),
            pltpu.VMEM((3, 32, rows), F32),
            pltpu.SemaphoreType.DMA((13,)),
        ],
        compiler_params=pltpu.CompilerParams(vmem_limit_bytes=40 * 2**20),
        cost_estimate=pl.CostEstimate(
            flops=30 * 10 * rows * rows * LANES, bytes_accessed=30 * rows * width, transcendentals=30 * rows * rows
        ),
        name="far_pairs",
    )(y1, y2, w, r1, r2, s1, s2)


def near_pairs(y1, y2, w, key_edge, query_edge):
    rows, width = y2.shape
    half = width // 2
    count = half // LANES
    heads = 2 * count
    total = rows + EDGE

    def body(y1, y2, w, kedge, qedge, dw, dy1, dy2, dkedge, dqedge, qbuf, kbuf, dq, dk, kmeta, qmeta, info, sems):
        low = lax.axis_index("ctx") < 2
        left, right = pl.ds(0, half), pl.ds(half, half)
        own, past = pl.ds(0, rows), pl.ds(rows, EDGE)
        main = pl.ds(0, width)

        def halves(array, there, back=False):
            todo = []
            for i in range(2):
                for j in range(array.shape[1] // width):
                    wide = array.at[:, pl.ds(j * width + i * half, half)]
                    narrow = there(i, right if j else left)
                    todo.append((narrow, wide) if back else (wide, narrow))
            return todo

        shared = run_copies(
            [
                (y1.at[:, pl.ds(width, LANES)], kmeta.at[own]),
                (y1.at[:, pl.ds(width, LANES)], qmeta.at[own]),
                (kedge.at[:, pl.ds(2 * width, LANES)], kmeta.at[past]),
                (qedge.at[:, pl.ds(2 * width, LANES)], qmeta.at[past]),
            ]
            + halves(kedge, lambda i, cols: kbuf.at[i, past, cols])
            + halves(qedge, lambda i, cols: qbuf.at[i, past, cols]),
            sems,
        )

        @pl.when(low)
        def _():
            todo = halves(w, lambda i, cols: qbuf.at[i, own, cols])
            todo += [(y2, kbuf.at[0, own]), (y1.at[:, main], kbuf.at[1, own])]
            wait_all(run_copies(todo, sems, 12))

        @pl.when(jnp.logical_not(low))
        def _():
            todo = halves(w, lambda i, cols: kbuf.at[i, own, cols])
            todo += [(y1.at[:, main], qbuf.at[0, own]), (y2, qbuf.at[1, own])]
            wait_all(run_copies(todo, sems, 12))

        wait_all(shared)
        info[...] = token_rows(qmeta[...], heads)
        id_lane = lax.broadcasted_iota(jnp.int32, (total, LANES), 1) == 3 * heads
        key_ids = jnp.sum(jnp.where(id_lane, kmeta[...].astype(F32), 0.0), axis=1, keepdims=True)
        at_key = lax.broadcasted_iota(jnp.int32, (total, total), 0)
        at_query = lax.broadcasted_iota(jnp.int32, (total, total), 1)
        visible = (key_ids <= info[2 * heads : 2 * heads + 1, :]) & ((at_key < rows) | (at_query < rows - EDGE))
        for i in range(2):

            def step(c, carry, i=i):
                a = pl.ds(pl.multiple_of(c * LANES, LANES), LANES)
                b = pl.ds(pl.multiple_of(half + c * LANES, LANES), LANES)
                head = i * count + c
                query_term, key_term, value_term = pair_terms(
                    qbuf[i, :, a],
                    qbuf[i, :, b],
                    kbuf[i, :, a],
                    kbuf[i, :, b],
                    info[pl.ds(head, 1), :],
                    info[pl.ds(heads + head, 1), :],
                    visible,
                )
                dq[i, :, a] = query_term.astype(BF16)
                dk[i, :, a] = key_term.astype(BF16)
                dk[i, :, b] = value_term.astype(BF16)
                return carry

            lax.fori_loop(0, count, step, 0)

        made = run_copies(
            halves(dkedge, lambda i, cols: dk.at[i, past, cols], back=True)
            + halves(dqedge, lambda i, cols: dq.at[i, past, cols], back=True),
            sems,
        )

        @pl.when(low)
        def _():
            todo = [(dq.at[0, own], dw.at[:, left]), (dq.at[1, own], dw.at[:, right])]
            todo += [(dk.at[0, own], dy2), (dk.at[1, own], dy1)]
            wait_all(run_copies(todo, sems, 12))

        @pl.when(jnp.logical_not(low))
        def _():
            todo = halves(dw, lambda i, cols: dk.at[i, own, cols], back=True)
            todo += [(dq.at[0, own], dy1.at[:, left]), (dq.at[1, own], dy2.at[:, left])]
            wait_all(run_copies(todo, sems, 12))

        wait_all(made)

    return pl.pallas_call(
        body,
        out_shape=[
            jax.ShapeDtypeStruct((rows, 2 * width), BF16),
            jax.ShapeDtypeStruct((rows, width), BF16),
            jax.ShapeDtypeStruct((rows, width), BF16),
            jax.ShapeDtypeStruct((EDGE, 2 * width), BF16),
            jax.ShapeDtypeStruct((EDGE, width), BF16),
        ],
        in_specs=anywhere(5),
        out_specs=anywhere(5),
        scratch_shapes=[
            pltpu.VMEM((2, total, width), BF16),
            pltpu.VMEM((2, total, width), BF16),
            pltpu.VMEM((2, total, half), BF16),
            pltpu.VMEM((2, total, width), BF16),
            pltpu.VMEM((total, LANES), BF16),
            pltpu.VMEM((total, LANES), BF16),
            pltpu.VMEM((32, total), F32),
            pltpu.SemaphoreType.DMA((18,)),
        ],
        compiler_params=pltpu.CompilerParams(vmem_limit_bytes=32 * 2**20),
        cost_estimate=pl.CostEstimate(
            flops=10 * 10 * rows * rows * LANES, bytes_accessed=16 * rows * width, transcendentals=10 * rows * rows
        ),
        name="near_pairs",
    )(y1, y2, w, key_edge, query_edge)


def unpack(e1, e2, e3):
    groups, rows, width = e1.shape
    half = width // 2

    def body(e1, e2, e3, dq, dk, dv, first, second, third, sems):
        low = lax.axis_index("ctx") < 2
        left, right = pl.ds(0, half), pl.ds(half, half)
        todo = []
        for h in range(groups):
            todo.append((e1.at[h], first.at[:, pl.ds(h * width, width)]))
        for h in range(groups):
            todo.append((e2.at[h, :, right], third.at[:, pl.ds(h * width, half)]))
            todo.append((e3.at[h, :, right], third.at[:, pl.ds(h * width + half, half)]))
        for e, near in ((e2, jnp.where(low, 0, half)), (e3, jnp.where(low, half, 0))):
            for h in range(groups):
                at = pl.multiple_of(h * width + near, LANES)
                todo.append((e.at[h, :, left], second.at[:, pl.ds(at, half)]))
        loads = run_copies(todo, sems)
        count = len(loads)
        wait_all(loads[:groups])

        def stores(near, far):
            return [
                pltpu.make_async_copy(src, dst, sems.at[count + i])
                for i, (src, dst) in enumerate([(first, near), (third, dv), (second, far)])
            ]

        @pl.when(low)
        def _():
            stores(dq, dk)[0].start()

        @pl.when(jnp.logical_not(low))
        def _():
            stores(dk, dq)[0].start()

        wait_all(loads[groups:])

        @pl.when(low)
        def _():
            made = stores(dq, dk)
            made[1].start()
            made[2].start()
            wait_all(made)

        @pl.when(jnp.logical_not(low))
        def _():
            made = stores(dk, dq)
            made[1].start()
            made[2].start()
            wait_all(made)

    shape = jax.ShapeDtypeStruct((rows, groups * width), BF16)
    return pl.pallas_call(
        body,
        out_shape=[shape] * 3,
        in_specs=anywhere(3),
        out_specs=anywhere(3),
        scratch_shapes=[pltpu.VMEM((rows, groups * width), BF16)] * 3 + [pltpu.SemaphoreType.DMA((3 + 5 * groups,))],
        cost_estimate=pl.CostEstimate(flops=0, bytes_accessed=6 * rows * groups * width * 2, transcendentals=0),
        name="unpack",
    )(e1, e2, e3)


def local_split(queries, keys_in, values_in, attn_out, out_grad, log_norm, span_id):
    groups = lax.axis_size("head")
    width = queries.shape[1] // groups
    half = width // 2
    z = lax.axis_index("ctx")
    low = z < 2
    middle = (z == 1) | (z == 2)

    def to_heads(x):
        y = lax.all_to_all(x, "head", split_axis=0, concat_axis=0, tiled=True)
        return y.reshape(-1, y.shape[2])

    def to_tokens(x):
        x = x.reshape(groups, -1, x.shape[1])
        return lax.all_to_all(x, "head", split_axis=0, concat_axis=0, tiled=True)

    x1, x2, x3 = pack(queries, keys_in, values_in, attn_out, out_grad, span_id.reshape(1, -1), groups, width)
    y1 = add_norm(to_heads(x1), log_norm.T)
    r1 = lax.ppermute(y1, "ctx", INWARD)
    s1 = lax.ppermute(y1, "ctx", SWAP)
    x2, y1 = lax.optimization_barrier((x2, y1))
    y2 = to_heads(x2)
    x3, y2 = lax.optimization_barrier((x3, y2))
    r2 = lax.ppermute(y2, "ctx", INWARD)
    s2 = lax.ppermute(r1, "ctx", SWAP)
    w = to_heads(x3)

    def joined(first, second, at):
        return jnp.concatenate([first[at, :half], second[at, :half], first[at, half:width], second[at, half:width]], axis=1)

    top, bottom = slice(0, EDGE), slice(y2.shape[0] - EDGE, None)
    key_edge = jnp.where(low, joined(y2, y1, top), w[top])
    query_edge = jnp.where(low, w[bottom], joined(y1, y2, bottom))
    key_edge = lax.ppermute(jnp.concatenate([key_edge, y1[top, width:]], axis=1), "ctx", DOWN)
    query_edge = lax.ppermute(jnp.concatenate([query_edge, y1[bottom, width:]], axis=1), "ctx", UP)

    swap1, out1, swap2, l1, l2, l3 = far_pairs(y1, y2, w, r1, r2, s1, s2)
    swap1 = lax.ppermute(swap1, "ctx", SWAP)
    out1 = lax.ppermute(out1, "ctx", OUTWARD)
    swap2 = lax.ppermute(swap2, "ctx", SWAP)
    dw, dy1, dy2, dkedge, dqedge = near_pairs(y1, y2, w, key_edge, query_edge)
    dkedge = lax.ppermute(dkedge, "ctx", UP)
    dqedge = lax.ppermute(dqedge, "ctx", DOWN)
    out2 = (swap1.astype(F32) + l3.astype(F32)).astype(BF16)
    out2 = lax.ppermute(out2, "ctx", OUTWARD)

    def wide(x):
        return x.astype(F32)

    def kept(x):
        return jnp.where(middle, x.astype(F32), 0.0)

    def edged(total, first, last):
        return jnp.concatenate([total[:EDGE] + first, total[EDGE:-EDGE], total[-EDGE:] + last], axis=0).astype(BF16)

    def sides(x):
        parts = jnp.split(x, x.shape[1] // half, axis=1)
        return jnp.concatenate(parts[0::2], axis=1), jnp.concatenate(parts[1::2], axis=1)

    dk_low, dk_high = jnp.where(low, wide(dkedge), 0.0), jnp.where(low, 0.0, wide(dkedge))
    dq_low, dq_high = jnp.where(low, wide(dqedge), 0.0), jnp.where(low, 0.0, wide(dqedge))
    dq_low, dq_high = (jnp.concatenate([x, jnp.zeros_like(x)], axis=1) for x in (dq_low, dq_high))
    gw = edged(wide(dw) + kept(l1), dk_high, dq_low)
    first_k, second_k = sides(dk_low)
    first_q, second_q = sides(dq_high)
    g2 = edged(wide(dy2) + kept(l2) + wide(out1), first_k, second_q)
    g1 = edged(wide(dy1) + wide(swap2) + wide(out2), second_k, first_q)
    e1 = to_tokens(gw[:, :width])
    e2 = to_tokens(
        jnp.concatenate([g2[:, :half], jnp.where(low, g2[:, half:], gw[:, width : width + half])], axis=1)
    )
    e3 = to_tokens(jnp.concatenate([g1[:, :half], jnp.where(low, g1[:, half:], gw[:, width + half :])], axis=1))
    return tuple(unpack(e1, e2, e3))


def splits(tokens, blocks, head_width, heads):
    if blocks != 4 or heads % 2 or head_width != LANES or 6 * heads + 1 > LANES:
        return False
    block = tokens // blocks
    span = -(-tokens // SPANS)
    for offset in range(SPANS * span - tokens + 1):
        for end in range(block, tokens, block):
            start = (end - 1 + offset) // span * span - offset
            if min(end - start, start + span - end) > EDGE or max(end - start, span) > block:
                return False
    return block % EDGE == 0


def local(queries, keys_in, values_in, attn_out, out_grad, log_norm, span_id):
    blocks, groups = lax.axis_size("ctx"), lax.axis_size("head")
    heads = log_norm.shape[1]
    tokens = queries.shape[0] * blocks * groups
    plan = local_plain
    if splits(tokens, blocks, queries.shape[1] // (heads * groups), heads):
        plan = local_split
    return plan(queries, keys_in, values_in, attn_out, out_grad, log_norm, span_id)


def solution(mesh):
    placed = (
        P(("clip", "ctx", "head"), None),
        P(("clip", "ctx", "head"), None),
        P(("clip", "ctx", "head"), None),
        P(("clip", "ctx", "head"), None),
        P(("clip", "ctx", "head"), None),
        P(("clip", "ctx"), "head"),
        P(("clip", "ctx", "head")),
    )
    return jax.shard_map(
        local,
        mesh=mesh,
        in_specs=placed,
        out_specs=(
            P(("clip", "ctx", "head"), None),
            P(("clip", "ctx", "head"), None),
            P(("clip", "ctx", "head"), None),
        ),
        check_vma=False,
    )
```

```python
import math

import jax
import jax.numpy as jnp
from jax import lax
from jax.experimental import pallas as pl
from jax.experimental.pallas import tpu as pltpu
from jax.sharding import PartitionSpec as P

SPANS = 12
EDGE = 16
VMEM_LIMIT = 32 * 2**20
LANES = 128
BF16 = jnp.bfloat16
F32 = jnp.float32

INWARD = ((0, 1), (3, 2))
SWAP = ((1, 2), (2, 1))
OUTWARD = ((1, 0), (2, 3))
DOWN = ((1, 0), (2, 1), (3, 2))
UP = ((0, 1), (1, 2), (2, 3))


def tile_terms(query_blk, grad_blk, norm_blk, delta_blk, query_ids, key_blk, value_blk, key_ids):
    row_count = query_blk.shape[0]
    key_count = key_blk.shape[0]
    head_count = norm_blk.shape[1]
    head_width = query_blk.shape[1] // head_count
    scale = 1.0 / math.sqrt(head_width)
    query3 = query_blk.reshape(row_count, head_count, head_width)
    grad3 = grad_blk.reshape(row_count, head_count, head_width)
    key3 = key_blk.reshape(key_count, head_count, head_width)
    value3 = value_blk.reshape(key_count, head_count, head_width)
    scores = jnp.einsum("rhd,khd->hrk", query3, key3, preferred_element_type=jnp.float32)
    visible = key_ids[None, :] <= query_ids[:, None]
    weight = jnp.where(visible[None], jnp.exp(scores * scale - norm_blk.T[:, :, None]), 0.0)
    weight_low = weight.astype(jnp.bfloat16)
    dweight = jnp.einsum("rhd,khd->hrk", grad3, value3, preferred_element_type=jnp.float32)
    dscore = (weight * (dweight - delta_blk.T[:, :, None]) * scale).astype(jnp.bfloat16)
    query_term = jnp.einsum("hrk,khd->rhd", dscore, key3, preferred_element_type=jnp.float32)
    key_term = jnp.einsum("hrk,rhd->khd", dscore, query3, preferred_element_type=jnp.float32)
    value_term = jnp.einsum("hrk,rhd->khd", weight_low, grad3, preferred_element_type=jnp.float32)
    return (
        query_term.reshape(row_count, -1),
        key_term.reshape(key_count, -1),
        value_term.reshape(key_count, -1),
    )


def rounded(term):
    return lax.optimization_barrier(term.astype(jnp.bfloat16)).astype(jnp.float32)


def local_plain(queries, keys_in, values_in, attn_out, out_grad, log_norm, span_id):
    local_q, local_k, local_v, local_out, local_grad = (
        lax.all_to_all(queries, "head", split_axis=1, concat_axis=0, tiled=True),
        lax.all_to_all(keys_in, "head", split_axis=1, concat_axis=0, tiled=True),
        lax.all_to_all(values_in, "head", split_axis=1, concat_axis=0, tiled=True),
        lax.all_to_all(attn_out, "head", split_axis=1, concat_axis=0, tiled=True),
        lax.all_to_all(out_grad, "head", split_axis=1, concat_axis=0, tiled=True),
    )
    all_ids = lax.all_gather(span_id, ("ctx", "head"), axis=0, tiled=True)
    seg_rows = local_q.shape[0]
    block_count = lax.axis_size("ctx")
    head_count = log_norm.shape[1]
    head_width = local_q.shape[1] // head_count
    my_block = lax.axis_index("ctx")
    own_ids = lax.dynamic_slice_in_dim(all_ids, my_block * seg_rows, seg_rows)
    id_blocks = all_ids.reshape(block_count, seg_rows)
    deltas = jnp.sum(
        (local_grad.astype(jnp.float32) * local_out.astype(jnp.float32)).reshape(
            seg_rows, head_count, head_width
        ),
        axis=2,
    )
    far_queries, far_grads = (
        lax.all_gather(local_q, "ctx", axis=0, tiled=True),
        lax.all_gather(local_grad, "ctx", axis=0, tiled=True),
    )
    far_norms, far_deltas = (
        lax.all_gather(log_norm, "ctx", axis=0, tiled=True),
        lax.all_gather(deltas, "ctx", axis=0, tiled=True),
    )

    def query_step(totals, piece):
        query_blk, grad_blk, norm_blk, delta_blk, query_ids = piece
        query_term, key_term, value_term = tile_terms(
            query_blk, grad_blk, norm_blk, delta_blk, query_ids, local_k, local_v, own_ids
        )
        return ((totals[0] + rounded(key_term), totals[1] + rounded(value_term)), query_term)

    zero_block = jnp.zeros(local_k.shape, jnp.float32)
    (dk_total, dv_total), query_terms = lax.scan(
        query_step,
        (zero_block, zero_block),
        (
            far_queries.reshape(block_count, seg_rows, -1),
            far_grads.reshape(block_count, seg_rows, -1),
            far_norms.reshape(block_count, seg_rows, -1),
            far_deltas.reshape(block_count, seg_rows, -1),
            id_blocks,
        ),
    )
    query_sum = lax.psum_scatter(
        query_terms.reshape(block_count * seg_rows, -1).astype(jnp.bfloat16),
        "ctx",
        scatter_dimension=0,
        tiled=True,
    )
    dk_local = dk_total.astype(jnp.bfloat16)
    dv_local = dv_total.astype(jnp.bfloat16)
    query_grad, key_grad, value_grad = (
        lax.all_to_all(query_sum, "head", split_axis=0, concat_axis=1, tiled=True),
        lax.all_to_all(dk_local, "head", split_axis=0, concat_axis=1, tiled=True),
        lax.all_to_all(dv_local, "head", split_axis=0, concat_axis=1, tiled=True),
    )
    return (query_grad, key_grad, value_grad)


def nt(a, b):
    return lax.dot_general(a, b, (((1,), (1,)), ((), ())), preferred_element_type=F32)


def tn(a, b):
    return lax.dot_general(a, b, (((0,), (0,)), ((), ())), preferred_element_type=F32)


def pieces(value):
    high = value.astype(BF16)
    rest = value - high.astype(F32)
    middle = rest.astype(BF16)
    low = (rest - middle.astype(F32)).astype(BF16)
    return high, middle, low


def run_copies(pairs, sems, first=0):
    made = [pltpu.make_async_copy(src, dst, sems.at[first + i]) for i, (src, dst) in enumerate(pairs)]
    for copy in made:
        copy.start()
    return made


def wait_all(made):
    for copy in made:
        copy.wait()


def anywhere(count):
    return [pl.BlockSpec(memory_space=pl.ANY)] * count


def pack(queries, keys_in, values_in, attn_out, out_grad, span_row, groups, width):
    rows = queries.shape[0]
    heads = width // LANES
    half = width // 2

    def body(q, k, v, o, g, ids, x1, rest, q_v, k_v, v_v, o_v, g_v, meta, sems):
        low = lax.axis_index("ctx") < 2
        loads = run_copies([(k, k_v), (v, v_v), (q, q_v), (g, g_v), (o, o_v)], sems)

        def moves(first, second, third, fourth, near, far):
            todo = []
            for h in range(groups):
                base = h * width
                todo.append((first.at[:, pl.ds(base + near, half)], x1.at[h, :, pl.ds(0, half)]))
                todo.append((second.at[:, pl.ds(base + near, half)], x1.at[h, :, pl.ds(half, half)]))
            for h in range(groups):
                base = h * width
                todo.append((first.at[:, pl.ds(base + far, half)], rest.at[h, :, pl.ds(0, half)]))
                todo.append((second.at[:, pl.ds(base + far, half)], rest.at[h, :, pl.ds(half, half)]))
                todo.append((third.at[:, pl.ds(base, width)], rest.at[h, :, pl.ds(width, width)]))
                todo.append((fourth.at[:, pl.ds(base, width)], rest.at[h, :, pl.ds(2 * width, width)]))
            return [pltpu.make_async_copy(src, dst, sems.at[5 + i]) for i, (src, dst) in enumerate(todo)]

        low_moves = (k_v, v_v, q_v, g_v, half, 0)
        high_moves = (q_v, g_v, k_v, v_v, 0, half)
        wait_all(loads[:4])

        @pl.when(low)
        def _():
            for copy in moves(*low_moves):
                copy.start()

        @pl.when(jnp.logical_not(low))
        def _():
            for copy in moves(*high_moves):
                copy.start()

        wait_all(loads[4:])
        lane = lax.broadcasted_iota(jnp.int32, (rows, LANES), 1)
        slot = jnp.where(lane < 3 * heads, lane % heads, -1)
        at_row = lax.broadcasted_iota(jnp.int32, (rows, rows), 0)
        at_col = lax.broadcasted_iota(jnp.int32, (rows, rows), 1)
        own = jnp.sum(jnp.where(at_row == at_col, ids[...].astype(F32), 0.0), axis=1, keepdims=True)
        for h in range(groups):
            total = jnp.zeros((rows, LANES), F32)
            for c in range(heads):
                cols = pl.ds(h * width + c * LANES, LANES)
                delta = jnp.sum(o_v[:, cols].astype(F32) * g_v[:, cols].astype(F32), axis=1, keepdims=True)
                total = jnp.where(slot == c, delta, total)
            high, middle, lowest = pieces(total)
            kept = jnp.where(lane < heads, high, jnp.where(lane < 2 * heads, middle, lowest))
            meta[h] = jnp.where(lane < 3 * heads, kept, jnp.where(lane == 3 * heads, own.astype(BF16), 0.0).astype(BF16))
        last = run_copies([(meta, x1.at[:, :, pl.ds(width, LANES)])], sems, 5 + 6 * groups)

        @pl.when(low)
        def _():
            wait_all(moves(*low_moves))

        @pl.when(jnp.logical_not(low))
        def _():
            wait_all(moves(*high_moves))

        wait_all(last)

    whole = pltpu.VMEM((rows, groups * width), BF16)
    return pl.pallas_call(
        body,
        out_shape=[
            jax.ShapeDtypeStruct((groups, rows, width + LANES), BF16),
            jax.ShapeDtypeStruct((groups, rows, 3 * width), BF16),
        ],
        in_specs=anywhere(5) + [pl.BlockSpec(memory_space=pltpu.VMEM)],
        out_specs=anywhere(2),
        scratch_shapes=[whole] * 5
        + [pltpu.VMEM((groups, rows, LANES), BF16), pltpu.SemaphoreType.DMA((6 + 6 * groups,))],
        cost_estimate=pl.CostEstimate(flops=0, bytes_accessed=10 * rows * groups * width * 2, transcendentals=0),
        name="pack",
    )(queries, keys_in, values_in, attn_out, out_grad, span_row)


def add_norm(payload, norm_rows):
    rows, width = payload.shape
    heads = norm_rows.shape[0]
    block = pl.BlockSpec((rows, LANES), lambda i: (0, width // LANES - 1))

    def body(x, norm, y):
        at_row = lax.broadcasted_iota(jnp.int32, (heads, LANES), 0)
        at_lane = lax.broadcasted_iota(jnp.int32, (heads, LANES), 1)
        total = x[...].astype(F32)
        for i, piece in enumerate(pieces(norm[...])):
            place = jnp.where(at_lane == at_row + (3 * heads + 1 + i * heads), 1.0, 0.0).astype(BF16)
            total += tn(piece, place)
        y[...] = total.astype(BF16)

    return pl.pallas_call(
        body,
        grid=(1,),
        out_shape=jax.ShapeDtypeStruct(payload.shape, BF16),
        in_specs=[block, pl.BlockSpec((heads, rows), lambda i: (0, 0))],
        out_specs=block,
        input_output_aliases={0: 0},
        cost_estimate=pl.CostEstimate(flops=0, bytes_accessed=4 * rows * LANES, transcendentals=0),
        name="add_norm",
    )(payload, norm_rows)


def token_rows(meta, heads):
    at_row = lax.broadcasted_iota(jnp.int32, (32, LANES), 0)
    at_lane = lax.broadcasted_iota(jnp.int32, (32, LANES), 1)
    norm_lane = at_lane - (3 * heads + 1)
    is_norm = (norm_lane >= 0) & (norm_lane < 3 * heads) & (norm_lane % heads == at_row) & (at_row < heads)
    is_delta = (at_lane < 3 * heads) & (at_lane % heads == at_row - heads) & (at_row >= heads)
    is_id = (at_lane == 3 * heads) & (at_row == 2 * heads)
    chosen = jnp.where(is_norm | is_delta | is_id, 1.0, 0.0).astype(BF16)
    return nt(chosen, meta)


def pair_terms(query, grad, key, value, norm, delta, visible=None):
    scale = 1.0 / math.sqrt(query.shape[1])
    weight = jnp.exp(nt(key, query) * scale - norm)
    if visible is not None:
        weight = jnp.where(visible, weight, 0.0)
    dscore = (weight * (nt(value, grad) - delta) * scale).astype(BF16)
    value_term = jnp.dot(weight.astype(BF16), grad, preferred_element_type=F32)
    key_term = jnp.dot(dscore, query, preferred_element_type=F32)
    query_term = tn(dscore, key)
    return query_term, key_term, value_term


def cut(y1, rest):
    rows = rest.shape[0]
    width = rest.shape[1] // 3
    half = width // 2

    def body(y1, rest, y2, kedge, qedge, sems):
        low = lax.axis_index("ctx") < 2
        top, bottom, tail = pl.ds(0, EDGE), pl.ds(rows - EDGE, EDGE), pl.ds(width, LANES)
        end = pl.ds(2 * width, LANES)
        made = run_copies(
            [
                (y1.at[top, tail], kedge.at[:, end]),
                (y1.at[bottom, tail], qedge.at[:, end]),
                (rest.at[:, pl.ds(0, width)], y2),
            ],
            sems,
        )

        def joined(first, second, at, edge):
            todo = []
            for i in range(2):
                for j, part in enumerate((first, second)):
                    todo.append((part.at[at, pl.ds(i * half, half)], edge.at[:, pl.ds(i * width + j * half, half)]))
            return todo

        whole = pl.ds(width, 2 * width)

        @pl.when(low)
        def _():
            todo = joined(rest, y1, top, kedge) + [(rest.at[bottom, whole], qedge.at[:, pl.ds(0, 2 * width)])]
            wait_all(run_copies(todo, sems, 3))

        @pl.when(jnp.logical_not(low))
        def _():
            todo = joined(y1, rest, bottom, qedge) + [(rest.at[top, whole], kedge.at[:, pl.ds(0, 2 * width)])]
            wait_all(run_copies(todo, sems, 3))

        wait_all(made)

    edge = jax.ShapeDtypeStruct((EDGE, 2 * width + LANES), BF16)
    return pl.pallas_call(
        body,
        out_shape=[jax.ShapeDtypeStruct((rows, width), BF16), edge, edge],
        in_specs=anywhere(2),
        out_specs=[pl.BlockSpec(memory_space=pltpu.VMEM)] * 3,
        scratch_shapes=[pltpu.SemaphoreType.DMA((8,))],
        compiler_params=pltpu.CompilerParams(vmem_limit_bytes=60 * 2**20),
        cost_estimate=pl.CostEstimate(flops=0, bytes_accessed=4 * rows * width, transcendentals=0),
        name="cut",
    )(y1, rest)


def far_pairs(y1, rest, r1, r2, s1, s2):
    rows, width = r2.shape
    half = width // 2
    count = half // LANES
    heads = 2 * count

    def body(y1, rest, r1, r2, s1, s2, swap1, out1, swap2, l1, l2, l3, buf, grads, meta, info, sems):
        z = lax.axis_index("ctx")
        one = z == 1

        def pick(a, b):
            return jnp.where(one, a, b)

        @pl.when((z == 1) | (z == 2))
        def _():
            near = pl.multiple_of(pick(0, half), LANES)
            other = pl.multiple_of(pick(half, 0), LANES)
            main = pl.ds(0, width)
            tail = pl.ds(width, LANES)
            left, right = pl.ds(0, half), pl.ds(half, half)
            made = run_copies(
                [
                    (y1.at[:, tail], meta.at[pick(2, 0)]),
                    (s1.at[:, tail], meta.at[pick(0, 3)]),
                    (s2.at[:, tail], meta.at[pick(1, 4)]),
                    (r1.at[:, tail], meta.at[pick(3, 1)]),
                    (s1.at[:, main], buf.at[pick(0, 3)]),
                    (s2.at[:, main], buf.at[pick(1, 2)]),
                    (r2, buf.at[pick(2, 1)]),
                    (rest.at[:, main], buf.at[pick(3, 0)]),
                    (rest.at[:, pl.ds(width + near, half)], buf.at[4, :, left]),
                    (rest.at[:, pl.ds(2 * width + near, half)], buf.at[4, :, right]),
                    (rest.at[:, pl.ds(width + other, half)], buf.at[5, :, left]),
                    (rest.at[:, pl.ds(2 * width + other, half)], buf.at[5, :, right]),
                    (r1.at[:, main], buf.at[6]),
                ],
                sems,
            )
            wait_all(made)
            for i in range(3):
                info[i] = token_rows(meta[i], heads)
            first_active = pick(0, count)
            first_other = pick(count, 0)
            zero = jnp.zeros((rows, LANES), BF16)

            def single(q_slot, k_slot, c, head):
                a = pl.ds(pl.multiple_of(c * LANES, LANES), LANES)
                b = pl.ds(pl.multiple_of(half + c * LANES, LANES), LANES)
                own = pick(2, 1)
                return pair_terms(
                    buf[q_slot, :, a],
                    buf[q_slot, :, b],
                    buf[k_slot, :, a],
                    buf[k_slot, :, b],
                    info[own, pl.ds(head, 1), :],
                    info[own, pl.ds(heads + head, 1), :],
                )

            def step(c, carry):
                a = pl.ds(pl.multiple_of(c * LANES, LANES), LANES)
                b = pl.ds(pl.multiple_of(half + c * LANES, LANES), LANES)
                head = first_active + c
                extra_q, extra_k, extra_v = single(pick(4, 1), pick(2, 4), c, head)
                key = buf[2:4, :, a].reshape(2 * rows, LANES)
                value = buf[2:4, :, b].reshape(2 * rows, LANES)
                key_sum, value_sum = None, None
                for i in range(2):
                    query_term, key_term, value_term = pair_terms(
                        buf[i, :, a],
                        buf[i, :, b],
                        key,
                        value,
                        info[i, pl.ds(head, 1), :],
                        info[i, pl.ds(heads + head, 1), :],
                    )
                    if i == 1:
                        query_term += jnp.where(one, 0.0, extra_q)
                    grads[i, :, a] = query_term.astype(BF16)
                    grads[i, :, b] = zero
                    key_sum = key_term if i == 0 else key_sum + key_term
                    value_sum = value_term if i == 0 else value_sum + value_term
                grads[2, :, a] = (key_sum[:rows] + jnp.where(one, extra_k, 0.0)).astype(BF16)
                grads[2, :, b] = (value_sum[:rows] + jnp.where(one, extra_v, 0.0)).astype(BF16)
                grads[3, :, a] = key_sum[rows:].astype(BF16)
                grads[3, :, b] = value_sum[rows:].astype(BF16)
                grads[4, :, a] = jnp.where(one, extra_q, extra_k).astype(BF16)
                grads[4, :, b] = jnp.where(one, 0.0, extra_v).astype(BF16)
                extra_q, extra_k, extra_v = single(pick(5, 6), pick(6, 5), c, first_other + c)
                grads[5, :, a] = jnp.where(one, extra_q, extra_k).astype(BF16)
                grads[5, :, b] = jnp.where(one, 0.0, extra_v).astype(BF16)
                grads[6, :, a] = jnp.where(one, extra_k, extra_q).astype(BF16)
                grads[6, :, b] = jnp.where(one, extra_v, 0.0).astype(BF16)
                return carry

            lax.fori_loop(0, count, step, 0, unroll=True)
            made = run_copies(
                [
                    (grads.at[pick(1, 2)], swap1),
                    (grads.at[pick(2, 1)], out1),
                    (grads.at[pick(0, 3)], swap2),
                    (grads.at[pick(3, 0)], l2),
                    (grads.at[6], l3),
                    (grads.at[4, :, left], l1.at[:, pl.ds(near, half)]),
                    (grads.at[4, :, right], l1.at[:, pl.ds(width + near, half)]),
                    (grads.at[5, :, left], l1.at[:, pl.ds(other, half)]),
                    (grads.at[5, :, right], l1.at[:, pl.ds(width + other, half)]),
                ],
                sems,
            )
            wait_all(made)

    single_shape = jax.ShapeDtypeStruct((rows, width), BF16)
    return pl.pallas_call(
        body,
        out_shape=[
            single_shape,
            single_shape,
            single_shape,
            jax.ShapeDtypeStruct((rows, 2 * width), BF16),
            single_shape,
            single_shape,
        ],
        in_specs=anywhere(6),
        out_specs=anywhere(6),
        scratch_shapes=[
            pltpu.VMEM((7, rows, width), BF16),
            pltpu.VMEM((7, rows, width), BF16),
            pltpu.VMEM((5, rows, LANES), BF16),
            pltpu.VMEM((3, 32, rows), F32),
            pltpu.SemaphoreType.DMA((13,)),
        ],
        compiler_params=pltpu.CompilerParams(vmem_limit_bytes=VMEM_LIMIT),
        cost_estimate=pl.CostEstimate(
            flops=30 * 10 * rows * rows * LANES, bytes_accessed=30 * rows * width, transcendentals=30 * rows * rows
        ),
        name="far_pairs",
    )(y1, rest, r1, r2, s1, s2)


def near_pairs(y1, rest, key_edge, query_edge):
    rows = rest.shape[0]
    width = rest.shape[1] // 3
    half = width // 2
    count = half // LANES
    heads = 2 * count
    total = rows + EDGE

    def body(y1, rest, kedge, qedge, dw, dy1, dy2, dkedge, dqedge, qbuf, kbuf, dq, dk, kmeta, qmeta, info, sems):
        low = lax.axis_index("ctx") < 2
        left, right = pl.ds(0, half), pl.ds(half, half)
        own, past = pl.ds(0, rows), pl.ds(rows, EDGE)
        main = pl.ds(0, width)

        def halves(array, there, back=False, start=0, parts=2):
            todo = []
            for i in range(2):
                for j in range(parts):
                    wide = array.at[:, pl.ds(start + j * width + i * half, half)]
                    narrow = there(i, right if j else left)
                    todo.append((narrow, wide) if back else (wide, narrow))
            return todo

        shared = run_copies(
            [
                (y1.at[:, pl.ds(width, LANES)], kmeta.at[own]),
                (y1.at[:, pl.ds(width, LANES)], qmeta.at[own]),
                (kedge.at[:, pl.ds(2 * width, LANES)], kmeta.at[past]),
                (qedge.at[:, pl.ds(2 * width, LANES)], qmeta.at[past]),
            ]
            + halves(kedge, lambda i, cols: kbuf.at[i, past, cols])
            + halves(qedge, lambda i, cols: qbuf.at[i, past, cols]),
            sems,
        )

        @pl.when(low)
        def _():
            todo = halves(rest, lambda i, cols: qbuf.at[i, own, cols], start=width)
            todo += [(rest.at[:, main], kbuf.at[0, own]), (y1.at[:, main], kbuf.at[1, own])]
            wait_all(run_copies(todo, sems, 12))

        @pl.when(jnp.logical_not(low))
        def _():
            todo = halves(rest, lambda i, cols: kbuf.at[i, own, cols], start=width)
            todo += [(y1.at[:, main], qbuf.at[0, own]), (rest.at[:, main], qbuf.at[1, own])]
            wait_all(run_copies(todo, sems, 12))

        wait_all(shared)
        info[...] = token_rows(qmeta[...], heads)
        id_lane = lax.broadcasted_iota(jnp.int32, (total, LANES), 1) == 3 * heads
        key_ids = jnp.sum(jnp.where(id_lane, kmeta[...].astype(F32), 0.0), axis=1, keepdims=True)
        at_key = lax.broadcasted_iota(jnp.int32, (total, total), 0)
        at_query = lax.broadcasted_iota(jnp.int32, (total, total), 1)
        visible = (key_ids <= info[2 * heads : 2 * heads + 1, :]) & ((at_key < rows) | (at_query < rows - EDGE))
        for i in range(2):

            def step(c, carry, i=i):
                a = pl.ds(pl.multiple_of(c * LANES, LANES), LANES)
                b = pl.ds(pl.multiple_of(half + c * LANES, LANES), LANES)
                head = i * count + c
                query_term, key_term, value_term = pair_terms(
                    qbuf[i, :, a],
                    qbuf[i, :, b],
                    kbuf[i, :, a],
                    kbuf[i, :, b],
                    info[pl.ds(head, 1), :],
                    info[pl.ds(heads + head, 1), :],
                    visible,
                )
                dq[i, :, a] = query_term.astype(BF16)
                dk[i, :, a] = key_term.astype(BF16)
                dk[i, :, b] = value_term.astype(BF16)
                return carry

            lax.fori_loop(0, count, step, 0, unroll=True)

        made = run_copies(
            halves(dkedge, lambda i, cols: dk.at[i, past, cols], back=True)
            + halves(dqedge, lambda i, cols: dq.at[i, past, cols], back=True, parts=1),
            sems,
        )

        @pl.when(low)
        def _():
            todo = [(dq.at[0, own], dw.at[:, left]), (dq.at[1, own], dw.at[:, right])]
            todo += [(dk.at[0, own], dy2), (dk.at[1, own], dy1)]
            wait_all(run_copies(todo, sems, 12))

        @pl.when(jnp.logical_not(low))
        def _():
            todo = halves(dw, lambda i, cols: dk.at[i, own, cols], back=True)
            todo += [(dq.at[0, own], dy1.at[:, left]), (dq.at[1, own], dy2.at[:, left])]
            wait_all(run_copies(todo, sems, 12))

        wait_all(made)

    return pl.pallas_call(
        body,
        out_shape=[
            jax.ShapeDtypeStruct((rows, 2 * width), BF16),
            jax.ShapeDtypeStruct((rows, width), BF16),
            jax.ShapeDtypeStruct((rows, width), BF16),
            jax.ShapeDtypeStruct((EDGE, 2 * width), BF16),
            jax.ShapeDtypeStruct((EDGE, width), BF16),
        ],
        in_specs=anywhere(4),
        out_specs=anywhere(5),
        scratch_shapes=[
            pltpu.VMEM((2, total, width), BF16),
            pltpu.VMEM((2, total, width), BF16),
            pltpu.VMEM((2, total, half), BF16),
            pltpu.VMEM((2, total, width), BF16),
            pltpu.VMEM((total, LANES), BF16),
            pltpu.VMEM((total, LANES), BF16),
            pltpu.VMEM((32, total), F32),
            pltpu.SemaphoreType.DMA((18,)),
        ],
        compiler_params=pltpu.CompilerParams(vmem_limit_bytes=VMEM_LIMIT),
        cost_estimate=pl.CostEstimate(
            flops=10 * 10 * rows * rows * LANES, bytes_accessed=16 * rows * width, transcendentals=10 * rows * rows
        ),
        name="near_pairs",
    )(y1, rest, key_edge, query_edge)


def finish_first(dw, l1, dy2, l2, out1, dkedge, dqedge):
    rows, width = dy2.shape
    half = width // 2

    def body(dw, l1, dy2, l2, out1, dk, dq, e, v):
        z = lax.axis_index("ctx")
        low, middle = z < 2, (z == 1) | (z == 2)

        def own(cols):
            return dw[:, cols].astype(F32) + jnp.where(middle, l1[:, cols].astype(F32), 0.0)

        def second(cols):
            return dy2[:, cols].astype(F32) + jnp.where(middle, l2[:, cols].astype(F32), 0.0) + out1[:, cols].astype(F32)

        def put(dst, cols, total, first, last=None):
            end = total[rows - EDGE :] if last is None else total[rows - EDGE :] + last
            total = jnp.concatenate([total[:EDGE] + first, total[EDGE : rows - EDGE], end], axis=0)
            dst[:, cols] = total.astype(BF16)

        def key_edge(cols):
            return dk[:, cols].astype(F32)

        def query_edge(cols):
            return dq[:, cols].astype(F32)

        a, b = pl.ds(0, half), pl.ds(half, half)
        c, d = pl.ds(width, half), pl.ds(width + half, half)
        for cols in (a, b):
            put(e, cols, own(cols), jnp.where(low, 0.0, key_edge(cols)), jnp.where(low, query_edge(cols), 0.0))
        put(e, c, second(a), jnp.where(low, key_edge(a), 0.0), jnp.where(low, 0.0, query_edge(b)))
        put(e, d, jnp.where(low, second(b), own(c)), key_edge(c))
        put(v, pl.ds(0, half), own(d), key_edge(d))

    return pl.pallas_call(
        body,
        out_shape=[jax.ShapeDtypeStruct((rows, 2 * width), BF16), jax.ShapeDtypeStruct((rows, half), BF16)],
        in_specs=[pl.BlockSpec(memory_space=pltpu.VMEM)] * 7,
        out_specs=[pl.BlockSpec(memory_space=pltpu.VMEM)] * 2,
        compiler_params=pltpu.CompilerParams(vmem_limit_bytes=32 * 2**20),
        cost_estimate=pl.CostEstimate(flops=0, bytes_accessed=16 * rows * width, transcendentals=0),
        name="finish_first",
    )(dw, l1, dy2, l2, out1, dkedge, dqedge)


def finish_second(dy1, swap2, out2, v, dkedge, dqedge):
    rows, width = dy1.shape
    half = width // 2

    def body(dy1, swap2, out2, v, dk, dq, e):
        low = lax.axis_index("ctx") < 2
        a, b = pl.ds(0, half), pl.ds(half, half)
        end = pl.ds(width + half, half)

        def total(cols):
            return dy1[:, cols].astype(F32) + swap2[:, cols].astype(F32) + out2[:, cols].astype(F32)

        left = total(a)
        first = left[:EDGE] + jnp.where(low, dk[:, b].astype(F32), 0.0)
        last = left[rows - EDGE :] + jnp.where(low, 0.0, dq[:, a].astype(F32))
        e[:, a] = jnp.concatenate([first, left[EDGE : rows - EDGE], last], axis=0).astype(BF16)
        right = total(b)
        right = jnp.concatenate([right[:EDGE] + dk[:, end].astype(F32), right[EDGE:]], axis=0)
        e[:, b] = jnp.where(low, right.astype(BF16), v[...])

    return pl.pallas_call(
        body,
        out_shape=jax.ShapeDtypeStruct((rows, width), BF16),
        in_specs=[pl.BlockSpec(memory_space=pltpu.VMEM)] * 6,
        out_specs=pl.BlockSpec(memory_space=pltpu.VMEM),
        compiler_params=pltpu.CompilerParams(vmem_limit_bytes=32 * 2**20),
        cost_estimate=pl.CostEstimate(flops=0, bytes_accessed=9 * rows * width, transcendentals=0),
        name="finish_second",
    )(dy1, swap2, out2, v, dkedge, dqedge)


def unpack(early, late):
    groups, rows, width = late.shape
    half = width // 2

    def body(early, late, dq, dk, dv, first, second, third, sems):
        low = lax.axis_index("ctx") < 2
        todo = []
        for h in range(groups):
            todo.append((early.at[h, :, pl.ds(0, width)], first.at[:, pl.ds(h * width, width)]))
        for h in range(groups):
            todo.append((early.at[h, :, pl.ds(width + half, half)], third.at[:, pl.ds(h * width, half)]))
            todo.append((late.at[h, :, pl.ds(half, half)], third.at[:, pl.ds(h * width + half, half)]))
        for h in range(groups):
            here = pl.multiple_of(h * width + jnp.where(low, 0, half), LANES)
            there = pl.multiple_of(h * width + jnp.where(low, half, 0), LANES)
            todo.append((early.at[h, :, pl.ds(width, half)], second.at[:, pl.ds(here, half)]))
            todo.append((late.at[h, :, pl.ds(0, half)], second.at[:, pl.ds(there, half)]))
        loads = run_copies(todo, sems)
        count = len(loads)
        wait_all(loads[:groups])

        @pl.when(low)
        def _():
            run_copies([(first, dq)], sems, count)

        @pl.when(jnp.logical_not(low))
        def _():
            run_copies([(first, dk)], sems, count)

        wait_all(loads[groups : 3 * groups])
        run_copies([(third, dv)], sems, count + 1)
        wait_all(loads[3 * groups :])

        @pl.when(low)
        def _():
            wait_all(run_copies([(second, dk)], sems, count + 2))
            pltpu.make_async_copy(first, dq, sems.at[count]).wait()

        @pl.when(jnp.logical_not(low))
        def _():
            wait_all(run_copies([(second, dq)], sems, count + 2))
            pltpu.make_async_copy(first, dk, sems.at[count]).wait()

        pltpu.make_async_copy(third, dv, sems.at[count + 1]).wait()

    shape = jax.ShapeDtypeStruct((rows, groups * width), BF16)
    return pl.pallas_call(
        body,
        out_shape=[shape] * 3,
        in_specs=anywhere(2),
        out_specs=anywhere(3),
        scratch_shapes=[pltpu.VMEM((rows, groups * width), BF16)] * 3 + [pltpu.SemaphoreType.DMA((3 + 5 * groups,))],
        cost_estimate=pl.CostEstimate(flops=0, bytes_accessed=6 * rows * groups * width * 2, transcendentals=0),
        name="unpack",
    )(early, late)


def after(array, other):
    return lax.optimization_barrier((array, other))[0]


def local_split(queries, keys_in, values_in, attn_out, out_grad, log_norm, span_id):
    groups = lax.axis_size("head")
    width = queries.shape[1] // groups

    def to_heads(x):
        y = lax.all_to_all(x, "head", split_axis=0, concat_axis=0, tiled=True)
        return y.reshape(-1, y.shape[2])

    def to_tokens(x):
        x = x.reshape(groups, -1, x.shape[1])
        return lax.all_to_all(x, "head", split_axis=0, concat_axis=0, tiled=True)

    x1, rest = pack(queries, keys_in, values_in, attn_out, out_grad, span_id.reshape(1, -1), groups, width)
    y1 = add_norm(to_heads(x1), log_norm.T)
    r1 = lax.ppermute(y1, "ctx", INWARD)
    s1 = lax.ppermute(y1, "ctx", SWAP)
    rest = to_heads(after(rest, y1))
    y2, key_edge, query_edge = cut(y1, rest)
    y2, r1, s1 = lax.optimization_barrier((y2, r1, s1))
    r2 = lax.ppermute(y2, "ctx", INWARD)
    s2 = lax.ppermute(r1, "ctx", SWAP)
    key_edge = lax.ppermute(key_edge, "ctx", DOWN)
    query_edge = lax.ppermute(query_edge, "ctx", UP)
    rest, key_edge, query_edge = lax.optimization_barrier((rest, key_edge, query_edge))
    swap1, out1, swap2, l1, l2, l3 = far_pairs(y1, rest, r1, r2, s1, s2)
    dw, dy1, dy2, dkedge, dqedge = near_pairs(y1, rest, after(key_edge, l3), query_edge)
    swap1 = lax.ppermute(swap1, "ctx", SWAP)
    out1 = lax.ppermute(out1, "ctx", OUTWARD)
    dkedge = lax.ppermute(dkedge, "ctx", UP)
    dqedge = lax.ppermute(dqedge, "ctx", DOWN)
    sum1 = (swap1.astype(F32) + l3.astype(F32)).astype(BF16)
    swap2 = lax.ppermute(after(swap2, swap1), "ctx", SWAP)
    out2 = lax.ppermute(sum1, "ctx", OUTWARD)
    dkedge, dqedge, out1 = after((dkedge, dqedge, out1), sum1)
    early, kept = finish_first(dw, l1, dy2, l2, out1, dkedge, dqedge)
    late = finish_second(dy1, swap2, out2, kept, dkedge, dqedge)
    return tuple(unpack(to_tokens(early), to_tokens(late)))


def splits(tokens, blocks, head_width, heads):
    if blocks != 4 or heads % 2 or head_width != LANES or 6 * heads + 1 > LANES:
        return False
    block = tokens // blocks
    span = -(-tokens // SPANS)
    for offset in range(SPANS * span - tokens + 1):
        for end in range(block, tokens, block):
            start = (end - 1 + offset) // span * span - offset
            if min(end - start, start + span - end) > EDGE or max(end - start, span) > block:
                return False
    return block % EDGE == 0


def local(queries, keys_in, values_in, attn_out, out_grad, log_norm, span_id):
    blocks, groups = lax.axis_size("ctx"), lax.axis_size("head")
    heads = log_norm.shape[1]
    tokens = queries.shape[0] * blocks * groups
    plan = local_plain
    if splits(tokens, blocks, queries.shape[1] // (heads * groups), heads):
        plan = local_split
    return plan(queries, keys_in, values_in, attn_out, out_grad, log_norm, span_id)


def solution(mesh):
    placed = (
        P(("clip", "ctx", "head"), None),
        P(("clip", "ctx", "head"), None),
        P(("clip", "ctx", "head"), None),
        P(("clip", "ctx", "head"), None),
        P(("clip", "ctx", "head"), None),
        P(("clip", "ctx"), "head"),
        P(("clip", "ctx", "head")),
    )
    return jax.shard_map(
        local,
        mesh=mesh,
        in_specs=placed,
        out_specs=(
            P(("clip", "ctx", "head"), None),
            P(("clip", "ctx", "head"), None),
            P(("clip", "ctx", "head"), None),
        ),
        check_vma=False,
    )
```

```python
import math

import jax
import jax.numpy as jnp
from jax import lax
from jax.experimental import pallas as pl
from jax.experimental.pallas import tpu as pltpu
from jax.sharding import PartitionSpec as P

SPANS = 12
EDGE = 16
VMEM_LIMIT = 32 * 2**20
VMEM_SMALL = 16 * 2**20
VMEM_WHOLE = 60 * 2**20
LANES = 128
BF16 = jnp.bfloat16
F32 = jnp.float32

INWARD = ((0, 1), (3, 2))
SWAP = ((1, 2), (2, 1))
OUTWARD = ((1, 0), (2, 3))
DOWN = ((1, 0), (2, 1), (3, 2))
UP = ((0, 1), (1, 2), (2, 3))


def tile_terms(query_blk, grad_blk, norm_blk, delta_blk, query_ids, key_blk, value_blk, key_ids):
    row_count = query_blk.shape[0]
    key_count = key_blk.shape[0]
    head_count = norm_blk.shape[1]
    head_width = query_blk.shape[1] // head_count
    scale = 1.0 / math.sqrt(head_width)
    query3 = query_blk.reshape(row_count, head_count, head_width)
    grad3 = grad_blk.reshape(row_count, head_count, head_width)
    key3 = key_blk.reshape(key_count, head_count, head_width)
    value3 = value_blk.reshape(key_count, head_count, head_width)
    scores = jnp.einsum("rhd,khd->hrk", query3, key3, preferred_element_type=jnp.float32)
    visible = key_ids[None, :] <= query_ids[:, None]
    weight = jnp.where(visible[None], jnp.exp(scores * scale - norm_blk.T[:, :, None]), 0.0)
    weight_low = weight.astype(jnp.bfloat16)
    dweight = jnp.einsum("rhd,khd->hrk", grad3, value3, preferred_element_type=jnp.float32)
    dscore = (weight * (dweight - delta_blk.T[:, :, None]) * scale).astype(jnp.bfloat16)
    query_term = jnp.einsum("hrk,khd->rhd", dscore, key3, preferred_element_type=jnp.float32)
    key_term = jnp.einsum("hrk,rhd->khd", dscore, query3, preferred_element_type=jnp.float32)
    value_term = jnp.einsum("hrk,rhd->khd", weight_low, grad3, preferred_element_type=jnp.float32)
    return (
        query_term.reshape(row_count, -1),
        key_term.reshape(key_count, -1),
        value_term.reshape(key_count, -1),
    )


def rounded(term):
    return lax.optimization_barrier(term.astype(jnp.bfloat16)).astype(jnp.float32)


def local_plain(queries, keys_in, values_in, attn_out, out_grad, log_norm, span_id):
    local_q, local_k, local_v, local_out, local_grad = (
        lax.all_to_all(queries, "head", split_axis=1, concat_axis=0, tiled=True),
        lax.all_to_all(keys_in, "head", split_axis=1, concat_axis=0, tiled=True),
        lax.all_to_all(values_in, "head", split_axis=1, concat_axis=0, tiled=True),
        lax.all_to_all(attn_out, "head", split_axis=1, concat_axis=0, tiled=True),
        lax.all_to_all(out_grad, "head", split_axis=1, concat_axis=0, tiled=True),
    )
    all_ids = lax.all_gather(span_id, ("ctx", "head"), axis=0, tiled=True)
    seg_rows = local_q.shape[0]
    block_count = lax.axis_size("ctx")
    head_count = log_norm.shape[1]
    head_width = local_q.shape[1] // head_count
    my_block = lax.axis_index("ctx")
    own_ids = lax.dynamic_slice_in_dim(all_ids, my_block * seg_rows, seg_rows)
    id_blocks = all_ids.reshape(block_count, seg_rows)
    deltas = jnp.sum(
        (local_grad.astype(jnp.float32) * local_out.astype(jnp.float32)).reshape(
            seg_rows, head_count, head_width
        ),
        axis=2,
    )
    far_queries, far_grads = (
        lax.all_gather(local_q, "ctx", axis=0, tiled=True),
        lax.all_gather(local_grad, "ctx", axis=0, tiled=True),
    )
    far_norms, far_deltas = (
        lax.all_gather(log_norm, "ctx", axis=0, tiled=True),
        lax.all_gather(deltas, "ctx", axis=0, tiled=True),
    )

    def query_step(totals, piece):
        query_blk, grad_blk, norm_blk, delta_blk, query_ids = piece
        query_term, key_term, value_term = tile_terms(
            query_blk, grad_blk, norm_blk, delta_blk, query_ids, local_k, local_v, own_ids
        )
        return ((totals[0] + rounded(key_term), totals[1] + rounded(value_term)), query_term)

    zero_block = jnp.zeros(local_k.shape, jnp.float32)
    (dk_total, dv_total), query_terms = lax.scan(
        query_step,
        (zero_block, zero_block),
        (
            far_queries.reshape(block_count, seg_rows, -1),
            far_grads.reshape(block_count, seg_rows, -1),
            far_norms.reshape(block_count, seg_rows, -1),
            far_deltas.reshape(block_count, seg_rows, -1),
            id_blocks,
        ),
    )
    query_sum = lax.psum_scatter(
        query_terms.reshape(block_count * seg_rows, -1).astype(jnp.bfloat16),
        "ctx",
        scatter_dimension=0,
        tiled=True,
    )
    dk_local = dk_total.astype(jnp.bfloat16)
    dv_local = dv_total.astype(jnp.bfloat16)
    query_grad, key_grad, value_grad = (
        lax.all_to_all(query_sum, "head", split_axis=0, concat_axis=1, tiled=True),
        lax.all_to_all(dk_local, "head", split_axis=0, concat_axis=1, tiled=True),
        lax.all_to_all(dv_local, "head", split_axis=0, concat_axis=1, tiled=True),
    )
    return (query_grad, key_grad, value_grad)


def nt(a, b):
    return lax.dot_general(a, b, (((1,), (1,)), ((), ())), preferred_element_type=F32)


def tn(a, b):
    return lax.dot_general(a, b, (((0,), (0,)), ((), ())), preferred_element_type=F32)


def pieces(value):
    high = value.astype(BF16)
    rest = value - high.astype(F32)
    middle = rest.astype(BF16)
    low = (rest - middle.astype(F32)).astype(BF16)
    return high, middle, low


def run_copies(pairs, sems, first=0):
    made = [pltpu.make_async_copy(src, dst, sems.at[first + i]) for i, (src, dst) in enumerate(pairs)]
    for copy in made:
        copy.start()
    return made


def wait_all(made):
    for copy in made:
        copy.wait()


def anywhere(count):
    return [pl.BlockSpec(memory_space=pl.ANY)] * count


def pack(queries, keys_in, values_in, attn_out, out_grad, span_row, groups, width):
    rows = queries.shape[0]
    heads = width // LANES
    half = width // 2

    def body(q, k, v, o, g, ids, *refs):
        x1, x2, x3 = refs[:groups], refs[groups : 2 * groups], refs[2 * groups : 3 * groups]
        q_v, k_v, v_v, o_v, g_v, meta, sems = refs[3 * groups :]
        here = lax.axis_index("head")
        low = lax.axis_index("ctx") < 2
        loads = run_copies([(k, k_v), (v, v_v), (q, q_v), (g, g_v), (o, o_v)], sems)

        def moves(first, second, third, fourth, near, far):
            todo = []
            for m in range(groups):
                base = pl.multiple_of((here ^ m) * width, LANES)
                todo.append((first.at[:, pl.ds(base + near, half)], x1[m].at[:, pl.ds(0, half)]))
                todo.append((second.at[:, pl.ds(base + near, half)], x1[m].at[:, pl.ds(half, half)]))
            for m in range(groups):
                base = pl.multiple_of((here ^ m) * width, LANES)
                todo.append((first.at[:, pl.ds(base + far, half)], x2[m].at[:, pl.ds(0, half)]))
                todo.append((second.at[:, pl.ds(base + far, half)], x2[m].at[:, pl.ds(half, half)]))
                todo.append((third.at[:, pl.ds(base, width)], x3[m].at[:, pl.ds(0, width)]))
                todo.append((fourth.at[:, pl.ds(base, width)], x3[m].at[:, pl.ds(width, width)]))
            return [pltpu.make_async_copy(src, dst, sems.at[5 + i]) for i, (src, dst) in enumerate(todo)]

        low_moves = (k_v, v_v, q_v, g_v, half, 0)
        high_moves = (q_v, g_v, k_v, v_v, 0, half)
        wait_all(loads[:4])

        @pl.when(low)
        def _():
            for copy in moves(*low_moves):
                copy.start()

        @pl.when(jnp.logical_not(low))
        def _():
            for copy in moves(*high_moves):
                copy.start()

        wait_all(loads[4:])
        lane = lax.broadcasted_iota(jnp.int32, (rows, LANES), 1)
        slot = jnp.where(lane < 3 * heads, lane % heads, -1)
        at_row = lax.broadcasted_iota(jnp.int32, (rows, rows), 0)
        at_col = lax.broadcasted_iota(jnp.int32, (rows, rows), 1)
        own = jnp.sum(jnp.where(at_row == at_col, ids[...].astype(F32), 0.0), axis=1, keepdims=True)
        for h in range(groups):
            total = jnp.zeros((rows, LANES), F32)
            for c in range(heads):
                cols = pl.ds(h * width + c * LANES, LANES)
                delta = jnp.sum(o_v[:, cols].astype(F32) * g_v[:, cols].astype(F32), axis=1, keepdims=True)
                total = jnp.where(slot == c, delta, total)
            high, middle, lowest = pieces(total)
            kept = jnp.where(lane < heads, high, jnp.where(lane < 2 * heads, middle, lowest))
            meta[h] = jnp.where(lane < 3 * heads, kept, jnp.where(lane == 3 * heads, own.astype(BF16), 0.0).astype(BF16))
        last = run_copies(
            [(meta.at[here ^ m], x1[m].at[:, pl.ds(width, LANES)]) for m in range(groups)], sems, 5 + 6 * groups
        )

        @pl.when(low)
        def _():
            wait_all(moves(*low_moves))

        @pl.when(jnp.logical_not(low))
        def _():
            wait_all(moves(*high_moves))

        wait_all(last)

    whole = pltpu.VMEM((rows, groups * width), BF16)
    made = pl.pallas_call(
        body,
        out_shape=[
            jax.ShapeDtypeStruct((rows, size), BF16)
            for size in (width + LANES, width, 2 * width)
            for _ in range(groups)
        ],
        in_specs=anywhere(5) + [pl.BlockSpec(memory_space=pltpu.VMEM)],
        out_specs=anywhere(3 * groups),
        scratch_shapes=[whole] * 5
        + [pltpu.VMEM((groups, rows, LANES), BF16), pltpu.SemaphoreType.DMA((5 + 7 * groups,))],
        cost_estimate=pl.CostEstimate(flops=0, bytes_accessed=10 * rows * groups * width * 2, transcendentals=0),
        compiler_params=pltpu.CompilerParams(vmem_limit_bytes=VMEM_WHOLE),
        name="pack",
    )(queries, keys_in, values_in, attn_out, out_grad, span_row)
    return made[:groups], made[groups : 2 * groups], made[2 * groups :]


def join_first(parts, norm_rows):
    groups = len(parts)
    rows, width = parts[0].shape
    heads = norm_rows.shape[0]

    def body(*refs):
        norm, y, sems = refs[groups:]
        here = lax.axis_index("head")
        made = run_copies([(refs[m], y.at[here ^ m]) for m in range(groups)], sems)
        at_row = lax.broadcasted_iota(jnp.int32, (heads, LANES), 0)
        at_lane = lax.broadcasted_iota(jnp.int32, (heads, LANES), 1)
        total = jnp.zeros((groups * rows, LANES), F32)
        for i, piece in enumerate(pieces(norm[...])):
            place = jnp.where(at_lane == at_row + (3 * heads + 1 + i * heads), 1.0, 0.0).astype(BF16)
            total += tn(piece, place)
        wait_all(made)
        tail = pl.ds(width - LANES, LANES)
        for h in range(groups):
            y[h, :, tail] = (y[h, :, tail].astype(F32) + total[h * rows : (h + 1) * rows]).astype(BF16)

    return pl.pallas_call(
        body,
        out_shape=jax.ShapeDtypeStruct((groups, rows, width), BF16),
        in_specs=anywhere(groups) + [pl.BlockSpec(memory_space=pltpu.VMEM)],
        out_specs=pl.BlockSpec(memory_space=pltpu.VMEM),
        scratch_shapes=[pltpu.SemaphoreType.DMA((groups,))],
        cost_estimate=pl.CostEstimate(flops=0, bytes_accessed=4 * groups * rows * width, transcendentals=0),
        compiler_params=pltpu.CompilerParams(vmem_limit_bytes=VMEM_SMALL),
        name="join_first",
    )(*parts, norm_rows).reshape(groups * rows, width)


def join(parts):
    groups = len(parts)
    rows, width = parts[0].shape

    def body(*refs):
        y, sems = refs[groups:]
        here = lax.axis_index("head")
        wait_all(run_copies([(refs[m], y.at[here ^ m]) for m in range(groups)], sems))

    return pl.pallas_call(
        body,
        out_shape=jax.ShapeDtypeStruct((groups, rows, width), BF16),
        in_specs=anywhere(groups),
        out_specs=pl.BlockSpec(memory_space=pltpu.VMEM),
        scratch_shapes=[pltpu.SemaphoreType.DMA((groups,))],
        cost_estimate=pl.CostEstimate(flops=0, bytes_accessed=4 * groups * rows * width, transcendentals=0),
        compiler_params=pltpu.CompilerParams(vmem_limit_bytes=VMEM_SMALL),
        name="join",
    )(*parts).reshape(groups * rows, width)


def token_rows(meta, heads):
    at_row = lax.broadcasted_iota(jnp.int32, (32, LANES), 0)
    at_lane = lax.broadcasted_iota(jnp.int32, (32, LANES), 1)
    norm_lane = at_lane - (3 * heads + 1)
    is_norm = (norm_lane >= 0) & (norm_lane < 3 * heads) & (norm_lane % heads == at_row) & (at_row < heads)
    is_delta = (at_lane < 3 * heads) & (at_lane % heads == at_row - heads) & (at_row >= heads)
    is_id = (at_lane == 3 * heads) & (at_row == 2 * heads)
    chosen = jnp.where(is_norm | is_delta | is_id, 1.0, 0.0).astype(BF16)
    return nt(chosen, meta)


def pair_terms(query, grad, key, value, norm, delta, visible=None):
    scale = 1.0 / math.sqrt(query.shape[1])
    weight = jnp.exp(nt(key, query) * scale - norm)
    if visible is not None:
        weight = jnp.where(visible, weight, 0.0)
    dscore = (weight * (nt(value, grad) - delta) * scale).astype(BF16)
    value_term = jnp.dot(weight.astype(BF16), grad, preferred_element_type=F32)
    key_term = jnp.dot(dscore, query, preferred_element_type=F32)
    query_term = tn(dscore, key)
    return query_term, key_term, value_term


def join_last(parts, y1, y2):
    groups = len(parts)
    share = parts[0].shape[0]
    rows, width = y2.shape
    half = width // 2

    def body(*refs):
        y1, y2, w, kedge, qedge, sems = refs[groups:]
        here, low = lax.axis_index("head"), lax.axis_index("ctx") < 2
        top, bottom, tail = pl.ds(0, EDGE), pl.ds(rows - EDGE, EDGE), pl.ds(width, LANES)
        whole, end = pl.ds(0, 2 * width), pl.ds(2 * width, LANES)
        made = run_copies([(y1.at[top, tail], kedge.at[:, end]), (y1.at[bottom, tail], qedge.at[:, end])], sems)
        loads = run_copies([(refs[m], w.at[here ^ m]) for m in range(groups)], sems, 2)

        def joined(first, second, at, edge):
            todo = []
            for i in range(2):
                for j, part in enumerate((first, second)):
                    todo.append((part.at[at, pl.ds(i * half, half)], edge.at[:, pl.ds(i * width + j * half, half)]))
            return todo

        @pl.when(low)
        def _():
            wait_all(run_copies(joined(y2, y1, top, kedge), sems, 2 + groups))

        @pl.when(jnp.logical_not(low))
        def _():
            wait_all(run_copies(joined(y1, y2, bottom, qedge), sems, 2 + groups))

        wait_all(loads)

        @pl.when(low)
        def _():
            qedge[:, whole] = w[groups - 1, share - EDGE :, :]

        @pl.when(jnp.logical_not(low))
        def _():
            kedge[:, whole] = w[0, :EDGE, :]

        wait_all(made)

    edge = jax.ShapeDtypeStruct((EDGE, 2 * width + LANES), BF16)
    w, key_edge, query_edge = pl.pallas_call(
        body,
        out_shape=[jax.ShapeDtypeStruct((groups, share, 2 * width), BF16), edge, edge],
        in_specs=anywhere(groups + 2),
        out_specs=[pl.BlockSpec(memory_space=pltpu.VMEM)] * 3,
        scratch_shapes=[pltpu.SemaphoreType.DMA((6 + groups,))],
        compiler_params=pltpu.CompilerParams(vmem_limit_bytes=VMEM_SMALL),
        cost_estimate=pl.CostEstimate(flops=0, bytes_accessed=8 * rows * width, transcendentals=0),
        name="join_last",
    )(*parts, y1, y2)
    return w.reshape(rows, 2 * width), key_edge, query_edge


def far_pairs(y1, y2, w, r1, r2, s1, s2):
    rows, width = r2.shape
    half = width // 2
    count = half // LANES
    heads = 2 * count

    def body(y1, y2, w, r1, r2, s1, s2, swap1, out1, swap2, l1, l2, l3, buf, grads, meta, info, sems):
        z = lax.axis_index("ctx")
        one = z == 1

        def pick(a, b):
            return jnp.where(one, a, b)

        @pl.when((z == 1) | (z == 2))
        def _():
            near = pl.multiple_of(pick(0, half), LANES)
            other = pl.multiple_of(pick(half, 0), LANES)
            main = pl.ds(0, width)
            tail = pl.ds(width, LANES)
            left, right = pl.ds(0, half), pl.ds(half, half)
            made = run_copies(
                [
                    (y1.at[:, tail], meta.at[pick(2, 0)]),
                    (s1.at[:, tail], meta.at[pick(0, 3)]),
                    (s2.at[:, tail], meta.at[pick(1, 4)]),
                    (r1.at[:, tail], meta.at[pick(3, 1)]),
                    (s1.at[:, main], buf.at[pick(0, 3)]),
                    (s2.at[:, main], buf.at[pick(1, 2)]),
                    (r2, buf.at[pick(2, 1)]),
                    (y2, buf.at[pick(3, 0)]),
                    (w.at[:, pl.ds(near, half)], buf.at[4, :, left]),
                    (w.at[:, pl.ds(width + near, half)], buf.at[4, :, right]),
                    (w.at[:, pl.ds(other, half)], buf.at[5, :, left]),
                    (w.at[:, pl.ds(width + other, half)], buf.at[5, :, right]),
                    (r1.at[:, main], buf.at[6]),
                ],
                sems,
            )
            wait_all(made)
            for i in range(3):
                info[i] = token_rows(meta[i], heads)
            first_active = pick(0, count)
            first_other = pick(count, 0)
            zero = jnp.zeros((rows, LANES), BF16)

            def single(q_slot, k_slot, c, head):
                a = pl.ds(pl.multiple_of(c * LANES, LANES), LANES)
                b = pl.ds(pl.multiple_of(half + c * LANES, LANES), LANES)
                own = pick(2, 1)
                return pair_terms(
                    buf[q_slot, :, a],
                    buf[q_slot, :, b],
                    buf[k_slot, :, a],
                    buf[k_slot, :, b],
                    info[own, pl.ds(head, 1), :],
                    info[own, pl.ds(heads + head, 1), :],
                )

            def step(c, carry):
                a = pl.ds(pl.multiple_of(c * LANES, LANES), LANES)
                b = pl.ds(pl.multiple_of(half + c * LANES, LANES), LANES)
                head = first_active + c
                extra_q, extra_k, extra_v = single(pick(4, 1), pick(2, 4), c, head)
                key = buf[2:4, :, a].reshape(2 * rows, LANES)
                value = buf[2:4, :, b].reshape(2 * rows, LANES)
                key_sum, value_sum = None, None
                for i in range(2):
                    query_term, key_term, value_term = pair_terms(
                        buf[i, :, a],
                        buf[i, :, b],
                        key,
                        value,
                        info[i, pl.ds(head, 1), :],
                        info[i, pl.ds(heads + head, 1), :],
                    )
                    if i == 1:
                        query_term += jnp.where(one, 0.0, extra_q)
                    grads[i, :, a] = query_term.astype(BF16)
                    grads[i, :, b] = zero
                    key_sum = key_term if i == 0 else key_sum + key_term
                    value_sum = value_term if i == 0 else value_sum + value_term
                grads[2, :, a] = (key_sum[:rows] + jnp.where(one, extra_k, 0.0)).astype(BF16)
                grads[2, :, b] = (value_sum[:rows] + jnp.where(one, extra_v, 0.0)).astype(BF16)
                grads[3, :, a] = key_sum[rows:].astype(BF16)
                grads[3, :, b] = value_sum[rows:].astype(BF16)
                grads[4, :, a] = jnp.where(one, extra_q, extra_k).astype(BF16)
                grads[4, :, b] = jnp.where(one, 0.0, extra_v).astype(BF16)
                extra_q, extra_k, extra_v = single(pick(5, 6), pick(6, 5), c, first_other + c)
                grads[5, :, a] = jnp.where(one, extra_q, extra_k).astype(BF16)
                grads[5, :, b] = jnp.where(one, 0.0, extra_v).astype(BF16)
                grads[6, :, a] = jnp.where(one, extra_k, extra_q).astype(BF16)
                grads[6, :, b] = jnp.where(one, extra_v, 0.0).astype(BF16)
                return carry

            lax.fori_loop(0, count, step, 0, unroll=True)
            made = run_copies(
                [
                    (grads.at[pick(1, 2)], swap1),
                    (grads.at[pick(2, 1)], out1),
                    (grads.at[pick(0, 3)], swap2),
                    (grads.at[pick(3, 0)], l2),
                    (grads.at[6], l3),
                    (grads.at[4, :, left], l1.at[:, pl.ds(near, half)]),
                    (grads.at[4, :, right], l1.at[:, pl.ds(width + near, half)]),
                    (grads.at[5, :, left], l1.at[:, pl.ds(other, half)]),
                    (grads.at[5, :, right], l1.at[:, pl.ds(width + other, half)]),
                ],
                sems,
            )
            wait_all(made)

    single_shape = jax.ShapeDtypeStruct((rows, width), BF16)
    return pl.pallas_call(
        body,
        out_shape=[
            single_shape,
            single_shape,
            single_shape,
            jax.ShapeDtypeStruct((rows, 2 * width), BF16),
            single_shape,
            single_shape,
        ],
        in_specs=anywhere(7),
        out_specs=anywhere(6),
        scratch_shapes=[
            pltpu.VMEM((7, rows, width), BF16),
            pltpu.VMEM((7, rows, width), BF16),
            pltpu.VMEM((5, rows, LANES), BF16),
            pltpu.VMEM((3, 32, rows), F32),
            pltpu.SemaphoreType.DMA((13,)),
        ],
        compiler_params=pltpu.CompilerParams(vmem_limit_bytes=VMEM_LIMIT),
        cost_estimate=pl.CostEstimate(
            flops=30 * 10 * rows * rows * LANES, bytes_accessed=30 * rows * width, transcendentals=30 * rows * rows
        ),
        name="far_pairs",
    )(y1, y2, w, r1, r2, s1, s2)


def near_pairs(y1, y2, w, key_edge, query_edge):
    rows, width = y2.shape
    half = width // 2
    count = half // LANES
    heads = 2 * count
    total = rows + EDGE

    def body(y1, y2, w, kedge, qedge, dw, dy1, dy2, dkedge, dqedge, qbuf, kbuf, dq, dk, kmeta, qmeta, info, sems):
        low = lax.axis_index("ctx") < 2
        left, right = pl.ds(0, half), pl.ds(half, half)
        own, past = pl.ds(0, rows), pl.ds(rows, EDGE)
        main = pl.ds(0, width)

        def halves(array, there, back=False, parts=2):
            todo = []
            for i in range(2):
                for j in range(parts):
                    wide = array.at[:, pl.ds(j * width + i * half, half)]
                    narrow = there(i, right if j else left)
                    todo.append((narrow, wide) if back else (wide, narrow))
            return todo

        shared = run_copies(
            [
                (y1.at[:, pl.ds(width, LANES)], kmeta.at[own]),
                (y1.at[:, pl.ds(width, LANES)], qmeta.at[own]),
                (kedge.at[:, pl.ds(2 * width, LANES)], kmeta.at[past]),
                (qedge.at[:, pl.ds(2 * width, LANES)], qmeta.at[past]),
            ]
            + halves(kedge, lambda i, cols: kbuf.at[i, past, cols])
            + halves(qedge, lambda i, cols: qbuf.at[i, past, cols]),
            sems,
        )

        @pl.when(low)
        def _():
            todo = halves(w, lambda i, cols: qbuf.at[i, own, cols])
            todo += [(y2, kbuf.at[0, own]), (y1.at[:, main], kbuf.at[1, own])]
            wait_all(run_copies(todo, sems, 12))

        @pl.when(jnp.logical_not(low))
        def _():
            todo = halves(w, lambda i, cols: kbuf.at[i, own, cols])
            todo += [(y1.at[:, main], qbuf.at[0, own]), (y2, qbuf.at[1, own])]
            wait_all(run_copies(todo, sems, 12))

        wait_all(shared)
        info[...] = token_rows(qmeta[...], heads)
        id_lane = lax.broadcasted_iota(jnp.int32, (total, LANES), 1) == 3 * heads
        key_ids = jnp.sum(jnp.where(id_lane, kmeta[...].astype(F32), 0.0), axis=1, keepdims=True)
        at_key = lax.broadcasted_iota(jnp.int32, (total, total), 0)
        at_query = lax.broadcasted_iota(jnp.int32, (total, total), 1)
        visible = (key_ids <= info[2 * heads : 2 * heads + 1, :]) & ((at_key < rows) | (at_query < rows - EDGE))
        for i in range(2):

            def step(c, carry, i=i):
                a = pl.ds(pl.multiple_of(c * LANES, LANES), LANES)
                b = pl.ds(pl.multiple_of(half + c * LANES, LANES), LANES)
                head = i * count + c
                query_term, key_term, value_term = pair_terms(
                    qbuf[i, :, a],
                    qbuf[i, :, b],
                    kbuf[i, :, a],
                    kbuf[i, :, b],
                    info[pl.ds(head, 1), :],
                    info[pl.ds(heads + head, 1), :],
                    visible,
                )
                dq[i, :, a] = query_term.astype(BF16)
                dk[i, :, a] = key_term.astype(BF16)
                dk[i, :, b] = value_term.astype(BF16)
                return carry

            lax.fori_loop(0, count, step, 0, unroll=True)

        made = run_copies(
            halves(dkedge, lambda i, cols: dk.at[i, past, cols], back=True)
            + halves(dqedge, lambda i, cols: dq.at[i, past, cols], back=True, parts=1),
            sems,
        )

        @pl.when(low)
        def _():
            todo = [(dq.at[0, own], dw.at[:, left]), (dq.at[1, own], dw.at[:, right])]
            todo += [(dk.at[0, own], dy2), (dk.at[1, own], dy1)]
            wait_all(run_copies(todo, sems, 12))

        @pl.when(jnp.logical_not(low))
        def _():
            todo = halves(dw, lambda i, cols: dk.at[i, own, cols], back=True)
            todo += [(dq.at[0, own], dy1.at[:, left]), (dq.at[1, own], dy2.at[:, left])]
            wait_all(run_copies(todo, sems, 12))

        wait_all(made)

    return pl.pallas_call(
        body,
        out_shape=[
            jax.ShapeDtypeStruct((rows, 2 * width), BF16),
            jax.ShapeDtypeStruct((rows, width), BF16),
            jax.ShapeDtypeStruct((rows, width), BF16),
            jax.ShapeDtypeStruct((EDGE, 2 * width), BF16),
            jax.ShapeDtypeStruct((EDGE, width), BF16),
        ],
        in_specs=anywhere(5),
        out_specs=anywhere(5),
        scratch_shapes=[
            pltpu.VMEM((2, total, width), BF16),
            pltpu.VMEM((2, total, width), BF16),
            pltpu.VMEM((2, total, half), BF16),
            pltpu.VMEM((2, total, width), BF16),
            pltpu.VMEM((total, LANES), BF16),
            pltpu.VMEM((total, LANES), BF16),
            pltpu.VMEM((32, total), F32),
            pltpu.SemaphoreType.DMA((18,)),
        ],
        compiler_params=pltpu.CompilerParams(vmem_limit_bytes=VMEM_LIMIT),
        cost_estimate=pl.CostEstimate(
            flops=10 * 10 * rows * rows * LANES, bytes_accessed=16 * rows * width, transcendentals=10 * rows * rows
        ),
        name="near_pairs",
    )(y1, y2, w, key_edge, query_edge)


def finish_first(dw, l1, dy2, l2, out1, dkedge, dqedge, groups):
    rows, width = dy2.shape
    half = width // 2
    share = rows // groups

    def body(dw, l1, dy2, l2, out1, dk, dq, *refs):
        outs, v, e, sems = refs[:groups], *refs[groups:]
        here = lax.axis_index("head")
        z = lax.axis_index("ctx")
        low, middle = z < 2, (z == 1) | (z == 2)

        def own(cols):
            return dw[:, cols].astype(F32) + jnp.where(middle, l1[:, cols].astype(F32), 0.0)

        def second(cols):
            return dy2[:, cols].astype(F32) + jnp.where(middle, l2[:, cols].astype(F32), 0.0) + out1[:, cols].astype(F32)

        def put(dst, cols, total, first, last=None):
            end = total[rows - EDGE :] if last is None else total[rows - EDGE :] + last
            total = jnp.concatenate([total[:EDGE] + first, total[EDGE : rows - EDGE], end], axis=0)
            for h in range(groups):
                dst[h, :, cols] = total[h * share : (h + 1) * share].astype(BF16)

        def key_edge(cols):
            return dk[:, cols].astype(F32)

        def query_edge(cols):
            return dq[:, cols].astype(F32)

        a, b = pl.ds(0, half), pl.ds(half, half)
        c, d = pl.ds(width, half), pl.ds(width + half, half)
        for cols in (a, b):
            put(e, cols, own(cols), jnp.where(low, 0.0, key_edge(cols)), jnp.where(low, query_edge(cols), 0.0))
        put(e, c, second(a), jnp.where(low, key_edge(a), 0.0), jnp.where(low, 0.0, query_edge(b)))
        put(e, d, jnp.where(low, second(b), own(c)), key_edge(c))
        made = run_copies([(e.at[here ^ m], outs[m]) for m in range(groups)], sems)
        left_over = own(d)
        left_over = jnp.concatenate([left_over[:EDGE] + key_edge(d), left_over[EDGE:]], axis=0)
        v[...] = left_over.astype(BF16)
        wait_all(made)

    return pl.pallas_call(
        body,
        out_shape=[jax.ShapeDtypeStruct((share, 2 * width), BF16)] * groups + [jax.ShapeDtypeStruct((rows, half), BF16)],
        in_specs=[pl.BlockSpec(memory_space=pltpu.VMEM)] * 7,
        out_specs=anywhere(groups) + [pl.BlockSpec(memory_space=pltpu.VMEM)],
        scratch_shapes=[pltpu.VMEM((groups, share, 2 * width), BF16), pltpu.SemaphoreType.DMA((groups,))],
        compiler_params=pltpu.CompilerParams(vmem_limit_bytes=VMEM_SMALL),
        cost_estimate=pl.CostEstimate(flops=0, bytes_accessed=16 * rows * width, transcendentals=0),
        name="finish_first",
    )(dw, l1, dy2, l2, out1, dkedge, dqedge)


def finish_second(dy1, swap2, out2, v, dkedge, dqedge, groups):
    rows, width = dy1.shape
    half = width // 2
    share = rows // groups

    def body(dy1, swap2, out2, v, dk, dq, *refs):
        outs, e, sems = refs[:groups], *refs[groups:]
        here, low = lax.axis_index("head"), lax.axis_index("ctx") < 2

        def put(cols, whole):
            for h in range(groups):
                e[h, :, cols] = whole[h * share : (h + 1) * share].astype(BF16)

        a, b = pl.ds(0, half), pl.ds(half, half)
        end = pl.ds(width + half, half)

        def total(cols):
            return dy1[:, cols].astype(F32) + swap2[:, cols].astype(F32) + out2[:, cols].astype(F32)

        left = total(a)
        first = left[:EDGE] + jnp.where(low, dk[:, b].astype(F32), 0.0)
        last = left[rows - EDGE :] + jnp.where(low, 0.0, dq[:, a].astype(F32))
        put(a, jnp.concatenate([first, left[EDGE : rows - EDGE], last], axis=0))
        right = total(b)
        right = jnp.concatenate([right[:EDGE] + dk[:, end].astype(F32), right[EDGE:]], axis=0)
        put(b, jnp.where(low, right, v[...].astype(F32)))
        wait_all(run_copies([(e.at[here ^ m], outs[m]) for m in range(groups)], sems))

    return pl.pallas_call(
        body,
        out_shape=[jax.ShapeDtypeStruct((share, width), BF16)] * groups,
        in_specs=[pl.BlockSpec(memory_space=pltpu.VMEM)] * 6,
        out_specs=anywhere(groups),
        scratch_shapes=[pltpu.VMEM((groups, share, width), BF16), pltpu.SemaphoreType.DMA((groups,))],
        compiler_params=pltpu.CompilerParams(vmem_limit_bytes=VMEM_SMALL),
        cost_estimate=pl.CostEstimate(flops=0, bytes_accessed=9 * rows * width, transcendentals=0),
        name="finish_second",
    )(dy1, swap2, out2, v, dkedge, dqedge)


def unpack_early(parts):
    groups = len(parts)
    rows = parts[0].shape[0]
    width = parts[0].shape[1] // 2
    half = width // 2

    def body(*refs):
        dq, dk, dv, first, second, third, sems = refs[groups:]
        here, low = lax.axis_index("head"), lax.axis_index("ctx") < 2
        todo = []
        for m in range(groups):
            base = pl.multiple_of((here ^ m) * width, LANES)
            place = pl.multiple_of(base + jnp.where(low, 0, half), LANES)
            todo.append((refs[m].at[:, pl.ds(0, width)], first.at[:, pl.ds(base, width)]))
            todo.append((refs[m].at[:, pl.ds(width, half)], second.at[:, pl.ds(place, half)]))
            todo.append((refs[m].at[:, pl.ds(width + half, half)], third.at[:, pl.ds(base, half)]))
        wait_all(run_copies(todo, sems))

        @pl.when(low)
        def _():
            wait_all(run_copies([(first, dq), (second, dk), (third, dv)], sems))

        @pl.when(jnp.logical_not(low))
        def _():
            wait_all(run_copies([(first, dk), (second, dq), (third, dv)], sems))

    shape = jax.ShapeDtypeStruct((rows, groups * width), BF16)
    return pl.pallas_call(
        body,
        out_shape=[shape] * 3,
        in_specs=anywhere(groups),
        out_specs=anywhere(3),
        scratch_shapes=[pltpu.VMEM(shape.shape, BF16)] * 3 + [pltpu.SemaphoreType.DMA((3 * groups,))],
        cost_estimate=pl.CostEstimate(flops=0, bytes_accessed=10 * rows * groups * width, transcendentals=0),
        compiler_params=pltpu.CompilerParams(vmem_limit_bytes=VMEM_SMALL),
        name="unpack_early",
    )(*parts)


def unpack_late(parts, dq, dk, dv):
    groups = len(parts)
    rows, width = parts[0].shape
    half = width // 2

    def body(*refs):
        dq, dk, dv, held, sems = refs[groups + 3 :]
        here, low = lax.axis_index("head"), lax.axis_index("ctx") < 2
        loads = run_copies([(refs[m], held.at[m]) for m in range(groups)], sems)

        def moves(far, near):
            todo = []
            for m in range(groups):
                base = pl.multiple_of((here ^ m) * width, LANES)
                todo.append((held.at[m, :, pl.ds(0, half)], far.at[:, pl.ds(base + near, half)]))
                todo.append((held.at[m, :, pl.ds(half, half)], dv.at[:, pl.ds(base + half, half)]))
            return todo

        wait_all(loads)

        @pl.when(low)
        def _():
            wait_all(run_copies(moves(dk, half), sems))

        @pl.when(jnp.logical_not(low))
        def _():
            wait_all(run_copies(moves(dq, 0), sems))

    shape = jax.ShapeDtypeStruct(dq.shape, BF16)
    return pl.pallas_call(
        body,
        out_shape=[shape] * 3,
        in_specs=anywhere(groups + 3),
        out_specs=anywhere(3),
        scratch_shapes=[pltpu.VMEM((groups, rows, width), BF16), pltpu.SemaphoreType.DMA((2 * groups,))],
        input_output_aliases={groups: 0, groups + 1: 1, groups + 2: 2},
        compiler_params=pltpu.CompilerParams(vmem_limit_bytes=VMEM_SMALL),
        cost_estimate=pl.CostEstimate(flops=0, bytes_accessed=8 * rows * groups * width, transcendentals=0),
        name="unpack_late",
    )(*parts, dq, dk, dv)


def after(array, other):
    return lax.optimization_barrier((array, other))[0]


def local_split(queries, keys_in, values_in, attn_out, out_grad, log_norm, span_id):
    groups = lax.axis_size("head")
    width = queries.shape[1] // groups

    def swapped(parts):
        return [parts[0]] + [
            lax.ppermute(parts[m], "head", [(i, i ^ m) for i in range(groups)]) for m in range(1, groups)
        ]

    x1, x2, x3 = pack(queries, keys_in, values_in, attn_out, out_grad, span_id.reshape(1, -1), groups, width)
    x1 = swapped(x1)
    y1 = join_first(x1, log_norm.T)
    r1 = lax.ppermute(y1, "ctx", INWARD)
    s1 = lax.ppermute(y1, "ctx", SWAP)
    x2 = swapped(x2)
    x3 = swapped(x3)
    y2 = join(x2)
    y2, r1, s1, x3 = lax.optimization_barrier((y2, r1, s1, x3))
    r2 = lax.ppermute(y2, "ctx", INWARD)
    s2 = lax.ppermute(r1, "ctx", SWAP)
    w, key_edge, query_edge = join_last(x3, y1, y2)
    key_edge = lax.ppermute(key_edge, "ctx", DOWN)
    query_edge = lax.ppermute(query_edge, "ctx", UP)
    w, key_edge, query_edge = lax.optimization_barrier((w, key_edge, query_edge))
    swap1, out1, swap2, l1, l2, l3 = far_pairs(y1, y2, w, r1, r2, s1, s2)
    dw, dy1, dy2, dkedge, dqedge = near_pairs(y1, y2, w, after(key_edge, l3), query_edge)
    swap1 = lax.ppermute(swap1, "ctx", SWAP)
    out1 = lax.ppermute(out1, "ctx", OUTWARD)
    dkedge = lax.ppermute(dkedge, "ctx", UP)
    dqedge = lax.ppermute(dqedge, "ctx", DOWN)
    swap1, swap2, out1, dkedge, dqedge = lax.optimization_barrier((swap1, swap2, out1, dkedge, dqedge))
    swap2 = lax.ppermute(swap2, "ctx", SWAP)
    out2 = lax.ppermute((swap1.astype(F32) + l3.astype(F32)).astype(BF16), "ctx", OUTWARD)
    *early, kept = finish_first(dw, l1, dy2, l2, out1, dkedge, dqedge, groups)
    early = swapped(early)
    late = swapped(finish_second(dy1, swap2, out2, kept, dkedge, dqedge, groups))
    return tuple(unpack_late(late, *unpack_early(early)))


def splits(tokens, blocks, head_width, heads):
    if blocks != 4 or heads % 2 or head_width != LANES or 6 * heads + 1 > LANES:
        return False
    block = tokens // blocks
    span = -(-tokens // SPANS)
    for offset in range(SPANS * span - tokens + 1):
        for end in range(block, tokens, block):
            start = (end - 1 + offset) // span * span - offset
            if min(end - start, start + span - end) > EDGE or max(end - start, span) > block:
                return False
    return block % EDGE == 0


def local(queries, keys_in, values_in, attn_out, out_grad, log_norm, span_id):
    blocks, groups = lax.axis_size("ctx"), lax.axis_size("head")
    heads = log_norm.shape[1]
    tokens = queries.shape[0] * blocks * groups
    plan = local_plain
    if groups & (groups - 1) == 0 and splits(tokens, blocks, queries.shape[1] // (heads * groups), heads):
        plan = local_split
    return plan(queries, keys_in, values_in, attn_out, out_grad, log_norm, span_id)


def solution(mesh):
    placed = (
        P(("clip", "ctx", "head"), None),
        P(("clip", "ctx", "head"), None),
        P(("clip", "ctx", "head"), None),
        P(("clip", "ctx", "head"), None),
        P(("clip", "ctx", "head"), None),
        P(("clip", "ctx"), "head"),
        P(("clip", "ctx", "head")),
    )
    return jax.shard_map(
        local,
        mesh=mesh,
        in_specs=placed,
        out_specs=(
            P(("clip", "ctx", "head"), None),
            P(("clip", "ctx", "head"), None),
            P(("clip", "ctx", "head"), None),
        ),
        check_vma=False,
    )
```

```python
import math

import jax
import jax.numpy as jnp
from jax import lax
from jax.experimental import pallas as pl
from jax.experimental.pallas import tpu as pltpu
from jax.sharding import PartitionSpec as P

SPANS = 12
EDGE = 16
VMEM_LIMIT = 32 * 2**20
VMEM_SMALL = 16 * 2**20
VMEM_WHOLE = 60 * 2**20
LANES = 128
BF16 = jnp.bfloat16
F32 = jnp.float32

PAIRS = ((0, 1), (1, 0), (2, 3), (3, 2))
SWAP = ((1, 2), (2, 1))
DOWN = ((1, 0), (2, 1), (3, 2))
UP = ((0, 1), (1, 2), (2, 3))


def tile_terms(query_blk, grad_blk, norm_blk, delta_blk, query_ids, key_blk, value_blk, key_ids):
    row_count = query_blk.shape[0]
    key_count = key_blk.shape[0]
    head_count = norm_blk.shape[1]
    head_width = query_blk.shape[1] // head_count
    scale = 1.0 / math.sqrt(head_width)
    query3 = query_blk.reshape(row_count, head_count, head_width)
    grad3 = grad_blk.reshape(row_count, head_count, head_width)
    key3 = key_blk.reshape(key_count, head_count, head_width)
    value3 = value_blk.reshape(key_count, head_count, head_width)
    scores = jnp.einsum("rhd,khd->hrk", query3, key3, preferred_element_type=jnp.float32)
    visible = key_ids[None, :] <= query_ids[:, None]
    weight = jnp.where(visible[None], jnp.exp(scores * scale - norm_blk.T[:, :, None]), 0.0)
    weight_low = weight.astype(jnp.bfloat16)
    dweight = jnp.einsum("rhd,khd->hrk", grad3, value3, preferred_element_type=jnp.float32)
    dscore = (weight * (dweight - delta_blk.T[:, :, None]) * scale).astype(jnp.bfloat16)
    query_term = jnp.einsum("hrk,khd->rhd", dscore, key3, preferred_element_type=jnp.float32)
    key_term = jnp.einsum("hrk,rhd->khd", dscore, query3, preferred_element_type=jnp.float32)
    value_term = jnp.einsum("hrk,rhd->khd", weight_low, grad3, preferred_element_type=jnp.float32)
    return (
        query_term.reshape(row_count, -1),
        key_term.reshape(key_count, -1),
        value_term.reshape(key_count, -1),
    )


def rounded(term):
    return lax.optimization_barrier(term.astype(jnp.bfloat16)).astype(jnp.float32)


def local_plain(queries, keys_in, values_in, attn_out, out_grad, log_norm, span_id):
    local_q, local_k, local_v, local_out, local_grad = (
        lax.all_to_all(queries, "head", split_axis=1, concat_axis=0, tiled=True),
        lax.all_to_all(keys_in, "head", split_axis=1, concat_axis=0, tiled=True),
        lax.all_to_all(values_in, "head", split_axis=1, concat_axis=0, tiled=True),
        lax.all_to_all(attn_out, "head", split_axis=1, concat_axis=0, tiled=True),
        lax.all_to_all(out_grad, "head", split_axis=1, concat_axis=0, tiled=True),
    )
    all_ids = lax.all_gather(span_id, ("ctx", "head"), axis=0, tiled=True)
    seg_rows = local_q.shape[0]
    block_count = lax.axis_size("ctx")
    head_count = log_norm.shape[1]
    head_width = local_q.shape[1] // head_count
    my_block = lax.axis_index("ctx")
    own_ids = lax.dynamic_slice_in_dim(all_ids, my_block * seg_rows, seg_rows)
    id_blocks = all_ids.reshape(block_count, seg_rows)
    deltas = jnp.sum(
        (local_grad.astype(jnp.float32) * local_out.astype(jnp.float32)).reshape(
            seg_rows, head_count, head_width
        ),
        axis=2,
    )
    far_queries, far_grads = (
        lax.all_gather(local_q, "ctx", axis=0, tiled=True),
        lax.all_gather(local_grad, "ctx", axis=0, tiled=True),
    )
    far_norms, far_deltas = (
        lax.all_gather(log_norm, "ctx", axis=0, tiled=True),
        lax.all_gather(deltas, "ctx", axis=0, tiled=True),
    )

    def query_step(totals, piece):
        query_blk, grad_blk, norm_blk, delta_blk, query_ids = piece
        query_term, key_term, value_term = tile_terms(
            query_blk, grad_blk, norm_blk, delta_blk, query_ids, local_k, local_v, own_ids
        )
        return ((totals[0] + rounded(key_term), totals[1] + rounded(value_term)), query_term)

    zero_block = jnp.zeros(local_k.shape, jnp.float32)
    (dk_total, dv_total), query_terms = lax.scan(
        query_step,
        (zero_block, zero_block),
        (
            far_queries.reshape(block_count, seg_rows, -1),
            far_grads.reshape(block_count, seg_rows, -1),
            far_norms.reshape(block_count, seg_rows, -1),
            far_deltas.reshape(block_count, seg_rows, -1),
            id_blocks,
        ),
    )
    query_sum = lax.psum_scatter(
        query_terms.reshape(block_count * seg_rows, -1).astype(jnp.bfloat16),
        "ctx",
        scatter_dimension=0,
        tiled=True,
    )
    dk_local = dk_total.astype(jnp.bfloat16)
    dv_local = dv_total.astype(jnp.bfloat16)
    query_grad, key_grad, value_grad = (
        lax.all_to_all(query_sum, "head", split_axis=0, concat_axis=1, tiled=True),
        lax.all_to_all(dk_local, "head", split_axis=0, concat_axis=1, tiled=True),
        lax.all_to_all(dv_local, "head", split_axis=0, concat_axis=1, tiled=True),
    )
    return (query_grad, key_grad, value_grad)


def nt(a, b):
    return lax.dot_general(a, b, (((1,), (1,)), ((), ())), preferred_element_type=F32)


def tn(a, b):
    return lax.dot_general(a, b, (((0,), (0,)), ((), ())), preferred_element_type=F32)


def pieces(value):
    high = value.astype(BF16)
    rest = value - high.astype(F32)
    middle = rest.astype(BF16)
    low = (rest - middle.astype(F32)).astype(BF16)
    return high, middle, low


def run_copies(pairs, sems, first=0):
    made = [pltpu.make_async_copy(src, dst, sems.at[first + i]) for i, (src, dst) in enumerate(pairs)]
    for copy in made:
        copy.start()
    return made


def wait_all(made):
    for copy in made:
        copy.wait()


def anywhere(count):
    return [pl.BlockSpec(memory_space=pl.ANY)] * count


def pack(queries, keys_in, values_in, attn_out, out_grad, span_row, groups, width):
    rows = queries.shape[0]
    heads = width // LANES
    half = width // 2

    def body(q, k, v, o, g, ids, *refs):
        x1, x2, x3 = refs[:groups], refs[groups : 2 * groups], refs[2 * groups : 3 * groups]
        q_v, k_v, v_v, o_v, g_v, meta, sems = refs[3 * groups :]
        here = lax.axis_index("head")
        low = lax.axis_index("ctx") < 2
        loads = run_copies([(k, k_v), (v, v_v), (q, q_v), (g, g_v), (o, o_v)], sems)

        def moves(first, second, third, fourth, near, far):
            todo = []
            for m in range(groups):
                base = pl.multiple_of((here ^ m) * width, LANES)
                todo.append((first.at[:, pl.ds(base + near, half)], x1[m].at[:, pl.ds(0, half)]))
                todo.append((second.at[:, pl.ds(base + near, half)], x1[m].at[:, pl.ds(half, half)]))
            for m in range(groups):
                base = pl.multiple_of((here ^ m) * width, LANES)
                todo.append((first.at[:, pl.ds(base + far, half)], x2[m].at[:, pl.ds(0, half)]))
                todo.append((second.at[:, pl.ds(base + far, half)], x2[m].at[:, pl.ds(half, half)]))
                todo.append((third.at[:, pl.ds(base, width)], x3[m].at[:, pl.ds(0, width)]))
                todo.append((fourth.at[:, pl.ds(base, width)], x3[m].at[:, pl.ds(width, width)]))
            return [pltpu.make_async_copy(src, dst, sems.at[5 + i]) for i, (src, dst) in enumerate(todo)]

        low_moves = (k_v, v_v, q_v, g_v, half, 0)
        high_moves = (q_v, g_v, k_v, v_v, 0, half)
        wait_all(loads[:4])

        @pl.when(low)
        def _():
            for copy in moves(*low_moves):
                copy.start()

        @pl.when(jnp.logical_not(low))
        def _():
            for copy in moves(*high_moves):
                copy.start()

        wait_all(loads[4:])
        lane = lax.broadcasted_iota(jnp.int32, (rows, LANES), 1)
        slot = jnp.where(lane < 3 * heads, lane % heads, -1)
        at_row = lax.broadcasted_iota(jnp.int32, (rows, rows), 0)
        at_col = lax.broadcasted_iota(jnp.int32, (rows, rows), 1)
        own = jnp.sum(jnp.where(at_row == at_col, ids[...].astype(F32), 0.0), axis=1, keepdims=True)
        for h in range(groups):
            total = jnp.zeros((rows, LANES), F32)
            for c in range(heads):
                cols = pl.ds(h * width + c * LANES, LANES)
                delta = jnp.sum(o_v[:, cols].astype(F32) * g_v[:, cols].astype(F32), axis=1, keepdims=True)
                total = jnp.where(slot == c, delta, total)
            high, middle, lowest = pieces(total)
            kept = jnp.where(lane < heads, high, jnp.where(lane < 2 * heads, middle, lowest))
            meta[h] = jnp.where(lane < 3 * heads, kept, jnp.where(lane == 3 * heads, own.astype(BF16), 0.0).astype(BF16))
        last = run_copies(
            [(meta.at[here ^ m], x1[m].at[:, pl.ds(width, LANES)]) for m in range(groups)], sems, 5 + 6 * groups
        )

        @pl.when(low)
        def _():
            wait_all(moves(*low_moves))

        @pl.when(jnp.logical_not(low))
        def _():
            wait_all(moves(*high_moves))

        wait_all(last)

    whole = pltpu.VMEM((rows, groups * width), BF16)
    made = pl.pallas_call(
        body,
        out_shape=[
            jax.ShapeDtypeStruct((rows, size), BF16)
            for size in (width + LANES, width, 2 * width)
            for _ in range(groups)
        ],
        in_specs=anywhere(5) + [pl.BlockSpec(memory_space=pltpu.VMEM)],
        out_specs=anywhere(3 * groups),
        scratch_shapes=[whole] * 5
        + [pltpu.VMEM((groups, rows, LANES), BF16), pltpu.SemaphoreType.DMA((5 + 7 * groups,))],
        cost_estimate=pl.CostEstimate(flops=0, bytes_accessed=10 * rows * groups * width * 2, transcendentals=0),
        compiler_params=pltpu.CompilerParams(vmem_limit_bytes=VMEM_WHOLE),
        name="pack",
    )(queries, keys_in, values_in, attn_out, out_grad, span_row)
    return made[:groups], made[groups : 2 * groups], made[2 * groups :]


def join_first(parts, norm_rows):
    groups = len(parts)
    rows, width = parts[0].shape
    heads = norm_rows.shape[0]

    def body(*refs):
        norm, y, sems = refs[groups:]
        here = lax.axis_index("head")
        made = run_copies([(refs[m], y.at[here ^ m]) for m in range(groups)], sems)
        at_row = lax.broadcasted_iota(jnp.int32, (heads, LANES), 0)
        at_lane = lax.broadcasted_iota(jnp.int32, (heads, LANES), 1)
        total = jnp.zeros((groups * rows, LANES), F32)
        for i, piece in enumerate(pieces(norm[...])):
            place = jnp.where(at_lane == at_row + (3 * heads + 1 + i * heads), 1.0, 0.0).astype(BF16)
            total += tn(piece, place)
        wait_all(made)
        tail = pl.ds(width - LANES, LANES)
        for h in range(groups):
            y[h, :, tail] = (y[h, :, tail].astype(F32) + total[h * rows : (h + 1) * rows]).astype(BF16)

    return pl.pallas_call(
        body,
        out_shape=jax.ShapeDtypeStruct((groups, rows, width), BF16),
        in_specs=anywhere(groups) + [pl.BlockSpec(memory_space=pltpu.VMEM)],
        out_specs=pl.BlockSpec(memory_space=pltpu.VMEM),
        scratch_shapes=[pltpu.SemaphoreType.DMA((groups,))],
        cost_estimate=pl.CostEstimate(flops=0, bytes_accessed=4 * groups * rows * width, transcendentals=0),
        compiler_params=pltpu.CompilerParams(vmem_limit_bytes=VMEM_SMALL),
        name="join_first",
    )(*parts, norm_rows).reshape(groups * rows, width)


def join(parts):
    groups = len(parts)
    rows, width = parts[0].shape

    def body(*refs):
        y, sems = refs[groups:]
        here = lax.axis_index("head")
        wait_all(run_copies([(refs[m], y.at[here ^ m]) for m in range(groups)], sems))

    return pl.pallas_call(
        body,
        out_shape=jax.ShapeDtypeStruct((groups, rows, width), BF16),
        in_specs=anywhere(groups),
        out_specs=pl.BlockSpec(memory_space=pltpu.VMEM),
        scratch_shapes=[pltpu.SemaphoreType.DMA((groups,))],
        cost_estimate=pl.CostEstimate(flops=0, bytes_accessed=4 * groups * rows * width, transcendentals=0),
        compiler_params=pltpu.CompilerParams(vmem_limit_bytes=VMEM_SMALL),
        name="join",
    )(*parts).reshape(groups * rows, width)


def token_rows(meta, heads):
    at_row = lax.broadcasted_iota(jnp.int32, (32, LANES), 0)
    at_lane = lax.broadcasted_iota(jnp.int32, (32, LANES), 1)
    norm_lane = at_lane - (3 * heads + 1)
    is_norm = (norm_lane >= 0) & (norm_lane < 3 * heads) & (norm_lane % heads == at_row) & (at_row < heads)
    is_delta = (at_lane < 3 * heads) & (at_lane % heads == at_row - heads) & (at_row >= heads)
    is_id = (at_lane == 3 * heads) & (at_row == 2 * heads)
    chosen = jnp.where(is_norm | is_delta | is_id, 1.0, 0.0).astype(BF16)
    return nt(chosen, meta)


def pair_terms(query, grad, key, value, norm, delta, visible=None):
    scale = 1.0 / math.sqrt(query.shape[1])
    weight = jnp.exp(nt(key, query) * scale - norm)
    if visible is not None:
        weight = jnp.where(visible, weight, 0.0)
    dscore = (weight * (nt(value, grad) - delta) * scale).astype(BF16)
    value_term = jnp.dot(weight.astype(BF16), grad, preferred_element_type=F32)
    key_term = jnp.dot(dscore, query, preferred_element_type=F32)
    query_term = tn(dscore, key)
    return query_term, key_term, value_term


def join_last(parts, y1, y2):
    groups = len(parts)
    share = parts[0].shape[0]
    rows, width = y2.shape
    half = width // 2

    def body(*refs):
        y1, y2, w, kedge, qedge, sems = refs[groups:]
        here, low = lax.axis_index("head"), lax.axis_index("ctx") < 2
        top, bottom, tail = pl.ds(0, EDGE), pl.ds(rows - EDGE, EDGE), pl.ds(width, LANES)
        whole, end = pl.ds(0, 2 * width), pl.ds(2 * width, LANES)
        made = run_copies([(y1.at[top, tail], kedge.at[:, end]), (y1.at[bottom, tail], qedge.at[:, end])], sems)
        loads = run_copies([(refs[m], w.at[here ^ m]) for m in range(groups)], sems, 2)

        def joined(first, second, at, edge):
            todo = []
            for i in range(2):
                for j, part in enumerate((first, second)):
                    todo.append((part.at[at, pl.ds(i * half, half)], edge.at[:, pl.ds(i * width + j * half, half)]))
            return todo

        @pl.when(low)
        def _():
            wait_all(run_copies(joined(y2, y1, top, kedge), sems, 2 + groups))

        @pl.when(jnp.logical_not(low))
        def _():
            wait_all(run_copies(joined(y1, y2, bottom, qedge), sems, 2 + groups))

        wait_all(loads)

        @pl.when(low)
        def _():
            qedge[:, whole] = w[groups - 1, share - EDGE :, :]

        @pl.when(jnp.logical_not(low))
        def _():
            kedge[:, whole] = w[0, :EDGE, :]

        wait_all(made)

    edge = jax.ShapeDtypeStruct((EDGE, 2 * width + LANES), BF16)
    w, key_edge, query_edge = pl.pallas_call(
        body,
        out_shape=[jax.ShapeDtypeStruct((groups, share, 2 * width), BF16), edge, edge],
        in_specs=anywhere(groups + 2),
        out_specs=[pl.BlockSpec(memory_space=pltpu.VMEM)] * 3,
        scratch_shapes=[pltpu.SemaphoreType.DMA((6 + groups,))],
        compiler_params=pltpu.CompilerParams(vmem_limit_bytes=VMEM_SMALL),
        cost_estimate=pl.CostEstimate(flops=0, bytes_accessed=8 * rows * width, transcendentals=0),
        name="join_last",
    )(*parts, y1, y2)
    return w.reshape(rows, 2 * width), key_edge, query_edge


def far_pairs(y1, y2, w, r1, r2, s1, s2):
    rows, width = r2.shape
    half = width // 2
    count = half // LANES
    heads = 2 * count

    def body(y1, y2, w, r1, r2, s1, s2, swap1, out1, swap2, l1, l2, l3, buf, grads, meta, info, sems):
        z = lax.axis_index("ctx")
        one = z == 1

        def pick(a, b):
            return jnp.where(one, a, b)

        @pl.when((z == 1) | (z == 2))
        def _():
            near = pl.multiple_of(pick(0, half), LANES)
            other = pl.multiple_of(pick(half, 0), LANES)
            main = pl.ds(0, width)
            tail = pl.ds(width, LANES)
            left, right = pl.ds(0, half), pl.ds(half, half)
            made = run_copies(
                [
                    (y1.at[:, tail], meta.at[pick(2, 0)]),
                    (s1.at[:, tail], meta.at[pick(0, 3)]),
                    (s2.at[:, tail], meta.at[pick(1, 4)]),
                    (r1.at[:, tail], meta.at[pick(3, 1)]),
                    (s1.at[:, main], buf.at[pick(0, 3)]),
                    (s2.at[:, main], buf.at[pick(1, 2)]),
                    (r2, buf.at[pick(2, 1)]),
                    (y2, buf.at[pick(3, 0)]),
                    (w.at[:, pl.ds(near, half)], buf.at[4, :, left]),
                    (w.at[:, pl.ds(width + near, half)], buf.at[4, :, right]),
                    (w.at[:, pl.ds(other, half)], buf.at[5, :, left]),
                    (w.at[:, pl.ds(width + other, half)], buf.at[5, :, right]),
                    (r1.at[:, main], buf.at[6]),
                ],
                sems,
            )
            wait_all(made)
            for i in range(3):
                info[i] = token_rows(meta[i], heads)
            first_active = pick(0, count)
            first_other = pick(count, 0)
            zero = jnp.zeros((rows, LANES), BF16)

            def single(q_slot, k_slot, c, head):
                a = pl.ds(pl.multiple_of(c * LANES, LANES), LANES)
                b = pl.ds(pl.multiple_of(half + c * LANES, LANES), LANES)
                own = pick(2, 1)
                return pair_terms(
                    buf[q_slot, :, a],
                    buf[q_slot, :, b],
                    buf[k_slot, :, a],
                    buf[k_slot, :, b],
                    info[own, pl.ds(head, 1), :],
                    info[own, pl.ds(heads + head, 1), :],
                )

            def step(c, carry):
                a = pl.ds(pl.multiple_of(c * LANES, LANES), LANES)
                b = pl.ds(pl.multiple_of(half + c * LANES, LANES), LANES)
                head = first_active + c
                extra_q, extra_k, extra_v = single(pick(4, 1), pick(2, 4), c, head)
                key = buf[2:4, :, a].reshape(2 * rows, LANES)
                value = buf[2:4, :, b].reshape(2 * rows, LANES)
                key_sum, value_sum = None, None
                for i in range(2):
                    query_term, key_term, value_term = pair_terms(
                        buf[i, :, a],
                        buf[i, :, b],
                        key,
                        value,
                        info[i, pl.ds(head, 1), :],
                        info[i, pl.ds(heads + head, 1), :],
                    )
                    if i == 1:
                        query_term += jnp.where(one, 0.0, extra_q)
                    grads[i, :, a] = query_term.astype(BF16)
                    grads[i, :, b] = zero
                    key_sum = key_term if i == 0 else key_sum + key_term
                    value_sum = value_term if i == 0 else value_sum + value_term
                grads[2, :, a] = (key_sum[:rows] + jnp.where(one, extra_k, 0.0)).astype(BF16)
                grads[2, :, b] = (value_sum[:rows] + jnp.where(one, extra_v, 0.0)).astype(BF16)
                grads[3, :, a] = key_sum[rows:].astype(BF16)
                grads[3, :, b] = value_sum[rows:].astype(BF16)
                grads[4, :, a] = jnp.where(one, extra_q, extra_k).astype(BF16)
                grads[4, :, b] = jnp.where(one, 0.0, extra_v).astype(BF16)
                extra_q, extra_k, extra_v = single(pick(5, 6), pick(6, 5), c, first_other + c)
                grads[5, :, a] = jnp.where(one, extra_q, extra_k).astype(BF16)
                grads[5, :, b] = jnp.where(one, 0.0, extra_v).astype(BF16)
                grads[6, :, a] = jnp.where(one, extra_k, extra_q).astype(BF16)
                grads[6, :, b] = jnp.where(one, extra_v, 0.0).astype(BF16)
                return carry

            lax.fori_loop(0, count, step, 0, unroll=True)
            made = run_copies(
                [
                    (grads.at[pick(1, 2)], swap1),
                    (grads.at[pick(2, 1)], out1),
                    (grads.at[pick(0, 3)], swap2),
                    (grads.at[pick(3, 0)], l2),
                    (grads.at[6], l3),
                    (grads.at[4, :, left], l1.at[:, pl.ds(near, half)]),
                    (grads.at[4, :, right], l1.at[:, pl.ds(width + near, half)]),
                    (grads.at[5, :, left], l1.at[:, pl.ds(other, half)]),
                    (grads.at[5, :, right], l1.at[:, pl.ds(width + other, half)]),
                ],
                sems,
            )
            wait_all(made)

    single_shape = jax.ShapeDtypeStruct((rows, width), BF16)
    return pl.pallas_call(
        body,
        out_shape=[
            single_shape,
            single_shape,
            single_shape,
            jax.ShapeDtypeStruct((rows, 2 * width), BF16),
            single_shape,
            single_shape,
        ],
        in_specs=anywhere(7),
        out_specs=anywhere(6),
        scratch_shapes=[
            pltpu.VMEM((7, rows, width), BF16),
            pltpu.VMEM((7, rows, width), BF16),
            pltpu.VMEM((5, rows, LANES), BF16),
            pltpu.VMEM((3, 32, rows), F32),
            pltpu.SemaphoreType.DMA((13,)),
        ],
        compiler_params=pltpu.CompilerParams(vmem_limit_bytes=VMEM_LIMIT),
        cost_estimate=pl.CostEstimate(
            flops=30 * 10 * rows * rows * LANES, bytes_accessed=30 * rows * width, transcendentals=30 * rows * rows
        ),
        name="far_pairs",
    )(y1, y2, w, r1, r2, s1, s2)


def near_pairs(y1, y2, w, key_edge, query_edge):
    rows, width = y2.shape
    half = width // 2
    count = half // LANES
    heads = 2 * count
    total = rows + EDGE

    def body(y1, y2, w, kedge, qedge, dw, dy1, dy2, dkedge, dqedge, qbuf, kbuf, dq, dk, kmeta, qmeta, info, sems):
        low = lax.axis_index("ctx") < 2
        left, right = pl.ds(0, half), pl.ds(half, half)
        own, past = pl.ds(0, rows), pl.ds(rows, EDGE)
        main = pl.ds(0, width)

        def halves(array, there, back=False, parts=2):
            todo = []
            for i in range(2):
                for j in range(parts):
                    wide = array.at[:, pl.ds(j * width + i * half, half)]
                    narrow = there(i, right if j else left)
                    todo.append((narrow, wide) if back else (wide, narrow))
            return todo

        shared = run_copies(
            [
                (y1.at[:, pl.ds(width, LANES)], kmeta.at[own]),
                (y1.at[:, pl.ds(width, LANES)], qmeta.at[own]),
                (kedge.at[:, pl.ds(2 * width, LANES)], kmeta.at[past]),
                (qedge.at[:, pl.ds(2 * width, LANES)], qmeta.at[past]),
            ]
            + halves(kedge, lambda i, cols: kbuf.at[i, past, cols])
            + halves(qedge, lambda i, cols: qbuf.at[i, past, cols]),
            sems,
        )

        @pl.when(low)
        def _():
            todo = halves(w, lambda i, cols: qbuf.at[i, own, cols])
            todo += [(y2, kbuf.at[0, own]), (y1.at[:, main], kbuf.at[1, own])]
            wait_all(run_copies(todo, sems, 12))

        @pl.when(jnp.logical_not(low))
        def _():
            todo = halves(w, lambda i, cols: kbuf.at[i, own, cols])
            todo += [(y1.at[:, main], qbuf.at[0, own]), (y2, qbuf.at[1, own])]
            wait_all(run_copies(todo, sems, 12))

        wait_all(shared)
        info[...] = token_rows(qmeta[...], heads)
        id_lane = lax.broadcasted_iota(jnp.int32, (total, LANES), 1) == 3 * heads
        key_ids = jnp.sum(jnp.where(id_lane, kmeta[...].astype(F32), 0.0), axis=1, keepdims=True)
        at_key = lax.broadcasted_iota(jnp.int32, (total, total), 0)
        at_query = lax.broadcasted_iota(jnp.int32, (total, total), 1)
        last_key = jnp.where(lax.axis_index("ctx") < 3, total, rows)
        last_query = jnp.where(lax.axis_index("ctx") > 0, total, rows)
        visible = (key_ids <= info[2 * heads : 2 * heads + 1, :]) & ((at_key < rows) | (at_query < rows - EDGE))
        visible = visible & (at_key < last_key) & (at_query < last_query)
        for i in range(2):

            def step(c, carry, i=i):
                a = pl.ds(pl.multiple_of(c * LANES, LANES), LANES)
                b = pl.ds(pl.multiple_of(half + c * LANES, LANES), LANES)
                head = i * count + c
                query_term, key_term, value_term = pair_terms(
                    qbuf[i, :, a],
                    qbuf[i, :, b],
                    kbuf[i, :, a],
                    kbuf[i, :, b],
                    info[pl.ds(head, 1), :],
                    info[pl.ds(heads + head, 1), :],
                    visible,
                )
                dq[i, :, a] = query_term.astype(BF16)
                dk[i, :, a] = key_term.astype(BF16)
                dk[i, :, b] = value_term.astype(BF16)
                return carry

            lax.fori_loop(0, count, step, 0, unroll=True)

        made = run_copies(
            halves(dkedge, lambda i, cols: dk.at[i, past, cols], back=True)
            + halves(dqedge, lambda i, cols: dq.at[i, past, cols], back=True, parts=1),
            sems,
        )

        @pl.when(low)
        def _():
            todo = [(dq.at[0, own], dw.at[:, left]), (dq.at[1, own], dw.at[:, right])]
            todo += [(dk.at[0, own], dy2), (dk.at[1, own], dy1)]
            wait_all(run_copies(todo, sems, 12))

        @pl.when(jnp.logical_not(low))
        def _():
            todo = halves(dw, lambda i, cols: dk.at[i, own, cols], back=True)
            todo += [(dq.at[0, own], dy1.at[:, left]), (dq.at[1, own], dy2.at[:, left])]
            wait_all(run_copies(todo, sems, 12))

        wait_all(made)

    return pl.pallas_call(
        body,
        out_shape=[
            jax.ShapeDtypeStruct((rows, 2 * width), BF16),
            jax.ShapeDtypeStruct((rows, width), BF16),
            jax.ShapeDtypeStruct((rows, width), BF16),
            jax.ShapeDtypeStruct((EDGE, 2 * width), BF16),
            jax.ShapeDtypeStruct((EDGE, width), BF16),
        ],
        in_specs=anywhere(5),
        out_specs=anywhere(5),
        scratch_shapes=[
            pltpu.VMEM((2, total, width), BF16),
            pltpu.VMEM((2, total, width), BF16),
            pltpu.VMEM((2, total, half), BF16),
            pltpu.VMEM((2, total, width), BF16),
            pltpu.VMEM((total, LANES), BF16),
            pltpu.VMEM((total, LANES), BF16),
            pltpu.VMEM((32, total), F32),
            pltpu.SemaphoreType.DMA((18,)),
        ],
        compiler_params=pltpu.CompilerParams(vmem_limit_bytes=VMEM_LIMIT),
        cost_estimate=pl.CostEstimate(
            flops=10 * 10 * rows * rows * LANES, bytes_accessed=16 * rows * width, transcendentals=10 * rows * rows
        ),
        name="near_pairs",
    )(y1, y2, w, key_edge, query_edge)


def finish_first(dw, l1, dy2, l2, out1, dkedge, dqedge, groups):
    rows, width = dy2.shape
    half = width // 2
    share = rows // groups

    def body(dw, l1, dy2, l2, out1, dk, dq, *refs):
        outs, v, e, sems = refs[:groups], *refs[groups:]
        here = lax.axis_index("head")
        z = lax.axis_index("ctx")
        low, middle = z < 2, (z == 1) | (z == 2)
        after_first, before_last = z > 0, z < 3

        def own(cols):
            return dw[:, cols].astype(F32) + jnp.where(middle, l1[:, cols].astype(F32), 0.0)

        def second(cols):
            return dy2[:, cols].astype(F32) + jnp.where(middle, l2[:, cols], out1[:, cols]).astype(F32)

        def put(dst, cols, total, first, last=None):
            end = total[rows - EDGE :] if last is None else total[rows - EDGE :] + last
            total = jnp.concatenate([total[:EDGE] + first, total[EDGE : rows - EDGE], end], axis=0)
            for h in range(groups):
                dst[h, :, cols] = total[h * share : (h + 1) * share].astype(BF16)

        def key_edge(cols):
            return jnp.where(after_first, dk[:, cols].astype(F32), 0.0)

        def query_edge(cols):
            return jnp.where(before_last, dq[:, cols].astype(F32), 0.0)

        a, b = pl.ds(0, half), pl.ds(half, half)
        c, d = pl.ds(width, half), pl.ds(width + half, half)
        for cols in (a, b):
            put(e, cols, own(cols), jnp.where(low, 0.0, key_edge(cols)), jnp.where(low, query_edge(cols), 0.0))
        put(e, c, second(a), jnp.where(low, key_edge(a), 0.0), jnp.where(low, 0.0, query_edge(b)))
        put(e, d, jnp.where(low, second(b), own(c)), key_edge(c))
        made = run_copies([(e.at[here ^ m], outs[m]) for m in range(groups)], sems)
        left_over = own(d)
        left_over = jnp.concatenate([left_over[:EDGE] + key_edge(d), left_over[EDGE:]], axis=0)
        v[...] = left_over.astype(BF16)
        wait_all(made)

    return pl.pallas_call(
        body,
        out_shape=[jax.ShapeDtypeStruct((share, 2 * width), BF16)] * groups + [jax.ShapeDtypeStruct((rows, half), BF16)],
        in_specs=[pl.BlockSpec(memory_space=pltpu.VMEM)] * 7,
        out_specs=anywhere(groups) + [pl.BlockSpec(memory_space=pltpu.VMEM)],
        scratch_shapes=[pltpu.VMEM((groups, share, 2 * width), BF16), pltpu.SemaphoreType.DMA((groups,))],
        compiler_params=pltpu.CompilerParams(vmem_limit_bytes=VMEM_SMALL),
        cost_estimate=pl.CostEstimate(flops=0, bytes_accessed=16 * rows * width, transcendentals=0),
        name="finish_first",
    )(dw, l1, dy2, l2, out1, dkedge, dqedge)


def finish_second(dy1, swap2, out2, v, dkedge, dqedge, groups):
    rows, width = dy1.shape
    half = width // 2
    share = rows // groups

    def body(dy1, swap2, out2, v, dk, dq, *refs):
        outs, e, sems = refs[:groups], *refs[groups:]
        here, z = lax.axis_index("head"), lax.axis_index("ctx")
        low, middle = z < 2, (z == 1) | (z == 2)

        def put(cols, whole):
            for h in range(groups):
                e[h, :, cols] = whole[h * share : (h + 1) * share].astype(BF16)

        a, b = pl.ds(0, half), pl.ds(half, half)
        end = pl.ds(width + half, half)

        def total(cols):
            return dy1[:, cols].astype(F32) + jnp.where(middle, swap2[:, cols], out2[:, cols]).astype(F32)

        left = total(a)
        first = left[:EDGE] + jnp.where(z == 1, dk[:, b].astype(F32), 0.0)
        last = left[rows - EDGE :] + jnp.where(z == 2, dq[:, a].astype(F32), 0.0)
        put(a, jnp.concatenate([first, left[EDGE : rows - EDGE], last], axis=0))
        right = total(b)
        right = jnp.concatenate([right[:EDGE] + jnp.where(z > 0, dk[:, end].astype(F32), 0.0), right[EDGE:]], axis=0)
        put(b, jnp.where(low, right, v[...].astype(F32)))
        wait_all(run_copies([(e.at[here ^ m], outs[m]) for m in range(groups)], sems))

    return pl.pallas_call(
        body,
        out_shape=[jax.ShapeDtypeStruct((share, width), BF16)] * groups,
        in_specs=[pl.BlockSpec(memory_space=pltpu.VMEM)] * 6,
        out_specs=anywhere(groups),
        scratch_shapes=[pltpu.VMEM((groups, share, width), BF16), pltpu.SemaphoreType.DMA((groups,))],
        compiler_params=pltpu.CompilerParams(vmem_limit_bytes=VMEM_SMALL),
        cost_estimate=pl.CostEstimate(flops=0, bytes_accessed=9 * rows * width, transcendentals=0),
        name="finish_second",
    )(dy1, swap2, out2, v, dkedge, dqedge)


def unpack_early(parts):
    groups = len(parts)
    rows = parts[0].shape[0]
    width = parts[0].shape[1] // 2
    half = width // 2

    def body(*refs):
        dq, dk, dv, first, second, third, sems = refs[groups:]
        here, low = lax.axis_index("head"), lax.axis_index("ctx") < 2
        todo = []
        for m in range(groups):
            base = pl.multiple_of((here ^ m) * width, LANES)
            place = pl.multiple_of(base + jnp.where(low, 0, half), LANES)
            todo.append((refs[m].at[:, pl.ds(0, width)], first.at[:, pl.ds(base, width)]))
            todo.append((refs[m].at[:, pl.ds(width, half)], second.at[:, pl.ds(place, half)]))
            todo.append((refs[m].at[:, pl.ds(width + half, half)], third.at[:, pl.ds(base, half)]))
        wait_all(run_copies(todo, sems))

        @pl.when(low)
        def _():
            wait_all(run_copies([(first, dq), (second, dk), (third, dv)], sems))

        @pl.when(jnp.logical_not(low))
        def _():
            wait_all(run_copies([(first, dk), (second, dq), (third, dv)], sems))

    shape = jax.ShapeDtypeStruct((rows, groups * width), BF16)
    return pl.pallas_call(
        body,
        out_shape=[shape] * 3,
        in_specs=anywhere(groups),
        out_specs=anywhere(3),
        scratch_shapes=[pltpu.VMEM(shape.shape, BF16)] * 3 + [pltpu.SemaphoreType.DMA((3 * groups,))],
        cost_estimate=pl.CostEstimate(flops=0, bytes_accessed=10 * rows * groups * width, transcendentals=0),
        compiler_params=pltpu.CompilerParams(vmem_limit_bytes=VMEM_SMALL),
        name="unpack_early",
    )(*parts)


def unpack_late(parts, dq, dk, dv):
    groups = len(parts)
    rows, width = parts[0].shape
    half = width // 2

    def body(*refs):
        dq, dk, dv, held, sems = refs[groups + 3 :]
        here, low = lax.axis_index("head"), lax.axis_index("ctx") < 2
        loads = run_copies([(refs[m], held.at[m]) for m in range(groups)], sems)

        def moves(far, near):
            todo = []
            for m in range(groups):
                base = pl.multiple_of((here ^ m) * width, LANES)
                todo.append((held.at[m, :, pl.ds(0, half)], far.at[:, pl.ds(base + near, half)]))
                todo.append((held.at[m, :, pl.ds(half, half)], dv.at[:, pl.ds(base + half, half)]))
            return todo

        wait_all(loads)

        @pl.when(low)
        def _():
            wait_all(run_copies(moves(dk, half), sems))

        @pl.when(jnp.logical_not(low))
        def _():
            wait_all(run_copies(moves(dq, 0), sems))

    shape = jax.ShapeDtypeStruct(dq.shape, BF16)
    return pl.pallas_call(
        body,
        out_shape=[shape] * 3,
        in_specs=anywhere(groups + 3),
        out_specs=anywhere(3),
        scratch_shapes=[pltpu.VMEM((groups, rows, width), BF16), pltpu.SemaphoreType.DMA((2 * groups,))],
        input_output_aliases={groups: 0, groups + 1: 1, groups + 2: 2},
        compiler_params=pltpu.CompilerParams(vmem_limit_bytes=VMEM_SMALL),
        cost_estimate=pl.CostEstimate(flops=0, bytes_accessed=8 * rows * groups * width, transcendentals=0),
        name="unpack_late",
    )(*parts, dq, dk, dv)


def after(array, other):
    return lax.optimization_barrier((array, other))[0]


def local_split(queries, keys_in, values_in, attn_out, out_grad, log_norm, span_id):
    groups = lax.axis_size("head")
    width = queries.shape[1] // groups

    def swapped(parts):
        return [parts[0]] + [
            lax.ppermute(parts[m], "head", [(i, i ^ m) for i in range(groups)]) for m in range(1, groups)
        ]

    x1, x2, x3 = pack(queries, keys_in, values_in, attn_out, out_grad, span_id.reshape(1, -1), groups, width)
    x1 = swapped(x1)
    y1 = join_first(x1, log_norm.T)
    r1 = lax.ppermute(y1, "ctx", PAIRS)
    s1 = lax.ppermute(y1, "ctx", SWAP)
    x2 = swapped(x2)
    x3 = swapped(x3)
    y2 = join(x2)
    y2, r1, s1, x3 = lax.optimization_barrier((y2, r1, s1, x3))
    r2 = lax.ppermute(y2, "ctx", PAIRS)
    s2 = lax.ppermute(r1, "ctx", SWAP)
    w, key_edge, query_edge = join_last(x3, y1, y2)
    key_edge = lax.ppermute(key_edge, "ctx", DOWN)
    query_edge = lax.ppermute(query_edge, "ctx", UP)
    w, key_edge, query_edge = lax.optimization_barrier((w, key_edge, query_edge))
    swap1, out1, swap2, l1, l2, l3 = far_pairs(y1, y2, w, r1, r2, s1, s2)
    dw, dy1, dy2, dkedge, dqedge = near_pairs(y1, y2, w, after(key_edge, l3), query_edge)
    swap1 = lax.ppermute(swap1, "ctx", SWAP)
    out1 = lax.ppermute(out1, "ctx", PAIRS)
    dkedge = lax.ppermute(dkedge, "ctx", UP)
    dqedge = lax.ppermute(dqedge, "ctx", DOWN)
    swap1, swap2, out1, dkedge, dqedge = lax.optimization_barrier((swap1, swap2, out1, dkedge, dqedge))
    swap2 = lax.ppermute(swap2, "ctx", SWAP)
    out2 = lax.ppermute((swap1.astype(F32) + l3.astype(F32)).astype(BF16), "ctx", PAIRS)
    *early, kept = finish_first(dw, l1, dy2, l2, out1, dkedge, dqedge, groups)
    early = swapped(early)
    late = swapped(finish_second(dy1, swap2, out2, kept, dkedge, dqedge, groups))
    return tuple(unpack_late(late, *unpack_early(early)))


def splits(tokens, blocks, head_width, heads):
    if blocks != 4 or heads % 2 or head_width != LANES or 6 * heads + 1 > LANES:
        return False
    block = tokens // blocks
    span = -(-tokens // SPANS)
    for offset in range(SPANS * span - tokens + 1):
        for end in range(block, tokens, block):
            start = (end - 1 + offset) // span * span - offset
            if min(end - start, start + span - end) > EDGE or max(end - start, span) > block:
                return False
    return block % EDGE == 0


def local(queries, keys_in, values_in, attn_out, out_grad, log_norm, span_id):
    blocks, groups = lax.axis_size("ctx"), lax.axis_size("head")
    heads = log_norm.shape[1]
    tokens = queries.shape[0] * blocks * groups
    plan = local_plain
    if groups & (groups - 1) == 0 and splits(tokens, blocks, queries.shape[1] // (heads * groups), heads):
        plan = local_split
    return plan(queries, keys_in, values_in, attn_out, out_grad, log_norm, span_id)


def solution(mesh):
    placed = (
        P(("clip", "ctx", "head"), None),
        P(("clip", "ctx", "head"), None),
        P(("clip", "ctx", "head"), None),
        P(("clip", "ctx", "head"), None),
        P(("clip", "ctx", "head"), None),
        P(("clip", "ctx"), "head"),
        P(("clip", "ctx", "head")),
    )
    return jax.shard_map(
        local,
        mesh=mesh,
        in_specs=placed,
        out_specs=(
            P(("clip", "ctx", "head"), None),
            P(("clip", "ctx", "head"), None),
            P(("clip", "ctx", "head"), None),
        ),
        check_vma=False,
    )
```

```python
import math

import jax
import jax.numpy as jnp
from jax import lax
from jax.experimental import pallas as pl
from jax.experimental.pallas import tpu as pltpu
from jax.sharding import PartitionSpec as P

SPANS = 12
EDGE = 16
VMEM_LIMIT = 32 * 2**20
VMEM_SMALL = 16 * 2**20
VMEM_WHOLE = 60 * 2**20
LANES = 128
BF16 = jnp.bfloat16
F32 = jnp.float32

PAIRS = ((0, 1), (1, 0), (2, 3), (3, 2))
SWAP = ((1, 2), (2, 1))
DOWN = ((1, 0), (2, 1), (3, 2))
UP = ((0, 1), (1, 2), (2, 3))


def tile_terms(query_blk, grad_blk, norm_blk, delta_blk, query_ids, key_blk, value_blk, key_ids):
    row_count = query_blk.shape[0]
    key_count = key_blk.shape[0]
    head_count = norm_blk.shape[1]
    head_width = query_blk.shape[1] // head_count
    scale = 1.0 / math.sqrt(head_width)
    query3 = query_blk.reshape(row_count, head_count, head_width)
    grad3 = grad_blk.reshape(row_count, head_count, head_width)
    key3 = key_blk.reshape(key_count, head_count, head_width)
    value3 = value_blk.reshape(key_count, head_count, head_width)
    scores = jnp.einsum("rhd,khd->hrk", query3, key3, preferred_element_type=jnp.float32)
    visible = key_ids[None, :] <= query_ids[:, None]
    weight = jnp.where(visible[None], jnp.exp(scores * scale - norm_blk.T[:, :, None]), 0.0)
    weight_low = weight.astype(jnp.bfloat16)
    dweight = jnp.einsum("rhd,khd->hrk", grad3, value3, preferred_element_type=jnp.float32)
    dscore = (weight * (dweight - delta_blk.T[:, :, None]) * scale).astype(jnp.bfloat16)
    query_term = jnp.einsum("hrk,khd->rhd", dscore, key3, preferred_element_type=jnp.float32)
    key_term = jnp.einsum("hrk,rhd->khd", dscore, query3, preferred_element_type=jnp.float32)
    value_term = jnp.einsum("hrk,rhd->khd", weight_low, grad3, preferred_element_type=jnp.float32)
    return (
        query_term.reshape(row_count, -1),
        key_term.reshape(key_count, -1),
        value_term.reshape(key_count, -1),
    )


def rounded(term):
    return lax.optimization_barrier(term.astype(jnp.bfloat16)).astype(jnp.float32)


def local_plain(queries, keys_in, values_in, attn_out, out_grad, log_norm, span_id):
    local_q, local_k, local_v, local_out, local_grad = (
        lax.all_to_all(queries, "head", split_axis=1, concat_axis=0, tiled=True),
        lax.all_to_all(keys_in, "head", split_axis=1, concat_axis=0, tiled=True),
        lax.all_to_all(values_in, "head", split_axis=1, concat_axis=0, tiled=True),
        lax.all_to_all(attn_out, "head", split_axis=1, concat_axis=0, tiled=True),
        lax.all_to_all(out_grad, "head", split_axis=1, concat_axis=0, tiled=True),
    )
    all_ids = lax.all_gather(span_id, ("ctx", "head"), axis=0, tiled=True)
    seg_rows = local_q.shape[0]
    block_count = lax.axis_size("ctx")
    head_count = log_norm.shape[1]
    head_width = local_q.shape[1] // head_count
    my_block = lax.axis_index("ctx")
    own_ids = lax.dynamic_slice_in_dim(all_ids, my_block * seg_rows, seg_rows)
    id_blocks = all_ids.reshape(block_count, seg_rows)
    deltas = jnp.sum(
        (local_grad.astype(jnp.float32) * local_out.astype(jnp.float32)).reshape(
            seg_rows, head_count, head_width
        ),
        axis=2,
    )
    far_queries, far_grads = (
        lax.all_gather(local_q, "ctx", axis=0, tiled=True),
        lax.all_gather(local_grad, "ctx", axis=0, tiled=True),
    )
    far_norms, far_deltas = (
        lax.all_gather(log_norm, "ctx", axis=0, tiled=True),
        lax.all_gather(deltas, "ctx", axis=0, tiled=True),
    )

    def query_step(totals, piece):
        query_blk, grad_blk, norm_blk, delta_blk, query_ids = piece
        query_term, key_term, value_term = tile_terms(
            query_blk, grad_blk, norm_blk, delta_blk, query_ids, local_k, local_v, own_ids
        )
        return ((totals[0] + rounded(key_term), totals[1] + rounded(value_term)), query_term)

    zero_block = jnp.zeros(local_k.shape, jnp.float32)
    (dk_total, dv_total), query_terms = lax.scan(
        query_step,
        (zero_block, zero_block),
        (
            far_queries.reshape(block_count, seg_rows, -1),
            far_grads.reshape(block_count, seg_rows, -1),
            far_norms.reshape(block_count, seg_rows, -1),
            far_deltas.reshape(block_count, seg_rows, -1),
            id_blocks,
        ),
    )
    query_sum = lax.psum_scatter(
        query_terms.reshape(block_count * seg_rows, -1).astype(jnp.bfloat16),
        "ctx",
        scatter_dimension=0,
        tiled=True,
    )
    dk_local = dk_total.astype(jnp.bfloat16)
    dv_local = dv_total.astype(jnp.bfloat16)
    query_grad, key_grad, value_grad = (
        lax.all_to_all(query_sum, "head", split_axis=0, concat_axis=1, tiled=True),
        lax.all_to_all(dk_local, "head", split_axis=0, concat_axis=1, tiled=True),
        lax.all_to_all(dv_local, "head", split_axis=0, concat_axis=1, tiled=True),
    )
    return (query_grad, key_grad, value_grad)


def nt(a, b):
    return lax.dot_general(a, b, (((1,), (1,)), ((), ())), preferred_element_type=F32)


def tn(a, b):
    return lax.dot_general(a, b, (((0,), (0,)), ((), ())), preferred_element_type=F32)


def pieces(value):
    high = value.astype(BF16)
    rest = value - high.astype(F32)
    middle = rest.astype(BF16)
    low = (rest - middle.astype(F32)).astype(BF16)
    return high, middle, low


def run_copies(pairs, sems, first=0):
    made = [pltpu.make_async_copy(src, dst, sems.at[first + i]) for i, (src, dst) in enumerate(pairs)]
    for copy in made:
        copy.start()
    return made


def wait_all(made):
    for copy in made:
        copy.wait()


def anywhere(count):
    return [pl.BlockSpec(memory_space=pl.ANY)] * count


def pack(queries, keys_in, values_in, attn_out, out_grad, span_row, groups, width):
    rows = queries.shape[0]
    heads = width // LANES
    half = width // 2

    def body(q, k, v, o, g, ids, *refs):
        x1, x2, x3 = refs[:groups], refs[groups : 2 * groups], refs[2 * groups : 3 * groups]
        q_v, k_v, v_v, o_v, g_v, meta, sems = refs[3 * groups :]
        here = lax.axis_index("head")
        low = lax.axis_index("ctx") < 2
        loads = run_copies([(k, k_v), (v, v_v), (q, q_v), (g, g_v), (o, o_v)], sems)

        def moves(first, second, third, fourth, near, far):
            todo = []
            for m in range(groups):
                base = pl.multiple_of((here ^ m) * width, LANES)
                todo.append((first.at[:, pl.ds(base + near, half)], x1[m].at[:, pl.ds(0, half)]))
                todo.append((second.at[:, pl.ds(base + near, half)], x1[m].at[:, pl.ds(half, half)]))
            for m in range(groups):
                base = pl.multiple_of((here ^ m) * width, LANES)
                todo.append((first.at[:, pl.ds(base + far, half)], x2[m].at[:, pl.ds(0, half)]))
                todo.append((second.at[:, pl.ds(base + far, half)], x2[m].at[:, pl.ds(half, half)]))
                todo.append((third.at[:, pl.ds(base, width)], x3[m].at[:, pl.ds(0, width)]))
                todo.append((fourth.at[:, pl.ds(base, width)], x3[m].at[:, pl.ds(width, width)]))
            return [pltpu.make_async_copy(src, dst, sems.at[5 + i]) for i, (src, dst) in enumerate(todo)]

        low_moves = (k_v, v_v, q_v, g_v, half, 0)
        high_moves = (q_v, g_v, k_v, v_v, 0, half)
        wait_all(loads[:4])

        @pl.when(low)
        def _():
            for copy in moves(*low_moves):
                copy.start()

        @pl.when(jnp.logical_not(low))
        def _():
            for copy in moves(*high_moves):
                copy.start()

        wait_all(loads[4:])
        lane = lax.broadcasted_iota(jnp.int32, (rows, LANES), 1)
        slot = jnp.where(lane < 3 * heads, lane % heads, -1)
        at_row = lax.broadcasted_iota(jnp.int32, (rows, rows), 0)
        at_col = lax.broadcasted_iota(jnp.int32, (rows, rows), 1)
        own = jnp.sum(jnp.where(at_row == at_col, ids[...].astype(F32), 0.0), axis=1, keepdims=True)
        for h in range(groups):
            total = jnp.zeros((rows, LANES), F32)
            for c in range(heads):
                cols = pl.ds(h * width + c * LANES, LANES)
                delta = jnp.sum(o_v[:, cols].astype(F32) * g_v[:, cols].astype(F32), axis=1, keepdims=True)
                total = jnp.where(slot == c, delta, total)
            high, middle, lowest = pieces(total)
            kept = jnp.where(lane < heads, high, jnp.where(lane < 2 * heads, middle, lowest))
            meta[h] = jnp.where(lane < 3 * heads, kept, jnp.where(lane == 3 * heads, own.astype(BF16), 0.0).astype(BF16))
        last = run_copies(
            [(meta.at[here ^ m], x1[m].at[:, pl.ds(width, LANES)]) for m in range(groups)], sems, 5 + 6 * groups
        )

        @pl.when(low)
        def _():
            wait_all(moves(*low_moves))

        @pl.when(jnp.logical_not(low))
        def _():
            wait_all(moves(*high_moves))

        wait_all(last)

    whole = pltpu.VMEM((rows, groups * width), BF16)
    made = pl.pallas_call(
        body,
        out_shape=[
            jax.ShapeDtypeStruct((rows, size), BF16)
            for size in (width + LANES, width, 2 * width)
            for _ in range(groups)
        ],
        in_specs=anywhere(5) + [pl.BlockSpec(memory_space=pltpu.VMEM)],
        out_specs=anywhere(3 * groups),
        scratch_shapes=[whole] * 5
        + [pltpu.VMEM((groups, rows, LANES), BF16), pltpu.SemaphoreType.DMA((5 + 7 * groups,))],
        cost_estimate=pl.CostEstimate(flops=0, bytes_accessed=10 * rows * groups * width * 2, transcendentals=0),
        compiler_params=pltpu.CompilerParams(vmem_limit_bytes=VMEM_WHOLE),
        name="pack",
    )(queries, keys_in, values_in, attn_out, out_grad, span_row)
    return made[:groups], made[groups : 2 * groups], made[2 * groups :]


def join_first(parts, norm_rows):
    groups = len(parts)
    rows, width = parts[0].shape
    heads = norm_rows.shape[0]

    def body(*refs):
        norm, y, sems = refs[groups:]
        here = lax.axis_index("head")
        made = run_copies([(refs[m], y.at[here ^ m]) for m in range(groups)], sems)
        at_row = lax.broadcasted_iota(jnp.int32, (heads, LANES), 0)
        at_lane = lax.broadcasted_iota(jnp.int32, (heads, LANES), 1)
        total = jnp.zeros((groups * rows, LANES), F32)
        for i, piece in enumerate(pieces(norm[...])):
            place = jnp.where(at_lane == at_row + (3 * heads + 1 + i * heads), 1.0, 0.0).astype(BF16)
            total += tn(piece, place)
        wait_all(made)
        tail = pl.ds(width - LANES, LANES)
        for h in range(groups):
            y[h, :, tail] = (y[h, :, tail].astype(F32) + total[h * rows : (h + 1) * rows]).astype(BF16)

    return pl.pallas_call(
        body,
        out_shape=jax.ShapeDtypeStruct((groups, rows, width), BF16),
        in_specs=anywhere(groups) + [pl.BlockSpec(memory_space=pltpu.VMEM)],
        out_specs=pl.BlockSpec(memory_space=pltpu.VMEM),
        scratch_shapes=[pltpu.SemaphoreType.DMA((groups,))],
        cost_estimate=pl.CostEstimate(flops=0, bytes_accessed=4 * groups * rows * width, transcendentals=0),
        compiler_params=pltpu.CompilerParams(vmem_limit_bytes=VMEM_SMALL),
        name="join_first",
    )(*parts, norm_rows).reshape(groups * rows, width)


def join(parts):
    groups = len(parts)
    rows, width = parts[0].shape

    def body(*refs):
        y, sems = refs[groups:]
        here = lax.axis_index("head")
        wait_all(run_copies([(refs[m], y.at[here ^ m]) for m in range(groups)], sems))

    return pl.pallas_call(
        body,
        out_shape=jax.ShapeDtypeStruct((groups, rows, width), BF16),
        in_specs=anywhere(groups),
        out_specs=pl.BlockSpec(memory_space=pltpu.VMEM),
        scratch_shapes=[pltpu.SemaphoreType.DMA((groups,))],
        cost_estimate=pl.CostEstimate(flops=0, bytes_accessed=4 * groups * rows * width, transcendentals=0),
        compiler_params=pltpu.CompilerParams(vmem_limit_bytes=VMEM_SMALL),
        name="join",
    )(*parts).reshape(groups * rows, width)


def token_rows(meta, heads):
    at_row = lax.broadcasted_iota(jnp.int32, (32, LANES), 0)
    at_lane = lax.broadcasted_iota(jnp.int32, (32, LANES), 1)
    norm_lane = at_lane - (3 * heads + 1)
    is_norm = (norm_lane >= 0) & (norm_lane < 3 * heads) & (norm_lane % heads == at_row) & (at_row < heads)
    is_delta = (at_lane < 3 * heads) & (at_lane % heads == at_row - heads) & (at_row >= heads)
    is_id = (at_lane == 3 * heads) & (at_row == 2 * heads)
    chosen = jnp.where(is_norm | is_delta | is_id, 1.0, 0.0).astype(BF16)
    return nt(chosen, meta)


def pair_terms(query, grad, key, value, norm, delta, visible=None):
    scale = 1.0 / math.sqrt(query.shape[1])
    weight = jnp.exp(nt(key, query) * scale - norm)
    if visible is not None:
        weight = jnp.where(visible, weight, 0.0)
    dscore = (weight * (nt(value, grad) - delta) * scale).astype(BF16)
    value_term = jnp.dot(weight.astype(BF16), grad, preferred_element_type=F32)
    key_term = jnp.dot(dscore, query, preferred_element_type=F32)
    query_term = tn(dscore, key)
    return query_term, key_term, value_term


def join_last(parts, y1, y2):
    groups = len(parts)
    share = parts[0].shape[0]
    rows, width = y2.shape
    half = width // 2

    def body(*refs):
        y1, y2, w, kedge, qedge, sems = refs[groups:]
        here, low = lax.axis_index("head"), lax.axis_index("ctx") < 2
        top, bottom, tail = pl.ds(0, EDGE), pl.ds(rows - EDGE, EDGE), pl.ds(width, LANES)
        whole, end = pl.ds(0, 2 * width), pl.ds(2 * width, LANES)
        made = run_copies([(y1.at[top, tail], kedge.at[:, end]), (y1.at[bottom, tail], qedge.at[:, end])], sems)
        loads = run_copies([(refs[m], w.at[here ^ m]) for m in range(groups)], sems, 2)

        def joined(first, second, at, edge):
            todo = []
            for i in range(2):
                for j, part in enumerate((first, second)):
                    todo.append((part.at[at, pl.ds(i * half, half)], edge.at[:, pl.ds(i * width + j * half, half)]))
            return todo

        @pl.when(low)
        def _():
            wait_all(run_copies(joined(y2, y1, top, kedge), sems, 2 + groups))

        @pl.when(jnp.logical_not(low))
        def _():
            wait_all(run_copies(joined(y1, y2, bottom, qedge), sems, 2 + groups))

        wait_all(loads)

        @pl.when(low)
        def _():
            qedge[:, whole] = w[groups - 1, share - EDGE :, :]

        @pl.when(jnp.logical_not(low))
        def _():
            kedge[:, whole] = w[0, :EDGE, :]

        wait_all(made)

    edge = jax.ShapeDtypeStruct((EDGE, 2 * width + LANES), BF16)
    w, key_edge, query_edge = pl.pallas_call(
        body,
        out_shape=[jax.ShapeDtypeStruct((groups, share, 2 * width), BF16), edge, edge],
        in_specs=anywhere(groups + 2),
        out_specs=[pl.BlockSpec(memory_space=pltpu.VMEM)] * 3,
        scratch_shapes=[pltpu.SemaphoreType.DMA((6 + groups,))],
        compiler_params=pltpu.CompilerParams(vmem_limit_bytes=VMEM_SMALL),
        cost_estimate=pl.CostEstimate(flops=0, bytes_accessed=8 * rows * width, transcendentals=0),
        name="join_last",
    )(*parts, y1, y2)
    return w.reshape(rows, 2 * width), key_edge, query_edge


def in_vmem(count):
    return [pl.BlockSpec(memory_space=pltpu.VMEM)] * count


def far_pairs(y1, y2, w, r1, r2, s1, s2):
    rows, width = y2.shape
    half = width // 2
    count = half // LANES
    heads = 2 * count

    def body(y1, y2, w, r1, r2, s1, s2, swap1, out1, swap2, l1, l2, l3, info):
        z = lax.axis_index("ctx")

        def both(ref, at=0, gap=half):
            return lambda c: (
                ref[:, at + c * LANES : at + (c + 1) * LANES],
                ref[:, at + gap + c * LANES : at + gap + (c + 1) * LANES],
            )

        def put(ref, at, value):
            ref[:, at : at + LANES] = value.astype(BF16)

        def scalars(slot, head):
            return info[slot, head : head + 1, :], info[slot, heads + head : heads + head + 1, :]

        def square(query_2, query_3, key_0, key_1, c, head):
            keys, values = zip(key_0(c), key_1(c))
            key, value = jnp.concatenate(keys, axis=0), jnp.concatenate(values, axis=0)
            first = pair_terms(*query_2(c), key, value, *scalars(0, head))
            second = pair_terms(*query_3(c), key, value, *scalars(1, head))
            return first[0], second[0], first[1] + second[1], first[2] + second[2]

        tail = pl.ds(width, LANES)

        @pl.when(z == 1)
        def _():
            for slot, ref in enumerate((s1, s2, y1)):
                info[slot] = token_rows(ref[:, tail], heads)
            for c in range(count):
                a, b = c * LANES, half + c * LANES
                own = pair_terms(*both(w, 0, width)(c), *both(r2)(c), *scalars(2, c))
                query_2, query_3, key, value = square(both(s1), both(s2), both(r2), both(y2), c, c)
                put(swap1, a, query_3)
                put(swap2, a, query_2)
                put(out1, a, key[:rows] + own[1])
                put(out1, b, value[:rows] + own[2])
                put(l2, a, key[rows:])
                put(l2, b, value[rows:])
                put(l1, a, own[0])
                own = pair_terms(*both(w, half, width)(c), *both(r1)(c), *scalars(2, count + c))
                put(l1, half + a, own[0])
                put(l3, a, own[1])
                put(l3, b, own[2])

        @pl.when(z == 2)
        def _():
            for slot, ref in enumerate((y1, r1)):
                info[slot] = token_rows(ref[:, tail], heads)
            for c in range(count):
                a, b = c * LANES, half + c * LANES
                own = pair_terms(*both(r2)(c), *both(w, half, width)(c), *scalars(1, count + c))
                query_2, query_3, key, value = square(both(y2), both(r2), both(s2), both(s1), c, count + c)
                put(swap1, a, key[:rows])
                put(swap1, b, value[:rows])
                put(swap2, a, key[rows:])
                put(swap2, b, value[rows:])
                put(out1, a, query_3 + own[0])
                put(l2, a, query_2)
                put(l1, b, own[1])
                put(l1, width + b, own[2])
                own = pair_terms(*both(r1)(c), *both(w, 0, width)(c), *scalars(1, c))
                put(l1, a, own[1])
                put(l1, width + a, own[2])
                put(l3, a, own[0])

    single = jax.ShapeDtypeStruct((rows, width), BF16)
    return pl.pallas_call(
        body,
        out_shape=[single, single, single, jax.ShapeDtypeStruct((rows, 2 * width), BF16), single, single],
        in_specs=in_vmem(7),
        out_specs=in_vmem(6),
        scratch_shapes=[pltpu.VMEM((3, 32, rows), F32)],
        compiler_params=pltpu.CompilerParams(vmem_limit_bytes=VMEM_LIMIT),
        cost_estimate=pl.CostEstimate(
            flops=30 * 10 * rows * rows * LANES, bytes_accessed=30 * rows * width, transcendentals=30 * rows * rows
        ),
        name="far_pairs",
    )(y1, y2, w, r1, r2, s1, s2)


def near_pairs(y1, y2, w, key_edge, query_edge):
    rows, width = y2.shape
    half = width // 2
    count = half // LANES
    heads = 2 * count
    total = rows + EDGE

    def body(y1, y2, w, kedge, qedge, dw, dy1, dy2, dkedge, dqedge, info):
        z = lax.axis_index("ctx")
        tail, end = pl.ds(width, LANES), pl.ds(2 * width, LANES)
        info[...] = token_rows(jnp.concatenate([y1[:, tail], qedge[:, end]], axis=0), heads)
        key_meta = jnp.concatenate([y1[:, tail], kedge[:, end]], axis=0).astype(F32)
        id_lane = lax.broadcasted_iota(jnp.int32, (total, LANES), 1) == 3 * heads
        key_ids = jnp.sum(jnp.where(id_lane, key_meta, 0.0), axis=1, keepdims=True)
        at_key = lax.broadcasted_iota(jnp.int32, (total, total), 0)
        at_query = lax.broadcasted_iota(jnp.int32, (total, total), 1)
        last_key = jnp.where(z < 3, total, rows)
        last_query = jnp.where(z > 0, total, rows)
        visible = (key_ids <= info[2 * heads : 2 * heads + 1, :]) & ((at_key < rows) | (at_query < rows - EDGE))
        visible = visible & (at_key < last_key) & (at_query < last_query)

        def head_terms(i, c, payload):
            a, b = i * half + c * LANES, width + i * half + c * LANES
            small, large = c * LANES, half + c * LANES
            wide = w[:, a : a + LANES], w[:, b : b + LANES]
            narrow = payload[:, small : small + LANES], payload[:, large : large + LANES]
            edge_k, edge_q = (
                (edge[:, a : a + LANES], edge[:, b : b + LANES]) for edge in (kedge, qedge)
            )

            def terms(queries, keys):
                query, grad = (jnp.concatenate(x, axis=0) for x in zip(queries, edge_q))
                key, value = (jnp.concatenate(x, axis=0) for x in zip(keys, edge_k))
                scalars = info[i * count + c : i * count + c + 1, :], info[heads + i * count + c : heads + i * count + c + 1, :]
                made = [x.astype(BF16) for x in pair_terms(query, grad, key, value, *scalars, visible)]
                dqedge[:, a : a + LANES] = made[0][rows:]
                dkedge[:, a : a + LANES] = made[1][rows:]
                dkedge[:, b : b + LANES] = made[2][rows:]
                return [x[:rows] for x in made]

            return a, b, small, large, wide, narrow, terms

        @pl.when(z < 2)
        def _():
            for i, (payload, result) in enumerate(((y2, dy2), (y1, dy1))):
                for c in range(count):
                    a, b, small, large, wide, narrow, terms = head_terms(i, c, payload)
                    query_term, key_term, value_term = terms(wide, narrow)
                    dw[:, a : a + LANES] = query_term
                    result[:, small : small + LANES] = key_term
                    result[:, large : large + LANES] = value_term

        @pl.when(z >= 2)
        def _():
            for i, (payload, result) in enumerate(((y1, dy1), (y2, dy2))):
                for c in range(count):
                    a, b, small, large, wide, narrow, terms = head_terms(i, c, payload)
                    query_term, key_term, value_term = terms(narrow, wide)
                    result[:, small : small + LANES] = query_term
                    dw[:, a : a + LANES] = key_term
                    dw[:, b : b + LANES] = value_term

    return pl.pallas_call(
        body,
        out_shape=[
            jax.ShapeDtypeStruct((rows, 2 * width), BF16),
            jax.ShapeDtypeStruct((rows, width), BF16),
            jax.ShapeDtypeStruct((rows, width), BF16),
            jax.ShapeDtypeStruct((EDGE, 2 * width), BF16),
            jax.ShapeDtypeStruct((EDGE, width), BF16),
        ],
        in_specs=in_vmem(5),
        out_specs=in_vmem(5),
        scratch_shapes=[pltpu.VMEM((32, total), F32)],
        compiler_params=pltpu.CompilerParams(vmem_limit_bytes=VMEM_LIMIT),
        cost_estimate=pl.CostEstimate(
            flops=10 * 10 * rows * rows * LANES, bytes_accessed=16 * rows * width, transcendentals=10 * rows * rows
        ),
        name="near_pairs",
    )(y1, y2, w, key_edge, query_edge)


def finish_first(dw, l1, dy2, l2, out1, dkedge, dqedge, groups):
    rows, width = dy2.shape
    half = width // 2
    share = rows // groups

    def body(dw, l1, dy2, l2, out1, dk, dq, *refs):
        outs, v, e, sems = refs[:groups], *refs[groups:]
        here = lax.axis_index("head")
        z = lax.axis_index("ctx")
        low, middle = z < 2, (z == 1) | (z == 2)
        after_first, before_last = z > 0, z < 3

        def own(cols):
            return dw[:, cols].astype(F32) + jnp.where(middle, l1[:, cols].astype(F32), 0.0)

        def second(cols):
            return dy2[:, cols].astype(F32) + jnp.where(middle, l2[:, cols], out1[:, cols]).astype(F32)

        def put(dst, cols, total, first, last=None):
            end = total[rows - EDGE :] if last is None else total[rows - EDGE :] + last
            total = jnp.concatenate([total[:EDGE] + first, total[EDGE : rows - EDGE], end], axis=0)
            for h in range(groups):
                dst[h, :, cols] = total[h * share : (h + 1) * share].astype(BF16)

        def key_edge(cols):
            return jnp.where(after_first, dk[:, cols].astype(F32), 0.0)

        def query_edge(cols):
            return jnp.where(before_last, dq[:, cols].astype(F32), 0.0)

        a, b = pl.ds(0, half), pl.ds(half, half)
        c, d = pl.ds(width, half), pl.ds(width + half, half)
        for cols in (a, b):
            put(e, cols, own(cols), jnp.where(low, 0.0, key_edge(cols)), jnp.where(low, query_edge(cols), 0.0))
        put(e, c, second(a), jnp.where(low, key_edge(a), 0.0), jnp.where(low, 0.0, query_edge(b)))
        put(e, d, jnp.where(low, second(b), own(c)), key_edge(c))
        made = run_copies([(e.at[here ^ m], outs[m]) for m in range(groups)], sems)
        left_over = own(d)
        left_over = jnp.concatenate([left_over[:EDGE] + key_edge(d), left_over[EDGE:]], axis=0)
        v[...] = left_over.astype(BF16)
        wait_all(made)

    return pl.pallas_call(
        body,
        out_shape=[jax.ShapeDtypeStruct((share, 2 * width), BF16)] * groups + [jax.ShapeDtypeStruct((rows, half), BF16)],
        in_specs=[pl.BlockSpec(memory_space=pltpu.VMEM)] * 7,
        out_specs=anywhere(groups) + [pl.BlockSpec(memory_space=pltpu.VMEM)],
        scratch_shapes=[pltpu.VMEM((groups, share, 2 * width), BF16), pltpu.SemaphoreType.DMA((groups,))],
        compiler_params=pltpu.CompilerParams(vmem_limit_bytes=VMEM_SMALL),
        cost_estimate=pl.CostEstimate(flops=0, bytes_accessed=16 * rows * width, transcendentals=0),
        name="finish_first",
    )(dw, l1, dy2, l2, out1, dkedge, dqedge)


def finish_second(dy1, swap2, out2, v, dkedge, dqedge, groups):
    rows, width = dy1.shape
    half = width // 2
    share = rows // groups

    def body(dy1, swap2, out2, v, dk, dq, *refs):
        outs, e, sems = refs[:groups], *refs[groups:]
        here, z = lax.axis_index("head"), lax.axis_index("ctx")
        low, middle = z < 2, (z == 1) | (z == 2)

        def put(cols, whole):
            for h in range(groups):
                e[h, :, cols] = whole[h * share : (h + 1) * share].astype(BF16)

        a, b = pl.ds(0, half), pl.ds(half, half)
        end = pl.ds(width + half, half)

        def total(cols):
            return dy1[:, cols].astype(F32) + jnp.where(middle, swap2[:, cols], out2[:, cols]).astype(F32)

        left = total(a)
        first = left[:EDGE] + jnp.where(z == 1, dk[:, b].astype(F32), 0.0)
        last = left[rows - EDGE :] + jnp.where(z == 2, dq[:, a].astype(F32), 0.0)
        put(a, jnp.concatenate([first, left[EDGE : rows - EDGE], last], axis=0))
        right = total(b)
        right = jnp.concatenate([right[:EDGE] + jnp.where(z > 0, dk[:, end].astype(F32), 0.0), right[EDGE:]], axis=0)
        put(b, jnp.where(low, right, v[...].astype(F32)))
        wait_all(run_copies([(e.at[here ^ m], outs[m]) for m in range(groups)], sems))

    return pl.pallas_call(
        body,
        out_shape=[jax.ShapeDtypeStruct((share, width), BF16)] * groups,
        in_specs=[pl.BlockSpec(memory_space=pltpu.VMEM)] * 6,
        out_specs=anywhere(groups),
        scratch_shapes=[pltpu.VMEM((groups, share, width), BF16), pltpu.SemaphoreType.DMA((groups,))],
        compiler_params=pltpu.CompilerParams(vmem_limit_bytes=VMEM_SMALL),
        cost_estimate=pl.CostEstimate(flops=0, bytes_accessed=9 * rows * width, transcendentals=0),
        name="finish_second",
    )(dy1, swap2, out2, v, dkedge, dqedge)


def unpack_early(parts):
    groups = len(parts)
    rows = parts[0].shape[0]
    width = parts[0].shape[1] // 2
    half = width // 2

    def body(*refs):
        dq, dk, dv, first, second, third, sems = refs[groups:]
        here, low = lax.axis_index("head"), lax.axis_index("ctx") < 2
        todo = []
        for m in range(groups):
            base = pl.multiple_of((here ^ m) * width, LANES)
            place = pl.multiple_of(base + jnp.where(low, 0, half), LANES)
            todo.append((refs[m].at[:, pl.ds(0, width)], first.at[:, pl.ds(base, width)]))
            todo.append((refs[m].at[:, pl.ds(width, half)], second.at[:, pl.ds(place, half)]))
            todo.append((refs[m].at[:, pl.ds(width + half, half)], third.at[:, pl.ds(base, half)]))
        wait_all(run_copies(todo, sems))

        @pl.when(low)
        def _():
            wait_all(run_copies([(first, dq), (second, dk), (third, dv)], sems))

        @pl.when(jnp.logical_not(low))
        def _():
            wait_all(run_copies([(first, dk), (second, dq), (third, dv)], sems))

    shape = jax.ShapeDtypeStruct((rows, groups * width), BF16)
    return pl.pallas_call(
        body,
        out_shape=[shape] * 3,
        in_specs=anywhere(groups),
        out_specs=anywhere(3),
        scratch_shapes=[pltpu.VMEM(shape.shape, BF16)] * 3 + [pltpu.SemaphoreType.DMA((3 * groups,))],
        cost_estimate=pl.CostEstimate(flops=0, bytes_accessed=10 * rows * groups * width, transcendentals=0),
        compiler_params=pltpu.CompilerParams(vmem_limit_bytes=VMEM_SMALL),
        name="unpack_early",
    )(*parts)


def unpack_late(parts, dq, dk, dv):
    groups = len(parts)
    rows, width = parts[0].shape
    half = width // 2

    def body(*refs):
        dq, dk, dv, held, sems = refs[groups + 3 :]
        here, low = lax.axis_index("head"), lax.axis_index("ctx") < 2
        loads = run_copies([(refs[m], held.at[m]) for m in range(groups)], sems)

        def moves(far, near):
            todo = []
            for m in range(groups):
                base = pl.multiple_of((here ^ m) * width, LANES)
                todo.append((held.at[m, :, pl.ds(0, half)], far.at[:, pl.ds(base + near, half)]))
                todo.append((held.at[m, :, pl.ds(half, half)], dv.at[:, pl.ds(base + half, half)]))
            return todo

        wait_all(loads)

        @pl.when(low)
        def _():
            wait_all(run_copies(moves(dk, half), sems))

        @pl.when(jnp.logical_not(low))
        def _():
            wait_all(run_copies(moves(dq, 0), sems))

    shape = jax.ShapeDtypeStruct(dq.shape, BF16)
    return pl.pallas_call(
        body,
        out_shape=[shape] * 3,
        in_specs=anywhere(groups + 3),
        out_specs=anywhere(3),
        scratch_shapes=[pltpu.VMEM((groups, rows, width), BF16), pltpu.SemaphoreType.DMA((2 * groups,))],
        input_output_aliases={groups: 0, groups + 1: 1, groups + 2: 2},
        compiler_params=pltpu.CompilerParams(vmem_limit_bytes=VMEM_SMALL),
        cost_estimate=pl.CostEstimate(flops=0, bytes_accessed=8 * rows * groups * width, transcendentals=0),
        name="unpack_late",
    )(*parts, dq, dk, dv)


def after(array, other):
    return lax.optimization_barrier((array, other))[0]


def local_split(queries, keys_in, values_in, attn_out, out_grad, log_norm, span_id):
    groups = lax.axis_size("head")
    width = queries.shape[1] // groups

    def swapped(parts):
        return [parts[0]] + [
            lax.ppermute(parts[m], "head", [(i, i ^ m) for i in range(groups)]) for m in range(1, groups)
        ]

    x1, x2, x3 = pack(queries, keys_in, values_in, attn_out, out_grad, span_id.reshape(1, -1), groups, width)
    x1, x2 = swapped(x1), swapped(x2)
    y1 = join_first(x1, log_norm.T)
    y1, x2[1], x2[2] = lax.optimization_barrier((y1, x2[1], x2[2]))
    r1 = lax.ppermute(y1, "ctx", PAIRS)
    s1 = lax.ppermute(y1, "ctx", SWAP)
    x3 = swapped(x3)
    y2 = join(x2)
    y2, r1, s1, x3 = lax.optimization_barrier((y2, r1, s1, x3))
    r2 = lax.ppermute(y2, "ctx", PAIRS)
    s2 = lax.ppermute(r1, "ctx", SWAP)
    w, key_edge, query_edge = join_last(x3, y1, y2)
    key_edge = lax.ppermute(key_edge, "ctx", DOWN)
    query_edge = lax.ppermute(query_edge, "ctx", UP)
    w, key_edge, query_edge = lax.optimization_barrier((w, key_edge, query_edge))
    swap1, out1, swap2, l1, l2, l3 = far_pairs(y1, y2, w, r1, r2, s1, s2)
    dw, dy1, dy2, dkedge, dqedge = near_pairs(y1, y2, w, after(key_edge, l3), query_edge)
    swap1 = lax.ppermute(swap1, "ctx", SWAP)
    out1 = lax.ppermute(out1, "ctx", PAIRS)
    dkedge = lax.ppermute(dkedge, "ctx", UP)
    dqedge = lax.ppermute(dqedge, "ctx", DOWN)
    swap1, swap2, out1, dkedge, dqedge = lax.optimization_barrier((swap1, swap2, out1, dkedge, dqedge))
    swap2 = lax.ppermute(swap2, "ctx", SWAP)
    out2 = lax.ppermute((swap1.astype(F32) + l3.astype(F32)).astype(BF16), "ctx", PAIRS)
    *early, kept = finish_first(dw, l1, dy2, l2, out1, dkedge, dqedge, groups)
    early = swapped(early)
    late = swapped(finish_second(dy1, swap2, out2, kept, dkedge, dqedge, groups))
    return tuple(unpack_late(late, *unpack_early(early)))


def splits(tokens, blocks, head_width, heads):
    if blocks != 4 or heads % 2 or head_width != LANES or 6 * heads + 1 > LANES:
        return False
    block = tokens // blocks
    span = -(-tokens // SPANS)
    for offset in range(SPANS * span - tokens + 1):
        for end in range(block, tokens, block):
            start = (end - 1 + offset) // span * span - offset
            if min(end - start, start + span - end) > EDGE or max(end - start, span) > block:
                return False
    return block % EDGE == 0


def local(queries, keys_in, values_in, attn_out, out_grad, log_norm, span_id):
    blocks, groups = lax.axis_size("ctx"), lax.axis_size("head")
    heads = log_norm.shape[1]
    tokens = queries.shape[0] * blocks * groups
    plan = local_plain
    if groups & (groups - 1) == 0 and splits(tokens, blocks, queries.shape[1] // (heads * groups), heads):
        plan = local_split
    return plan(queries, keys_in, values_in, attn_out, out_grad, log_norm, span_id)


def solution(mesh):
    placed = (
        P(("clip", "ctx", "head"), None),
        P(("clip", "ctx", "head"), None),
        P(("clip", "ctx", "head"), None),
        P(("clip", "ctx", "head"), None),
        P(("clip", "ctx", "head"), None),
        P(("clip", "ctx"), "head"),
        P(("clip", "ctx", "head")),
    )
    return jax.shard_map(
        local,
        mesh=mesh,
        in_specs=placed,
        out_specs=(
            P(("clip", "ctx", "head"), None),
            P(("clip", "ctx", "head"), None),
            P(("clip", "ctx", "head"), None),
        ),
        check_vma=False,
    )
```

```python
import math

import jax
import jax.numpy as jnp
from jax import lax
from jax.experimental import pallas as pl
from jax.experimental.pallas import tpu as pltpu
from jax.sharding import PartitionSpec as P

SPANS = 12
EDGE = 16
VMEM_LIMIT = 32 * 2**20
VMEM_SMALL = 16 * 2**20
VMEM_WHOLE = 60 * 2**20
LANES = 128
BF16 = jnp.bfloat16
F32 = jnp.float32

PAIRS = ((0, 1), (1, 0), (2, 3), (3, 2))
SWAP = ((1, 2), (2, 1))


def tile_terms(query_blk, grad_blk, norm_blk, delta_blk, query_ids, key_blk, value_blk, key_ids):
    row_count = query_blk.shape[0]
    key_count = key_blk.shape[0]
    head_count = norm_blk.shape[1]
    head_width = query_blk.shape[1] // head_count
    scale = 1.0 / math.sqrt(head_width)
    query3 = query_blk.reshape(row_count, head_count, head_width)
    grad3 = grad_blk.reshape(row_count, head_count, head_width)
    key3 = key_blk.reshape(key_count, head_count, head_width)
    value3 = value_blk.reshape(key_count, head_count, head_width)
    scores = jnp.einsum("rhd,khd->hrk", query3, key3, preferred_element_type=jnp.float32)
    visible = key_ids[None, :] <= query_ids[:, None]
    weight = jnp.where(visible[None], jnp.exp(scores * scale - norm_blk.T[:, :, None]), 0.0)
    weight_low = weight.astype(jnp.bfloat16)
    dweight = jnp.einsum("rhd,khd->hrk", grad3, value3, preferred_element_type=jnp.float32)
    dscore = (weight * (dweight - delta_blk.T[:, :, None]) * scale).astype(jnp.bfloat16)
    query_term = jnp.einsum("hrk,khd->rhd", dscore, key3, preferred_element_type=jnp.float32)
    key_term = jnp.einsum("hrk,rhd->khd", dscore, query3, preferred_element_type=jnp.float32)
    value_term = jnp.einsum("hrk,rhd->khd", weight_low, grad3, preferred_element_type=jnp.float32)
    return (
        query_term.reshape(row_count, -1),
        key_term.reshape(key_count, -1),
        value_term.reshape(key_count, -1),
    )


def rounded(term):
    return lax.optimization_barrier(term.astype(jnp.bfloat16)).astype(jnp.float32)


def local_plain(queries, keys_in, values_in, attn_out, out_grad, log_norm, span_id):
    local_q, local_k, local_v, local_out, local_grad = (
        lax.all_to_all(queries, "head", split_axis=1, concat_axis=0, tiled=True),
        lax.all_to_all(keys_in, "head", split_axis=1, concat_axis=0, tiled=True),
        lax.all_to_all(values_in, "head", split_axis=1, concat_axis=0, tiled=True),
        lax.all_to_all(attn_out, "head", split_axis=1, concat_axis=0, tiled=True),
        lax.all_to_all(out_grad, "head", split_axis=1, concat_axis=0, tiled=True),
    )
    all_ids = lax.all_gather(span_id, ("ctx", "head"), axis=0, tiled=True)
    seg_rows = local_q.shape[0]
    block_count = lax.axis_size("ctx")
    head_count = log_norm.shape[1]
    head_width = local_q.shape[1] // head_count
    my_block = lax.axis_index("ctx")
    own_ids = lax.dynamic_slice_in_dim(all_ids, my_block * seg_rows, seg_rows)
    id_blocks = all_ids.reshape(block_count, seg_rows)
    deltas = jnp.sum(
        (local_grad.astype(jnp.float32) * local_out.astype(jnp.float32)).reshape(
            seg_rows, head_count, head_width
        ),
        axis=2,
    )
    far_queries, far_grads = (
        lax.all_gather(local_q, "ctx", axis=0, tiled=True),
        lax.all_gather(local_grad, "ctx", axis=0, tiled=True),
    )
    far_norms, far_deltas = (
        lax.all_gather(log_norm, "ctx", axis=0, tiled=True),
        lax.all_gather(deltas, "ctx", axis=0, tiled=True),
    )

    def query_step(totals, piece):
        query_blk, grad_blk, norm_blk, delta_blk, query_ids = piece
        query_term, key_term, value_term = tile_terms(
            query_blk, grad_blk, norm_blk, delta_blk, query_ids, local_k, local_v, own_ids
        )
        return ((totals[0] + rounded(key_term), totals[1] + rounded(value_term)), query_term)

    zero_block = jnp.zeros(local_k.shape, jnp.float32)
    (dk_total, dv_total), query_terms = lax.scan(
        query_step,
        (zero_block, zero_block),
        (
            far_queries.reshape(block_count, seg_rows, -1),
            far_grads.reshape(block_count, seg_rows, -1),
            far_norms.reshape(block_count, seg_rows, -1),
            far_deltas.reshape(block_count, seg_rows, -1),
            id_blocks,
        ),
    )
    query_sum = lax.psum_scatter(
        query_terms.reshape(block_count * seg_rows, -1).astype(jnp.bfloat16),
        "ctx",
        scatter_dimension=0,
        tiled=True,
    )
    dk_local = dk_total.astype(jnp.bfloat16)
    dv_local = dv_total.astype(jnp.bfloat16)
    query_grad, key_grad, value_grad = (
        lax.all_to_all(query_sum, "head", split_axis=0, concat_axis=1, tiled=True),
        lax.all_to_all(dk_local, "head", split_axis=0, concat_axis=1, tiled=True),
        lax.all_to_all(dv_local, "head", split_axis=0, concat_axis=1, tiled=True),
    )
    return (query_grad, key_grad, value_grad)


def nt(a, b):
    return lax.dot_general(a, b, (((1,), (1,)), ((), ())), preferred_element_type=F32)


def tn(a, b):
    return lax.dot_general(a, b, (((0,), (0,)), ((), ())), preferred_element_type=F32)


def pieces(value):
    high = value.astype(BF16)
    rest = value - high.astype(F32)
    middle = rest.astype(BF16)
    low = (rest - middle.astype(F32)).astype(BF16)
    return high, middle, low


def run_copies(pairs, sems, first=0):
    made = [pltpu.make_async_copy(src, dst, sems.at[first + i]) for i, (src, dst) in enumerate(pairs)]
    for copy in made:
        copy.start()
    return made


def wait_all(made):
    for copy in made:
        copy.wait()


def anywhere(count):
    return [pl.BlockSpec(memory_space=pl.ANY)] * count


def pack(queries, keys_in, values_in, attn_out, out_grad, span_row, groups, width):
    rows = queries.shape[0]
    heads = width // LANES
    half = width // 2

    def body(q, k, v, o, g, ids, *refs):
        x1, x2, x3 = refs[:groups], refs[groups : 2 * groups], refs[2 * groups : 3 * groups]
        q_v, k_v, v_v, o_v, g_v, meta, sems = refs[3 * groups :]
        here = lax.axis_index("head")
        low = lax.axis_index("ctx") < 2
        loads = run_copies([(k, k_v), (v, v_v), (q, q_v), (g, g_v), (o, o_v)], sems)

        def moves(first, second, third, fourth, near, far):
            todo = []
            for m in range(groups):
                base = pl.multiple_of((here ^ m) * width, LANES)
                todo.append((first.at[:, pl.ds(base + near, half)], x1[m].at[:, pl.ds(0, half)]))
                todo.append((second.at[:, pl.ds(base + near, half)], x1[m].at[:, pl.ds(half, half)]))
            for m in range(groups):
                base = pl.multiple_of((here ^ m) * width, LANES)
                todo.append((first.at[:, pl.ds(base + far, half)], x2[m].at[:, pl.ds(0, half)]))
                todo.append((second.at[:, pl.ds(base + far, half)], x2[m].at[:, pl.ds(half, half)]))
                todo.append((third.at[:, pl.ds(base, width)], x3[m].at[:, pl.ds(0, width)]))
                todo.append((fourth.at[:, pl.ds(base, width)], x3[m].at[:, pl.ds(width, width)]))
            return [pltpu.make_async_copy(src, dst, sems.at[5 + i]) for i, (src, dst) in enumerate(todo)]

        low_moves = (k_v, v_v, q_v, g_v, half, 0)
        high_moves = (q_v, g_v, k_v, v_v, 0, half)
        wait_all(loads[:4])

        @pl.when(low)
        def _():
            for copy in moves(*low_moves):
                copy.start()

        @pl.when(jnp.logical_not(low))
        def _():
            for copy in moves(*high_moves):
                copy.start()

        wait_all(loads[4:])
        lane = lax.broadcasted_iota(jnp.int32, (rows, LANES), 1)
        slot = jnp.where(lane < 3 * heads, lane % heads, -1)
        at_row = lax.broadcasted_iota(jnp.int32, (rows, rows), 0)
        at_col = lax.broadcasted_iota(jnp.int32, (rows, rows), 1)
        own = jnp.sum(jnp.where(at_row == at_col, ids[...].astype(F32), 0.0), axis=1, keepdims=True)
        for h in range(groups):
            total = jnp.zeros((rows, LANES), F32)
            for c in range(heads):
                cols = pl.ds(h * width + c * LANES, LANES)
                delta = jnp.sum(o_v[:, cols].astype(F32) * g_v[:, cols].astype(F32), axis=1, keepdims=True)
                total = jnp.where(slot == c, delta, total)
            high, middle, lowest = pieces(total)
            kept = jnp.where(lane < heads, high, jnp.where(lane < 2 * heads, middle, lowest))
            meta[h] = jnp.where(lane < 3 * heads, kept, jnp.where(lane == 3 * heads, own.astype(BF16), 0.0).astype(BF16))
        last = run_copies(
            [(meta.at[here ^ m], x1[m].at[:, pl.ds(width, LANES)]) for m in range(groups)], sems, 5 + 6 * groups
        )

        @pl.when(low)
        def _():
            wait_all(moves(*low_moves))

        @pl.when(jnp.logical_not(low))
        def _():
            wait_all(moves(*high_moves))

        wait_all(last)

    whole = pltpu.VMEM((rows, groups * width), BF16)
    made = pl.pallas_call(
        body,
        out_shape=[
            jax.ShapeDtypeStruct((rows, size), BF16)
            for size in (width + LANES, width, 2 * width)
            for _ in range(groups)
        ],
        in_specs=anywhere(5) + [pl.BlockSpec(memory_space=pltpu.VMEM)],
        out_specs=anywhere(3 * groups),
        scratch_shapes=[whole] * 5
        + [pltpu.VMEM((groups, rows, LANES), BF16), pltpu.SemaphoreType.DMA((5 + 7 * groups,))],
        cost_estimate=pl.CostEstimate(flops=0, bytes_accessed=10 * rows * groups * width * 2, transcendentals=0),
        compiler_params=pltpu.CompilerParams(vmem_limit_bytes=VMEM_WHOLE),
        name="pack",
    )(queries, keys_in, values_in, attn_out, out_grad, span_row)
    return made[:groups], made[groups : 2 * groups], made[2 * groups :]


def join_first(parts, norm_rows):
    groups = len(parts)
    rows, width = parts[0].shape
    heads = norm_rows.shape[0]

    def body(*refs):
        norm, y, sems = refs[groups:]
        here = lax.axis_index("head")
        made = run_copies([(refs[m], y.at[here ^ m]) for m in range(groups)], sems)
        at_row = lax.broadcasted_iota(jnp.int32, (heads, LANES), 0)
        at_lane = lax.broadcasted_iota(jnp.int32, (heads, LANES), 1)
        total = jnp.zeros((groups * rows, LANES), F32)
        for i, piece in enumerate(pieces(norm[...])):
            place = jnp.where(at_lane == at_row + (3 * heads + 1 + i * heads), 1.0, 0.0).astype(BF16)
            total += tn(piece, place)
        wait_all(made)
        tail = pl.ds(width - LANES, LANES)
        for h in range(groups):
            y[h, :, tail] = (y[h, :, tail].astype(F32) + total[h * rows : (h + 1) * rows]).astype(BF16)

    return pl.pallas_call(
        body,
        out_shape=jax.ShapeDtypeStruct((groups, rows, width), BF16),
        in_specs=anywhere(groups) + [pl.BlockSpec(memory_space=pltpu.VMEM)],
        out_specs=pl.BlockSpec(memory_space=pltpu.VMEM),
        scratch_shapes=[pltpu.SemaphoreType.DMA((groups,))],
        cost_estimate=pl.CostEstimate(flops=0, bytes_accessed=4 * groups * rows * width, transcendentals=0),
        compiler_params=pltpu.CompilerParams(vmem_limit_bytes=VMEM_SMALL),
        name="join_first",
    )(*parts, norm_rows).reshape(groups * rows, width)


def join(parts):
    groups = len(parts)
    rows, width = parts[0].shape

    def body(*refs):
        y, sems = refs[groups:]
        here = lax.axis_index("head")
        wait_all(run_copies([(refs[m], y.at[here ^ m]) for m in range(groups)], sems))

    return pl.pallas_call(
        body,
        out_shape=jax.ShapeDtypeStruct((groups, rows, width), BF16),
        in_specs=anywhere(groups),
        out_specs=pl.BlockSpec(memory_space=pltpu.VMEM),
        scratch_shapes=[pltpu.SemaphoreType.DMA((groups,))],
        cost_estimate=pl.CostEstimate(flops=0, bytes_accessed=4 * groups * rows * width, transcendentals=0),
        compiler_params=pltpu.CompilerParams(vmem_limit_bytes=VMEM_SMALL),
        name="join",
    )(*parts).reshape(groups * rows, width)


def token_rows(meta, heads):
    at_row = lax.broadcasted_iota(jnp.int32, (32, LANES), 0)
    at_lane = lax.broadcasted_iota(jnp.int32, (32, LANES), 1)
    norm_lane = at_lane - (3 * heads + 1)
    is_norm = (norm_lane >= 0) & (norm_lane < 3 * heads) & (norm_lane % heads == at_row) & (at_row < heads)
    is_delta = (at_lane < 3 * heads) & (at_lane % heads == at_row - heads) & (at_row >= heads)
    is_id = (at_lane == 3 * heads) & (at_row == 2 * heads)
    chosen = jnp.where(is_norm | is_delta | is_id, 1.0, 0.0).astype(BF16)
    return nt(chosen, meta)


def pair_terms(query, grad, key, value, norm, delta, visible=None):
    scale = 1.0 / math.sqrt(query.shape[1])
    weight = jnp.exp(nt(key, query) * scale - norm)
    if visible is not None:
        weight = jnp.where(visible, weight, 0.0)
    dscore = (weight * (nt(value, grad) - delta) * scale).astype(BF16)
    value_term = jnp.dot(weight.astype(BF16), grad, preferred_element_type=F32)
    key_term = jnp.dot(dscore, query, preferred_element_type=F32)
    query_term = tn(dscore, key)
    return query_term, key_term, value_term


def join_last(parts, y1, y2):
    groups = len(parts)
    share = parts[0].shape[0]
    rows, width = y2.shape
    half = width // 2

    def body(*refs):
        y1, y2, w, pairs, swap, kedge, qedge, sems = refs[groups:]
        here, low = lax.axis_index("head"), lax.axis_index("ctx") < 2
        top, bottom, tail = pl.ds(0, EDGE), pl.ds(rows - EDGE, EDGE), pl.ds(width, LANES)
        whole, end = pl.ds(0, 2 * width), pl.ds(2 * width, LANES)
        made = run_copies([(y1.at[top, tail], kedge.at[:, end]), (y1.at[bottom, tail], qedge.at[:, end])], sems)
        loads = run_copies([(refs[m], w.at[here ^ m]) for m in range(groups)], sems, 2)

        def joined(first, second, at, edge):
            todo = []
            for i in range(2):
                for j, part in enumerate((first, second)):
                    todo.append((part.at[at, pl.ds(i * half, half)], edge.at[:, pl.ds(i * width + j * half, half)]))
            return todo

        @pl.when(low)
        def _():
            wait_all(run_copies(joined(y2, y1, top, kedge), sems, 2 + groups))

        @pl.when(jnp.logical_not(low))
        def _():
            wait_all(run_copies(joined(y1, y2, bottom, qedge), sems, 2 + groups))

        wait_all(loads)

        @pl.when(low)
        def _():
            qedge[:, whole] = w[groups - 1, share - EDGE :, :]

        @pl.when(jnp.logical_not(low))
        def _():
            kedge[:, whole] = w[0, :EDGE, :]

        wait_all(made)
        even = lax.axis_index("ctx") % 2 == 0
        pairs[...] = jnp.where(even, qedge[...], kedge[...])
        swap[...] = jnp.where(even, kedge[...], qedge[...])

    edge = jax.ShapeDtypeStruct((EDGE, 2 * width + LANES), BF16)
    w, for_pairs, for_swap = pl.pallas_call(
        body,
        out_shape=[jax.ShapeDtypeStruct((groups, share, 2 * width), BF16), edge, edge],
        in_specs=anywhere(groups + 2),
        out_specs=[pl.BlockSpec(memory_space=pltpu.VMEM)] * 3,
        scratch_shapes=[pltpu.VMEM(edge.shape, BF16)] * 2 + [pltpu.SemaphoreType.DMA((6 + groups,))],
        compiler_params=pltpu.CompilerParams(vmem_limit_bytes=VMEM_SMALL),
        cost_estimate=pl.CostEstimate(flops=0, bytes_accessed=8 * rows * width, transcendentals=0),
        name="join_last",
    )(*parts, y1, y2)
    return w.reshape(rows, 2 * width), for_pairs, for_swap


def in_vmem(count):
    return [pl.BlockSpec(memory_space=pltpu.VMEM)] * count


def both(ref, at, gap):
    return lambda c: (
        ref[:, at + c * LANES : at + (c + 1) * LANES],
        ref[:, at + gap + c * LANES : at + gap + (c + 1) * LANES],
    )


def put(ref, at, value):
    ref[:, at : at + LANES] = value.astype(BF16)


def far_early(y1, y2, w, r1, s1):
    rows, width = y2.shape
    half = width // 2
    count = half // LANES
    heads = 2 * count

    def body(y1, y2, w, r1, s1, pq, pk, lo, l3, info):
        z = lax.axis_index("ctx")
        tail = pl.ds(width, LANES)

        def scalars(slot, head):
            return info[slot, head : head + 1, :], info[slot, heads + head : heads + head + 1, :]

        @pl.when(z == 1)
        def _():
            info[0] = token_rows(s1[:, tail], heads)
            info[1] = token_rows(y1[:, tail], heads)
            for c in range(count):
                a, b = c * LANES, half + c * LANES
                made = pair_terms(*both(s1, 0, half)(c), *both(y2, 0, half)(c), *scalars(0, c))
                own = pair_terms(*both(w, half, width)(c), *both(r1, 0, half)(c), *scalars(1, count + c))
                for ref, at, value in ((pq, a, made[0]), (pk, a, made[1]), (pk, b, made[2])):
                    put(ref, at, value)
                for ref, at, value in ((lo, a, own[0]), (l3, a, own[1]), (l3, b, own[2])):
                    put(ref, at, value)

        @pl.when(z == 2)
        def _():
            info[0] = token_rows(y1[:, tail], heads)
            info[1] = token_rows(r1[:, tail], heads)
            for c in range(count):
                a, b = c * LANES, half + c * LANES
                made = pair_terms(*both(y2, 0, half)(c), *both(s1, 0, half)(c), *scalars(0, count + c))
                own = pair_terms(*both(r1, 0, half)(c), *both(w, 0, width)(c), *scalars(1, c))
                for ref, at, value in ((pq, a, made[0]), (pk, a, made[1]), (pk, b, made[2])):
                    put(ref, at, value)
                for ref, at, value in ((l3, a, own[0]), (lo, a, own[1]), (lo, b, own[2])):
                    put(ref, at, value)

    single = jax.ShapeDtypeStruct((rows, width), BF16)
    return pl.pallas_call(
        body,
        out_shape=[jax.ShapeDtypeStruct((rows, half), BF16), single, single, single],
        in_specs=in_vmem(5),
        out_specs=in_vmem(4),
        scratch_shapes=[pltpu.VMEM((2, 32, rows), F32)],
        compiler_params=pltpu.CompilerParams(vmem_limit_bytes=VMEM_LIMIT),
        cost_estimate=pl.CostEstimate(
            flops=10 * 10 * rows * rows * LANES, bytes_accessed=10 * rows * width, transcendentals=10 * rows * rows
        ),
        name="far_early",
    )(y1, y2, w, r1, s1)


def far_pairs(y1, y2, w, r1, r2, s1, s2, pq, pk):
    rows, width = y2.shape
    half = width // 2
    count = half // LANES
    heads = 2 * count

    def body(y1, y2, w, r1, r2, s1, s2, pq, pk, swap1, out1, swap2, la, l2, info):
        z = lax.axis_index("ctx")
        tail = pl.ds(width, LANES)

        def scalars(slot, head):
            return info[slot, head : head + 1, :], info[slot, heads + head : heads + head + 1, :]

        def before(ref, at):
            return ref[:, at : at + LANES].astype(F32)

        def corner(query_2, query_3, key_0, key_1, c, head):
            first, other = both(key_0, 0, half)(c), both(key_1, 0, half)(c)
            key, value = (jnp.concatenate(x, axis=0) for x in zip(first, other))
            third = pair_terms(*both(query_3, 0, half)(c), key, value, *scalars(1, head))
            second = pair_terms(*both(query_2, 0, half)(c), *first, *scalars(0, head))
            key_1_terms = third[1][rows:] + before(pk, c * LANES), third[2][rows:] + before(pk, half + c * LANES)
            key_0_terms = third[1][:rows] + second[1], third[2][:rows] + second[2]
            return second[0] + before(pq, c * LANES), third[0], key_0_terms, key_1_terms

        @pl.when(z == 1)
        def _():
            for slot, ref in enumerate((s1, s2, y1)):
                info[slot] = token_rows(ref[:, tail], heads)
            for c in range(count):
                a, b = c * LANES, half + c * LANES
                own = pair_terms(*both(w, 0, width)(c), *both(r2, 0, half)(c), *scalars(2, c))
                query_2, query_3, key_0, key_1 = corner(s1, s2, r2, y2, c, c)
                put(swap1, a, query_3)
                put(swap2, a, query_2)
                put(out1, a, key_0[0] + own[1])
                put(out1, b, key_0[1] + own[2])
                put(l2, a, key_1[0])
                put(l2, b, key_1[1])
                put(la, a, own[0])

        @pl.when(z == 2)
        def _():
            for slot, ref in enumerate((y1, r1)):
                info[slot] = token_rows(ref[:, tail], heads)
            for c in range(count):
                a, b = c * LANES, half + c * LANES
                own = pair_terms(*both(r2, 0, half)(c), *both(w, half, width)(c), *scalars(1, count + c))
                query_2, query_3, key_0, key_1 = corner(y2, r2, s2, s1, c, count + c)
                put(swap1, a, key_0[0])
                put(swap1, b, key_0[1])
                put(swap2, a, key_1[0])
                put(swap2, b, key_1[1])
                put(out1, a, query_3 + own[0])
                put(l2, a, query_2)
                put(la, a, own[1])
                put(la, b, own[2])

    single = jax.ShapeDtypeStruct((rows, width), BF16)
    return pl.pallas_call(
        body,
        out_shape=[single] * 5,
        in_specs=in_vmem(9),
        out_specs=in_vmem(5),
        scratch_shapes=[pltpu.VMEM((3, 32, rows), F32)],
        compiler_params=pltpu.CompilerParams(vmem_limit_bytes=VMEM_LIMIT),
        cost_estimate=pl.CostEstimate(
            flops=20 * 10 * rows * rows * LANES, bytes_accessed=30 * rows * width, transcendentals=20 * rows * rows
        ),
        name="far_pairs",
    )(y1, y2, w, r1, r2, s1, s2, pq, pk)


def near_pairs(y1, y2, w, from_pair, from_swap):
    rows, width = y2.shape
    half = width // 2
    count = half // LANES
    heads = 2 * count
    total = rows + EDGE

    def body(y1, y2, w, from_pair, from_swap, dw, dy1, dy2, to_pair, to_swap, info):
        z = lax.axis_index("ctx")
        even = z % 2 == 0

        def edge_part(at):
            pair, swap = from_pair[:, at : at + LANES], from_swap[:, at : at + LANES]
            return jnp.where(even, pair, swap), jnp.where(even, swap, pair)

        tail = pl.ds(width, LANES)
        key_tail, query_tail = edge_part(2 * width)
        info[...] = token_rows(jnp.concatenate([y1[:, tail], query_tail], axis=0), heads)
        key_meta = jnp.concatenate([y1[:, tail], key_tail], axis=0).astype(F32)
        id_lane = lax.broadcasted_iota(jnp.int32, (total, LANES), 1) == 3 * heads
        key_ids = jnp.sum(jnp.where(id_lane, key_meta, 0.0), axis=1, keepdims=True)
        at_key = lax.broadcasted_iota(jnp.int32, (total, total), 0)
        at_query = lax.broadcasted_iota(jnp.int32, (total, total), 1)
        last_key = jnp.where(z < 3, total, rows)
        last_query = jnp.where(z > 0, total, rows)
        visible = (key_ids <= info[2 * heads : 2 * heads + 1, :]) & ((at_key < rows) | (at_query < rows - EDGE))
        visible = visible & (at_key < last_key) & (at_query < last_query)

        def head_terms(i, c, payload):
            a, b = i * half + c * LANES, width + i * half + c * LANES
            small, large = c * LANES, half + c * LANES
            wide = w[:, a : a + LANES], w[:, b : b + LANES]
            narrow = payload[:, small : small + LANES], payload[:, large : large + LANES]
            edge_k, edge_q = zip(edge_part(a), edge_part(b))

            def terms(queries, keys):
                query, grad = (jnp.concatenate(x, axis=0) for x in zip(queries, edge_q))
                key, value = (jnp.concatenate(x, axis=0) for x in zip(keys, edge_k))
                scalars = info[i * count + c : i * count + c + 1, :], info[heads + i * count + c : heads + i * count + c + 1, :]
                made = [x.astype(BF16) for x in pair_terms(query, grad, key, value, *scalars, visible)]
                query_end, key_end, value_end = (x[rows:] for x in made)
                to_pair[:, a : a + LANES] = jnp.where(even, key_end, query_end)
                to_swap[:, a : a + LANES] = jnp.where(even, query_end, key_end)
                to_pair[:, b : b + LANES] = value_end
                to_swap[:, b : b + LANES] = value_end
                return [x[:rows] for x in made]

            return a, b, small, large, wide, narrow, terms

        @pl.when(z < 2)
        def _():
            for i, (payload, result) in enumerate(((y2, dy2), (y1, dy1))):
                for c in range(count):
                    a, b, small, large, wide, narrow, terms = head_terms(i, c, payload)
                    query_term, key_term, value_term = terms(wide, narrow)
                    dw[:, a : a + LANES] = query_term
                    result[:, small : small + LANES] = key_term
                    result[:, large : large + LANES] = value_term

        @pl.when(z >= 2)
        def _():
            for i, (payload, result) in enumerate(((y1, dy1), (y2, dy2))):
                for c in range(count):
                    a, b, small, large, wide, narrow, terms = head_terms(i, c, payload)
                    query_term, key_term, value_term = terms(narrow, wide)
                    result[:, small : small + LANES] = query_term
                    dw[:, a : a + LANES] = key_term
                    dw[:, b : b + LANES] = value_term

    return pl.pallas_call(
        body,
        out_shape=[
            jax.ShapeDtypeStruct((rows, 2 * width), BF16),
            jax.ShapeDtypeStruct((rows, width), BF16),
            jax.ShapeDtypeStruct((rows, width), BF16),
            jax.ShapeDtypeStruct((EDGE, 2 * width), BF16),
            jax.ShapeDtypeStruct((EDGE, 2 * width), BF16),
        ],
        in_specs=in_vmem(5),
        out_specs=in_vmem(5),
        scratch_shapes=[pltpu.VMEM((32, total), F32)],
        compiler_params=pltpu.CompilerParams(vmem_limit_bytes=VMEM_LIMIT),
        cost_estimate=pl.CostEstimate(
            flops=10 * 10 * rows * rows * LANES, bytes_accessed=16 * rows * width, transcendentals=10 * rows * rows
        ),
        name="near_pairs",
    )(y1, y2, w, from_pair, from_swap)


def finish_first(dw, la, lo, dy2, l2, out1, from_pair, from_swap, groups):
    rows, width = dy2.shape
    half = width // 2
    share = rows // groups

    def body(dw, la, lo, dy2, l2, out1, dp, ds, *refs):
        outs, v, e, sems = refs[:groups], *refs[groups:]
        here = lax.axis_index("head")
        z = lax.axis_index("ctx")
        low, middle = z < 2, (z == 1) | (z == 2)
        after_first, before_last, odd = z > 0, z < 3, z % 2 == 1

        def own(i):
            at, there = pl.ds(i * half, half), pl.ds(i // 2 * half, half)
            active, other = la[:, there].astype(F32), lo[:, there].astype(F32)
            one, two = (active, other) if i % 2 == 0 else (other, active)
            return dw[:, at].astype(F32) + jnp.where(middle, jnp.where(z == 1, one, two), 0.0)

        def second(cols):
            return dy2[:, cols].astype(F32) + jnp.where(middle, l2[:, cols], out1[:, cols]).astype(F32)

        def put(dst, cols, total, first, last=None):
            end = total[rows - EDGE :] if last is None else total[rows - EDGE :] + last
            total = jnp.concatenate([total[:EDGE] + first, total[EDGE : rows - EDGE], end], axis=0)
            for h in range(groups):
                dst[h, :, cols] = total[h * share : (h + 1) * share].astype(BF16)

        def key_edge(cols):
            return jnp.where(after_first, jnp.where(odd, dp[:, cols], ds[:, cols]).astype(F32), 0.0)

        def query_edge(cols):
            return jnp.where(before_last, jnp.where(odd, ds[:, cols], dp[:, cols]).astype(F32), 0.0)

        a, b = pl.ds(0, half), pl.ds(half, half)
        c, d = pl.ds(width, half), pl.ds(width + half, half)
        for i, cols in enumerate((a, b)):
            put(e, cols, own(i), jnp.where(low, 0.0, key_edge(cols)), jnp.where(low, query_edge(cols), 0.0))
        put(e, c, second(a), jnp.where(low, key_edge(a), 0.0), jnp.where(low, 0.0, query_edge(b)))
        put(e, d, jnp.where(low, second(b), own(2)), key_edge(c))
        made = run_copies([(e.at[here ^ m], outs[m]) for m in range(groups)], sems)
        left_over = own(3)
        left_over = jnp.concatenate([left_over[:EDGE] + key_edge(d), left_over[EDGE:]], axis=0)
        v[...] = left_over.astype(BF16)
        wait_all(made)

    return pl.pallas_call(
        body,
        out_shape=[jax.ShapeDtypeStruct((share, 2 * width), BF16)] * groups + [jax.ShapeDtypeStruct((rows, half), BF16)],
        in_specs=in_vmem(8),
        out_specs=anywhere(groups) + [pl.BlockSpec(memory_space=pltpu.VMEM)],
        scratch_shapes=[pltpu.VMEM((groups, share, 2 * width), BF16), pltpu.SemaphoreType.DMA((groups,))],
        compiler_params=pltpu.CompilerParams(vmem_limit_bytes=VMEM_SMALL),
        cost_estimate=pl.CostEstimate(flops=0, bytes_accessed=16 * rows * width, transcendentals=0),
        name="finish_first",
    )(dw, la, lo, dy2, l2, out1, from_pair, from_swap)


def finish_second(dy1, swap2, out2, v, from_pair, from_swap, groups):
    rows, width = dy1.shape
    half = width // 2
    share = rows // groups

    def body(dy1, swap2, out2, v, dp, ds, *refs):
        outs, e, sems = refs[:groups], *refs[groups:]
        here, z = lax.axis_index("head"), lax.axis_index("ctx")
        low, middle = z < 2, (z == 1) | (z == 2)

        def put(cols, whole):
            for h in range(groups):
                e[h, :, cols] = whole[h * share : (h + 1) * share].astype(BF16)

        a, b = pl.ds(0, half), pl.ds(half, half)
        end = pl.ds(width + half, half)

        def total(cols):
            return dy1[:, cols].astype(F32) + jnp.where(middle, swap2[:, cols], out2[:, cols]).astype(F32)

        left = total(a)
        first = left[:EDGE] + jnp.where(z == 1, dp[:, b].astype(F32), 0.0)
        last = left[rows - EDGE :] + jnp.where(z == 2, dp[:, a].astype(F32), 0.0)
        put(a, jnp.concatenate([first, left[EDGE : rows - EDGE], last], axis=0))
        right = total(b)
        right = jnp.concatenate([right[:EDGE] + jnp.where(z == 1, dp[:, end].astype(F32), 0.0), right[EDGE:]], axis=0)
        put(b, jnp.where(low, right, v[...].astype(F32)))
        wait_all(run_copies([(e.at[here ^ m], outs[m]) for m in range(groups)], sems))

    return pl.pallas_call(
        body,
        out_shape=[jax.ShapeDtypeStruct((share, width), BF16)] * groups,
        in_specs=[pl.BlockSpec(memory_space=pltpu.VMEM)] * 6,
        out_specs=anywhere(groups),
        scratch_shapes=[pltpu.VMEM((groups, share, width), BF16), pltpu.SemaphoreType.DMA((groups,))],
        compiler_params=pltpu.CompilerParams(vmem_limit_bytes=VMEM_SMALL),
        cost_estimate=pl.CostEstimate(flops=0, bytes_accessed=9 * rows * width, transcendentals=0),
        name="finish_second",
    )(dy1, swap2, out2, v, from_pair, from_swap)


def unpack_early(parts):
    groups = len(parts)
    rows = parts[0].shape[0]
    width = parts[0].shape[1] // 2
    half = width // 2

    def body(*refs):
        dq, dk, dv, first, second, third, sems = refs[groups:]
        here, low = lax.axis_index("head"), lax.axis_index("ctx") < 2
        todo = []
        for m in range(groups):
            base = pl.multiple_of((here ^ m) * width, LANES)
            place = pl.multiple_of(base + jnp.where(low, 0, half), LANES)
            todo.append((refs[m].at[:, pl.ds(0, width)], first.at[:, pl.ds(base, width)]))
            todo.append((refs[m].at[:, pl.ds(width, half)], second.at[:, pl.ds(place, half)]))
            todo.append((refs[m].at[:, pl.ds(width + half, half)], third.at[:, pl.ds(base, half)]))
        wait_all(run_copies(todo, sems))

        @pl.when(low)
        def _():
            wait_all(run_copies([(first, dq), (second, dk), (third, dv)], sems))

        @pl.when(jnp.logical_not(low))
        def _():
            wait_all(run_copies([(first, dk), (second, dq), (third, dv)], sems))

    shape = jax.ShapeDtypeStruct((rows, groups * width), BF16)
    return pl.pallas_call(
        body,
        out_shape=[shape] * 3,
        in_specs=anywhere(groups),
        out_specs=anywhere(3),
        scratch_shapes=[pltpu.VMEM(shape.shape, BF16)] * 3 + [pltpu.SemaphoreType.DMA((3 * groups,))],
        cost_estimate=pl.CostEstimate(flops=0, bytes_accessed=10 * rows * groups * width, transcendentals=0),
        compiler_params=pltpu.CompilerParams(vmem_limit_bytes=VMEM_SMALL),
        name="unpack_early",
    )(*parts)


def unpack_late(parts, dq, dk, dv):
    groups = len(parts)
    rows, width = parts[0].shape
    half = width // 2

    def body(*refs):
        dq, dk, dv, held, sems = refs[groups + 3 :]
        here, low = lax.axis_index("head"), lax.axis_index("ctx") < 2
        loads = run_copies([(refs[m], held.at[m]) for m in range(groups)], sems)

        def moves(far, near):
            todo = []
            for m in range(groups):
                base = pl.multiple_of((here ^ m) * width, LANES)
                todo.append((held.at[m, :, pl.ds(0, half)], far.at[:, pl.ds(base + near, half)]))
                todo.append((held.at[m, :, pl.ds(half, half)], dv.at[:, pl.ds(base + half, half)]))
            return todo

        wait_all(loads)

        @pl.when(low)
        def _():
            wait_all(run_copies(moves(dk, half), sems))

        @pl.when(jnp.logical_not(low))
        def _():
            wait_all(run_copies(moves(dq, 0), sems))

    shape = jax.ShapeDtypeStruct(dq.shape, BF16)
    return pl.pallas_call(
        body,
        out_shape=[shape] * 3,
        in_specs=anywhere(groups + 3),
        out_specs=anywhere(3),
        scratch_shapes=[pltpu.VMEM((groups, rows, width), BF16), pltpu.SemaphoreType.DMA((2 * groups,))],
        input_output_aliases={groups: 0, groups + 1: 1, groups + 2: 2},
        compiler_params=pltpu.CompilerParams(vmem_limit_bytes=VMEM_SMALL),
        cost_estimate=pl.CostEstimate(flops=0, bytes_accessed=8 * rows * groups * width, transcendentals=0),
        name="unpack_late",
    )(*parts, dq, dk, dv)


def after(array, other):
    return lax.optimization_barrier((array, other))[0]


def local_split(queries, keys_in, values_in, attn_out, out_grad, log_norm, span_id):
    groups = lax.axis_size("head")
    width = queries.shape[1] // groups

    def swapped(parts):
        return [parts[0]] + [
            lax.ppermute(parts[m], "head", [(i, i ^ m) for i in range(groups)]) for m in range(1, groups)
        ]

    x1, x2, x3 = pack(queries, keys_in, values_in, attn_out, out_grad, span_id.reshape(1, -1), groups, width)
    x1, x2 = swapped(x1), swapped(x2)
    y1 = join_first(x1, log_norm.T)
    y1, x2[1], x2[2] = lax.optimization_barrier((y1, x2[1], x2[2]))
    r1 = lax.ppermute(y1, "ctx", PAIRS)
    s1 = lax.ppermute(y1, "ctx", SWAP)
    x3 = swapped(x3)
    y2 = join(x2)
    y2, r1, s1, x3[:-1] = lax.optimization_barrier((y2, r1, s1, x3[:-1]))
    r2 = lax.ppermute(y2, "ctx", PAIRS)
    s2 = lax.ppermute(r1, "ctx", SWAP)
    w, from_pair, from_swap = join_last(x3, y1, y2)
    from_pair = lax.ppermute(from_pair, "ctx", PAIRS)
    from_swap = lax.ppermute(from_swap, "ctx", SWAP)
    pq, pk, lo, l3 = far_early(y1, y2, w, r1, s1)
    w, from_pair, from_swap = lax.optimization_barrier((w, from_pair, from_swap))
    swap1, out1, swap2, la, l2 = far_pairs(y1, y2, w, r1, r2, s1, s2, pq, pk)
    dw, dy1, dy2, to_pair, to_swap = near_pairs(y1, y2, w, after(from_pair, l2), from_swap)
    swap1 = lax.ppermute(swap1, "ctx", SWAP)
    out1 = lax.ppermute(out1, "ctx", PAIRS)
    to_pair = lax.ppermute(to_pair, "ctx", PAIRS)
    to_swap = lax.ppermute(to_swap, "ctx", SWAP)
    swap1, swap2, out1, to_pair, to_swap = lax.optimization_barrier((swap1, swap2, out1, to_pair, to_swap))
    swap2 = lax.ppermute(swap2, "ctx", SWAP)
    out2 = lax.ppermute((swap1.astype(F32) + l3.astype(F32)).astype(BF16), "ctx", PAIRS)
    *early, kept = finish_first(dw, la, lo, dy2, l2, out1, to_pair, to_swap, groups)
    early = swapped(early)
    late = swapped(finish_second(dy1, swap2, out2, kept, to_pair, to_swap, groups))
    return tuple(unpack_late(late, *unpack_early(early)))


def splits(tokens, blocks, head_width, heads):
    if blocks != 4 or heads % 2 or head_width != LANES or 6 * heads + 1 > LANES:
        return False
    block = tokens // blocks
    span = -(-tokens // SPANS)
    for offset in range(SPANS * span - tokens + 1):
        for end in range(block, tokens, block):
            start = (end - 1 + offset) // span * span - offset
            if min(end - start, start + span - end) > EDGE or max(end - start, span) > block:
                return False
    return block % EDGE == 0


def local(queries, keys_in, values_in, attn_out, out_grad, log_norm, span_id):
    blocks, groups = lax.axis_size("ctx"), lax.axis_size("head")
    heads = log_norm.shape[1]
    tokens = queries.shape[0] * blocks * groups
    plan = local_plain
    if groups & (groups - 1) == 0 and splits(tokens, blocks, queries.shape[1] // (heads * groups), heads):
        plan = local_split
    return plan(queries, keys_in, values_in, attn_out, out_grad, log_norm, span_id)


def solution(mesh):
    placed = (
        P(("clip", "ctx", "head"), None),
        P(("clip", "ctx", "head"), None),
        P(("clip", "ctx", "head"), None),
        P(("clip", "ctx", "head"), None),
        P(("clip", "ctx", "head"), None),
        P(("clip", "ctx"), "head"),
        P(("clip", "ctx", "head")),
    )
    return jax.shard_map(
        local,
        mesh=mesh,
        in_specs=placed,
        out_specs=(
            P(("clip", "ctx", "head"), None),
            P(("clip", "ctx", "head"), None),
            P(("clip", "ctx", "head"), None),
        ),
        check_vma=False,
    )
```

```python
import math

import jax
import jax.numpy as jnp
from jax import lax
from jax.experimental import pallas as pl
from jax.experimental.pallas import tpu as pltpu
from jax.sharding import PartitionSpec as P

SPANS = 12
EDGE = 16
VMEM_LIMIT = 32 * 2**20
VMEM_SMALL = 16 * 2**20
VMEM_WHOLE = 60 * 2**20
LANES = 128
BF16 = jnp.bfloat16
F32 = jnp.float32

PAIRS = ((0, 1), (1, 0), (2, 3), (3, 2))
SWAP = ((1, 2), (2, 1))


def tile_terms(query_blk, grad_blk, norm_blk, delta_blk, query_ids, key_blk, value_blk, key_ids):
    row_count = query_blk.shape[0]
    key_count = key_blk.shape[0]
    head_count = norm_blk.shape[1]
    head_width = query_blk.shape[1] // head_count
    scale = 1.0 / math.sqrt(head_width)
    query3 = query_blk.reshape(row_count, head_count, head_width)
    grad3 = grad_blk.reshape(row_count, head_count, head_width)
    key3 = key_blk.reshape(key_count, head_count, head_width)
    value3 = value_blk.reshape(key_count, head_count, head_width)
    scores = jnp.einsum("rhd,khd->hrk", query3, key3, preferred_element_type=jnp.float32)
    visible = key_ids[None, :] <= query_ids[:, None]
    weight = jnp.where(visible[None], jnp.exp(scores * scale - norm_blk.T[:, :, None]), 0.0)
    weight_low = weight.astype(jnp.bfloat16)
    dweight = jnp.einsum("rhd,khd->hrk", grad3, value3, preferred_element_type=jnp.float32)
    dscore = (weight * (dweight - delta_blk.T[:, :, None]) * scale).astype(jnp.bfloat16)
    query_term = jnp.einsum("hrk,khd->rhd", dscore, key3, preferred_element_type=jnp.float32)
    key_term = jnp.einsum("hrk,rhd->khd", dscore, query3, preferred_element_type=jnp.float32)
    value_term = jnp.einsum("hrk,rhd->khd", weight_low, grad3, preferred_element_type=jnp.float32)
    return (
        query_term.reshape(row_count, -1),
        key_term.reshape(key_count, -1),
        value_term.reshape(key_count, -1),
    )


def rounded(term):
    return lax.optimization_barrier(term.astype(jnp.bfloat16)).astype(jnp.float32)


def local_plain(queries, keys_in, values_in, attn_out, out_grad, log_norm, span_id):
    local_q, local_k, local_v, local_out, local_grad = (
        lax.all_to_all(queries, "head", split_axis=1, concat_axis=0, tiled=True),
        lax.all_to_all(keys_in, "head", split_axis=1, concat_axis=0, tiled=True),
        lax.all_to_all(values_in, "head", split_axis=1, concat_axis=0, tiled=True),
        lax.all_to_all(attn_out, "head", split_axis=1, concat_axis=0, tiled=True),
        lax.all_to_all(out_grad, "head", split_axis=1, concat_axis=0, tiled=True),
    )
    all_ids = lax.all_gather(span_id, ("ctx", "head"), axis=0, tiled=True)
    seg_rows = local_q.shape[0]
    block_count = lax.axis_size("ctx")
    head_count = log_norm.shape[1]
    head_width = local_q.shape[1] // head_count
    my_block = lax.axis_index("ctx")
    own_ids = lax.dynamic_slice_in_dim(all_ids, my_block * seg_rows, seg_rows)
    id_blocks = all_ids.reshape(block_count, seg_rows)
    deltas = jnp.sum(
        (local_grad.astype(jnp.float32) * local_out.astype(jnp.float32)).reshape(
            seg_rows, head_count, head_width
        ),
        axis=2,
    )
    far_queries, far_grads = (
        lax.all_gather(local_q, "ctx", axis=0, tiled=True),
        lax.all_gather(local_grad, "ctx", axis=0, tiled=True),
    )
    far_norms, far_deltas = (
        lax.all_gather(log_norm, "ctx", axis=0, tiled=True),
        lax.all_gather(deltas, "ctx", axis=0, tiled=True),
    )

    def query_step(totals, piece):
        query_blk, grad_blk, norm_blk, delta_blk, query_ids = piece
        query_term, key_term, value_term = tile_terms(
            query_blk, grad_blk, norm_blk, delta_blk, query_ids, local_k, local_v, own_ids
        )
        return ((totals[0] + rounded(key_term), totals[1] + rounded(value_term)), query_term)

    zero_block = jnp.zeros(local_k.shape, jnp.float32)
    (dk_total, dv_total), query_terms = lax.scan(
        query_step,
        (zero_block, zero_block),
        (
            far_queries.reshape(block_count, seg_rows, -1),
            far_grads.reshape(block_count, seg_rows, -1),
            far_norms.reshape(block_count, seg_rows, -1),
            far_deltas.reshape(block_count, seg_rows, -1),
            id_blocks,
        ),
    )
    query_sum = lax.psum_scatter(
        query_terms.reshape(block_count * seg_rows, -1).astype(jnp.bfloat16),
        "ctx",
        scatter_dimension=0,
        tiled=True,
    )
    dk_local = dk_total.astype(jnp.bfloat16)
    dv_local = dv_total.astype(jnp.bfloat16)
    query_grad, key_grad, value_grad = (
        lax.all_to_all(query_sum, "head", split_axis=0, concat_axis=1, tiled=True),
        lax.all_to_all(dk_local, "head", split_axis=0, concat_axis=1, tiled=True),
        lax.all_to_all(dv_local, "head", split_axis=0, concat_axis=1, tiled=True),
    )
    return (query_grad, key_grad, value_grad)


def nt(a, b):
    return lax.dot_general(a, b, (((1,), (1,)), ((), ())), preferred_element_type=F32)


def tn(a, b):
    return lax.dot_general(a, b, (((0,), (0,)), ((), ())), preferred_element_type=F32)


def pieces(value):
    high = value.astype(BF16)
    rest = value - high.astype(F32)
    middle = rest.astype(BF16)
    low = (rest - middle.astype(F32)).astype(BF16)
    return high, middle, low


def run_copies(pairs, sems, first=0):
    made = [pltpu.make_async_copy(src, dst, sems.at[first + i]) for i, (src, dst) in enumerate(pairs)]
    for copy in made:
        copy.start()
    return made


def wait_all(made):
    for copy in made:
        copy.wait()


def anywhere(count):
    return [pl.BlockSpec(memory_space=pl.ANY)] * count


def pack(queries, keys_in, values_in, attn_out, out_grad, span_row, groups, width):
    rows = queries.shape[0]
    heads = width // LANES
    half = width // 2

    def body(q, k, v, o, g, ids, *refs):
        x1, x2, x3 = refs[:groups], refs[groups : 2 * groups], refs[2 * groups : 3 * groups]
        q_v, k_v, v_v, o_v, g_v, meta, sems = refs[3 * groups :]
        here = lax.axis_index("head")
        low = lax.axis_index("ctx") < 2
        loads = run_copies([(k, k_v), (v, v_v), (q, q_v), (g, g_v), (o, o_v)], sems)

        def moves(first, second, third, fourth, near, far):
            todo = []
            for m in range(groups):
                base = pl.multiple_of((here ^ m) * width, LANES)
                todo.append((first.at[:, pl.ds(base + near, half)], x1[m].at[:, pl.ds(0, half)]))
                todo.append((second.at[:, pl.ds(base + near, half)], x1[m].at[:, pl.ds(half, half)]))
            for m in range(groups):
                base = pl.multiple_of((here ^ m) * width, LANES)
                todo.append((first.at[:, pl.ds(base + far, half)], x2[m].at[:, pl.ds(0, half)]))
                todo.append((second.at[:, pl.ds(base + far, half)], x2[m].at[:, pl.ds(half, half)]))
                todo.append((third.at[:, pl.ds(base, width)], x3[m].at[:, pl.ds(0, width)]))
                todo.append((fourth.at[:, pl.ds(base, width)], x3[m].at[:, pl.ds(width, width)]))
            return [pltpu.make_async_copy(src, dst, sems.at[5 + i]) for i, (src, dst) in enumerate(todo)]

        low_moves = (k_v, v_v, q_v, g_v, half, 0)
        high_moves = (q_v, g_v, k_v, v_v, 0, half)
        wait_all(loads[:4])

        @pl.when(low)
        def _():
            for copy in moves(*low_moves):
                copy.start()

        @pl.when(jnp.logical_not(low))
        def _():
            for copy in moves(*high_moves):
                copy.start()

        wait_all(loads[4:])
        lane = lax.broadcasted_iota(jnp.int32, (rows, LANES), 1)
        slot = jnp.where(lane < 3 * heads, lane % heads, -1)
        at_row = lax.broadcasted_iota(jnp.int32, (rows, rows), 0)
        at_col = lax.broadcasted_iota(jnp.int32, (rows, rows), 1)
        own = jnp.sum(jnp.where(at_row == at_col, ids[...].astype(F32), 0.0), axis=1, keepdims=True)
        for h in range(groups):
            total = jnp.zeros((rows, LANES), F32)
            for c in range(heads):
                cols = pl.ds(h * width + c * LANES, LANES)
                delta = jnp.sum(o_v[:, cols].astype(F32) * g_v[:, cols].astype(F32), axis=1, keepdims=True)
                total = jnp.where(slot == c, delta, total)
            high, middle, lowest = pieces(total)
            kept = jnp.where(lane < heads, high, jnp.where(lane < 2 * heads, middle, lowest))
            meta[h] = jnp.where(lane < 3 * heads, kept, jnp.where(lane == 3 * heads, own.astype(BF16), 0.0).astype(BF16))
        last = run_copies(
            [(meta.at[here ^ m], x1[m].at[:, pl.ds(width, LANES)]) for m in range(groups)], sems, 5 + 6 * groups
        )

        @pl.when(low)
        def _():
            wait_all(moves(*low_moves))

        @pl.when(jnp.logical_not(low))
        def _():
            wait_all(moves(*high_moves))

        wait_all(last)

    whole = pltpu.VMEM((rows, groups * width), BF16)
    made = pl.pallas_call(
        body,
        out_shape=[
            jax.ShapeDtypeStruct((rows, size), BF16)
            for size in (width + LANES, width, 2 * width)
            for _ in range(groups)
        ],
        in_specs=anywhere(5) + [pl.BlockSpec(memory_space=pltpu.VMEM)],
        out_specs=anywhere(3 * groups),
        scratch_shapes=[whole] * 5
        + [pltpu.VMEM((groups, rows, LANES), BF16), pltpu.SemaphoreType.DMA((5 + 7 * groups,))],
        cost_estimate=pl.CostEstimate(flops=0, bytes_accessed=10 * rows * groups * width * 2, transcendentals=0),
        compiler_params=pltpu.CompilerParams(vmem_limit_bytes=VMEM_WHOLE),
        name="pack",
    )(queries, keys_in, values_in, attn_out, out_grad, span_row)
    return made[:groups], made[groups : 2 * groups], made[2 * groups :]


def join_first(parts, norm_rows):
    groups = len(parts)
    rows, width = parts[0].shape
    heads = norm_rows.shape[0]

    def body(*refs):
        norm, y, sems = refs[groups:]
        here = lax.axis_index("head")
        made = run_copies([(refs[m], y.at[here ^ m]) for m in range(groups)], sems)
        at_row = lax.broadcasted_iota(jnp.int32, (heads, LANES), 0)
        at_lane = lax.broadcasted_iota(jnp.int32, (heads, LANES), 1)
        total = jnp.zeros((groups * rows, LANES), F32)
        for i, piece in enumerate(pieces(norm[...])):
            place = jnp.where(at_lane == at_row + (3 * heads + 1 + i * heads), 1.0, 0.0).astype(BF16)
            total += tn(piece, place)
        wait_all(made)
        tail = pl.ds(width - LANES, LANES)
        for h in range(groups):
            y[h, :, tail] = (y[h, :, tail].astype(F32) + total[h * rows : (h + 1) * rows]).astype(BF16)

    return pl.pallas_call(
        body,
        out_shape=jax.ShapeDtypeStruct((groups, rows, width), BF16),
        in_specs=anywhere(groups) + [pl.BlockSpec(memory_space=pltpu.VMEM)],
        out_specs=pl.BlockSpec(memory_space=pltpu.VMEM),
        scratch_shapes=[pltpu.SemaphoreType.DMA((groups,))],
        cost_estimate=pl.CostEstimate(flops=0, bytes_accessed=4 * groups * rows * width, transcendentals=0),
        compiler_params=pltpu.CompilerParams(vmem_limit_bytes=VMEM_SMALL),
        name="join_first",
    )(*parts, norm_rows).reshape(groups * rows, width)


def join(parts):
    groups = len(parts)
    rows, width = parts[0].shape

    def body(*refs):
        y, sems = refs[groups:]
        here = lax.axis_index("head")
        wait_all(run_copies([(refs[m], y.at[here ^ m]) for m in range(groups)], sems))

    return pl.pallas_call(
        body,
        out_shape=jax.ShapeDtypeStruct((groups, rows, width), BF16),
        in_specs=anywhere(groups),
        out_specs=pl.BlockSpec(memory_space=pltpu.VMEM),
        scratch_shapes=[pltpu.SemaphoreType.DMA((groups,))],
        cost_estimate=pl.CostEstimate(flops=0, bytes_accessed=4 * groups * rows * width, transcendentals=0),
        compiler_params=pltpu.CompilerParams(vmem_limit_bytes=VMEM_SMALL),
        name="join",
    )(*parts).reshape(groups * rows, width)


def token_rows(meta, heads):
    at_row = lax.broadcasted_iota(jnp.int32, (32, LANES), 0)
    at_lane = lax.broadcasted_iota(jnp.int32, (32, LANES), 1)
    norm_lane = at_lane - (3 * heads + 1)
    is_norm = (norm_lane >= 0) & (norm_lane < 3 * heads) & (norm_lane % heads == at_row) & (at_row < heads)
    is_delta = (at_lane < 3 * heads) & (at_lane % heads == at_row - heads) & (at_row >= heads)
    is_id = (at_lane == 3 * heads) & (at_row == 2 * heads)
    chosen = jnp.where(is_norm | is_delta | is_id, 1.0, 0.0).astype(BF16)
    return nt(chosen, meta)


def pair_terms(query, grad, key, value, norm, delta, visible=None):
    scale = 1.0 / math.sqrt(query.shape[1])
    weight = jnp.exp(nt(key, query) * scale - norm)
    if visible is not None:
        weight = jnp.where(visible, weight, 0.0)
    dscore = (weight * (nt(value, grad) - delta) * scale).astype(BF16)
    value_term = jnp.dot(weight.astype(BF16), grad, preferred_element_type=F32)
    key_term = jnp.dot(dscore, query, preferred_element_type=F32)
    query_term = tn(dscore, key)
    return query_term, key_term, value_term


def join_last(parts, y1, y2):
    groups = len(parts)
    share = parts[0].shape[0]
    rows, width = y2.shape
    half = width // 2

    def body(*refs):
        y1, y2, w, pairs, swap, kedge, qedge, sems = refs[groups:]
        here, low = lax.axis_index("head"), lax.axis_index("ctx") < 2
        top, bottom, tail = pl.ds(0, EDGE), pl.ds(rows - EDGE, EDGE), pl.ds(width, LANES)
        whole, end = pl.ds(0, 2 * width), pl.ds(2 * width, LANES)
        made = run_copies([(y1.at[top, tail], kedge.at[:, end]), (y1.at[bottom, tail], qedge.at[:, end])], sems)
        loads = run_copies([(refs[m], w.at[here ^ m]) for m in range(groups)], sems, 2)

        def joined(first, second, at, edge):
            todo = []
            for i in range(2):
                for j, part in enumerate((first, second)):
                    todo.append((part.at[at, pl.ds(i * half, half)], edge.at[:, pl.ds(i * width + j * half, half)]))
            return todo

        @pl.when(low)
        def _():
            wait_all(run_copies(joined(y2, y1, top, kedge), sems, 2 + groups))

        @pl.when(jnp.logical_not(low))
        def _():
            wait_all(run_copies(joined(y1, y2, bottom, qedge), sems, 2 + groups))

        wait_all(loads)

        @pl.when(low)
        def _():
            qedge[:, whole] = w[groups - 1, share - EDGE :, :]

        @pl.when(jnp.logical_not(low))
        def _():
            kedge[:, whole] = w[0, :EDGE, :]

        wait_all(made)
        even = lax.axis_index("ctx") % 2 == 0
        pairs[...] = jnp.where(even, qedge[...], kedge[...])
        swap[...] = jnp.where(even, kedge[...], qedge[...])

    edge = jax.ShapeDtypeStruct((EDGE, 2 * width + LANES), BF16)
    w, for_pairs, for_swap = pl.pallas_call(
        body,
        out_shape=[jax.ShapeDtypeStruct((groups, share, 2 * width), BF16), edge, edge],
        in_specs=anywhere(groups + 2),
        out_specs=[pl.BlockSpec(memory_space=pltpu.VMEM)] * 3,
        scratch_shapes=[pltpu.VMEM(edge.shape, BF16)] * 2 + [pltpu.SemaphoreType.DMA((6 + groups,))],
        compiler_params=pltpu.CompilerParams(vmem_limit_bytes=VMEM_SMALL),
        cost_estimate=pl.CostEstimate(flops=0, bytes_accessed=8 * rows * width, transcendentals=0),
        name="join_last",
    )(*parts, y1, y2)
    return w.reshape(rows, 2 * width), for_pairs, for_swap


def in_vmem(count):
    return [pl.BlockSpec(memory_space=pltpu.VMEM)] * count


def both(ref, at, gap):
    return lambda c: (
        ref[:, at + c * LANES : at + (c + 1) * LANES],
        ref[:, at + gap + c * LANES : at + gap + (c + 1) * LANES],
    )


def put(ref, at, value):
    ref[:, at : at + LANES] = value.astype(BF16)


def far_early(y1, y2, w, r1, s1):
    rows, width = y2.shape
    half = width // 2
    count = half // LANES
    heads = 2 * count

    def body(y1, y2, w, r1, s1, pq, pk, lo, l3, info):
        z = lax.axis_index("ctx")
        tail = pl.ds(width, LANES)

        def scalars(slot, head):
            return info[slot, head : head + 1, :], info[slot, heads + head : heads + head + 1, :]

        @pl.when(z == 1)
        def _():
            info[0] = token_rows(s1[:, tail], heads)
            info[1] = token_rows(y1[:, tail], heads)
            for c in range(count):
                a, b = c * LANES, half + c * LANES
                made = pair_terms(*both(s1, 0, half)(c), *both(y2, 0, half)(c), *scalars(0, c))
                own = pair_terms(*both(w, half, width)(c), *both(r1, 0, half)(c), *scalars(1, count + c))
                for ref, at, value in ((pq, a, made[0]), (pk, a, made[1]), (pk, b, made[2])):
                    put(ref, at, value)
                for ref, at, value in ((lo, a, own[0]), (l3, a, own[1]), (l3, b, own[2])):
                    put(ref, at, value)

        @pl.when(z == 2)
        def _():
            info[0] = token_rows(y1[:, tail], heads)
            info[1] = token_rows(r1[:, tail], heads)
            for c in range(count):
                a, b = c * LANES, half + c * LANES
                made = pair_terms(*both(y2, 0, half)(c), *both(s1, 0, half)(c), *scalars(0, count + c))
                own = pair_terms(*both(r1, 0, half)(c), *both(w, 0, width)(c), *scalars(1, c))
                for ref, at, value in ((pq, a, made[0]), (pk, a, made[1]), (pk, b, made[2])):
                    put(ref, at, value)
                for ref, at, value in ((l3, a, own[0]), (lo, a, own[1]), (lo, b, own[2])):
                    put(ref, at, value)

    single = jax.ShapeDtypeStruct((rows, width), BF16)
    return pl.pallas_call(
        body,
        out_shape=[jax.ShapeDtypeStruct((rows, half), BF16), single, single, single],
        in_specs=in_vmem(5),
        out_specs=in_vmem(4),
        scratch_shapes=[pltpu.VMEM((2, 32, rows), F32)],
        compiler_params=pltpu.CompilerParams(vmem_limit_bytes=VMEM_LIMIT),
        cost_estimate=pl.CostEstimate(
            flops=10 * 10 * rows * rows * LANES, bytes_accessed=10 * rows * width, transcendentals=10 * rows * rows
        ),
        name="far_early",
    )(y1, y2, w, r1, s1)


def far_pairs(y1, y2, w, r1, r2, s1, s2, pq, pk):
    rows, width = y2.shape
    half = width // 2
    count = half // LANES
    heads = 2 * count

    def body(y1, y2, w, r1, r2, s1, s2, pq, pk, swap1, out1, swap2, la, l2, info):
        z = lax.axis_index("ctx")
        tail = pl.ds(width, LANES)

        def scalars(slot, head):
            return info[slot, head : head + 1, :], info[slot, heads + head : heads + head + 1, :]

        def before(ref, at):
            return ref[:, at : at + LANES].astype(F32)

        def corner(query_2, query_3, key_0, key_1, c, head):
            first, other = both(key_0, 0, half)(c), both(key_1, 0, half)(c)
            key, value = (jnp.concatenate(x, axis=0) for x in zip(first, other))
            third = pair_terms(*both(query_3, 0, half)(c), key, value, *scalars(1, head))
            second = pair_terms(*both(query_2, 0, half)(c), *first, *scalars(0, head))
            key_1_terms = third[1][rows:] + before(pk, c * LANES), third[2][rows:] + before(pk, half + c * LANES)
            key_0_terms = third[1][:rows] + second[1], third[2][:rows] + second[2]
            return second[0] + before(pq, c * LANES), third[0], key_0_terms, key_1_terms

        @pl.when(z == 1)
        def _():
            for slot, ref in enumerate((s1, s2, y1)):
                info[slot] = token_rows(ref[:, tail], heads)
            for c in range(count):
                a, b = c * LANES, half + c * LANES
                own = pair_terms(*both(w, 0, width)(c), *both(r2, 0, half)(c), *scalars(2, c))
                query_2, query_3, key_0, key_1 = corner(s1, s2, r2, y2, c, c)
                put(swap1, a, query_3)
                put(swap2, a, query_2)
                put(out1, a, key_0[0] + own[1])
                put(out1, b, key_0[1] + own[2])
                put(l2, a, key_1[0])
                put(l2, b, key_1[1])
                put(la, a, own[0])

        @pl.when(z == 2)
        def _():
            for slot, ref in enumerate((y1, r1)):
                info[slot] = token_rows(ref[:, tail], heads)
            for c in range(count):
                a, b = c * LANES, half + c * LANES
                own = pair_terms(*both(r2, 0, half)(c), *both(w, half, width)(c), *scalars(1, count + c))
                query_2, query_3, key_0, key_1 = corner(y2, r2, s2, s1, c, count + c)
                put(swap1, a, key_0[0])
                put(swap1, b, key_0[1])
                put(swap2, a, key_1[0])
                put(swap2, b, key_1[1])
                put(out1, a, query_3 + own[0])
                put(l2, a, query_2)
                put(la, a, own[1])
                put(la, b, own[2])

    single = jax.ShapeDtypeStruct((rows, width), BF16)
    return pl.pallas_call(
        body,
        out_shape=[single] * 5,
        in_specs=in_vmem(9),
        out_specs=in_vmem(5),
        scratch_shapes=[pltpu.VMEM((3, 32, rows), F32)],
        compiler_params=pltpu.CompilerParams(vmem_limit_bytes=VMEM_LIMIT),
        cost_estimate=pl.CostEstimate(
            flops=20 * 10 * rows * rows * LANES, bytes_accessed=30 * rows * width, transcendentals=20 * rows * rows
        ),
        name="far_pairs",
    )(y1, y2, w, r1, r2, s1, s2, pq, pk)


def near_pairs(y1, y2, w, from_pair, from_swap):
    rows, width = y2.shape
    half = width // 2
    count = half // LANES
    heads = 2 * count
    total = rows + EDGE

    def body(y1, y2, w, from_pair, from_swap, dw, dy1, dy2, to_pair, to_swap, info):
        z = lax.axis_index("ctx")
        even = z % 2 == 0

        def edge_part(at):
            pair, swap = from_pair[:, at : at + LANES], from_swap[:, at : at + LANES]
            return jnp.where(even, pair, swap), jnp.where(even, swap, pair)

        tail = pl.ds(width, LANES)
        key_tail, query_tail = edge_part(2 * width)
        info[...] = token_rows(jnp.concatenate([y1[:, tail], query_tail], axis=0), heads)
        key_meta = jnp.concatenate([y1[:, tail], key_tail], axis=0).astype(F32)
        id_lane = lax.broadcasted_iota(jnp.int32, (total, LANES), 1) == 3 * heads
        key_ids = jnp.sum(jnp.where(id_lane, key_meta, 0.0), axis=1, keepdims=True)
        at_key = lax.broadcasted_iota(jnp.int32, (total, total), 0)
        at_query = lax.broadcasted_iota(jnp.int32, (total, total), 1)
        last_key = jnp.where(z < 3, total, rows)
        last_query = jnp.where(z > 0, total, rows)
        visible = (key_ids <= info[2 * heads : 2 * heads + 1, :]) & ((at_key < rows) | (at_query < rows - EDGE))
        visible = visible & (at_key < last_key) & (at_query < last_query)

        def head_terms(i, c, payload):
            a, b = i * half + c * LANES, width + i * half + c * LANES
            small, large = c * LANES, half + c * LANES
            wide = w[:, a : a + LANES], w[:, b : b + LANES]
            narrow = payload[:, small : small + LANES], payload[:, large : large + LANES]
            edge_k, edge_q = zip(edge_part(a), edge_part(b))

            def terms(queries, keys):
                query, grad = (jnp.concatenate(x, axis=0) for x in zip(queries, edge_q))
                key, value = (jnp.concatenate(x, axis=0) for x in zip(keys, edge_k))
                scalars = info[i * count + c : i * count + c + 1, :], info[heads + i * count + c : heads + i * count + c + 1, :]
                made = [x.astype(BF16) for x in pair_terms(query, grad, key, value, *scalars, visible)]
                query_end, key_end, value_end = (x[rows:] for x in made)
                to_pair[:, a : a + LANES] = jnp.where(even, key_end, query_end)
                to_swap[:, a : a + LANES] = jnp.where(even, query_end, key_end)
                to_pair[:, b : b + LANES] = value_end
                to_swap[:, b : b + LANES] = value_end
                return [x[:rows] for x in made]

            return a, b, small, large, wide, narrow, terms

        @pl.when(z < 2)
        def _():
            for i, (payload, result) in enumerate(((y2, dy2), (y1, dy1))):
                for c in range(count):
                    a, b, small, large, wide, narrow, terms = head_terms(i, c, payload)
                    query_term, key_term, value_term = terms(wide, narrow)
                    dw[:, a : a + LANES] = query_term
                    result[:, small : small + LANES] = key_term
                    result[:, large : large + LANES] = value_term

        @pl.when(z >= 2)
        def _():
            for i, (payload, result) in enumerate(((y1, dy1), (y2, dy2))):
                for c in range(count):
                    a, b, small, large, wide, narrow, terms = head_terms(i, c, payload)
                    query_term, key_term, value_term = terms(narrow, wide)
                    result[:, small : small + LANES] = query_term
                    dw[:, a : a + LANES] = key_term
                    dw[:, b : b + LANES] = value_term

    return pl.pallas_call(
        body,
        out_shape=[
            jax.ShapeDtypeStruct((rows, 2 * width), BF16),
            jax.ShapeDtypeStruct((rows, width), BF16),
            jax.ShapeDtypeStruct((rows, width), BF16),
            jax.ShapeDtypeStruct((EDGE, 2 * width), BF16),
            jax.ShapeDtypeStruct((EDGE, 2 * width), BF16),
        ],
        in_specs=in_vmem(5),
        out_specs=in_vmem(5),
        scratch_shapes=[pltpu.VMEM((32, total), F32)],
        compiler_params=pltpu.CompilerParams(vmem_limit_bytes=VMEM_LIMIT),
        cost_estimate=pl.CostEstimate(
            flops=10 * 10 * rows * rows * LANES, bytes_accessed=16 * rows * width, transcendentals=10 * rows * rows
        ),
        name="near_pairs",
    )(y1, y2, w, from_pair, from_swap)


def finish_first(dw, la, lo, dy2, l2, out1, from_pair, from_swap, groups):
    rows, width = dy2.shape
    half = width // 2
    share = rows // groups

    def body(dw, la, lo, dy2, l2, out1, dp, ds, *refs):
        outs, v, e, sems = refs[:groups], *refs[groups:]
        here = lax.axis_index("head")
        z = lax.axis_index("ctx")
        low, middle = z < 2, (z == 1) | (z == 2)
        after_first, before_last, odd = z > 0, z < 3, z % 2 == 1

        def own(i):
            at, there = pl.ds(i * half, half), pl.ds(i // 2 * half, half)
            active, other = la[:, there].astype(F32), lo[:, there].astype(F32)
            one, two = (active, other) if i % 2 == 0 else (other, active)
            return dw[:, at].astype(F32) + jnp.where(middle, jnp.where(z == 1, one, two), 0.0)

        def second(cols):
            return dy2[:, cols].astype(F32) + jnp.where(middle, l2[:, cols], out1[:, cols]).astype(F32)

        def put(dst, cols, total, first, last=None):
            end = total[rows - EDGE :] if last is None else total[rows - EDGE :] + last
            total = jnp.concatenate([total[:EDGE] + first, total[EDGE : rows - EDGE], end], axis=0)
            for h in range(groups):
                dst[h, :, cols] = total[h * share : (h + 1) * share].astype(BF16)

        def key_edge(cols):
            return jnp.where(after_first, jnp.where(odd, dp[:, cols], ds[:, cols]).astype(F32), 0.0)

        def query_edge(cols):
            return jnp.where(before_last, jnp.where(odd, ds[:, cols], dp[:, cols]).astype(F32), 0.0)

        a, b = pl.ds(0, half), pl.ds(half, half)
        c, d = pl.ds(width, half), pl.ds(width + half, half)
        for i, cols in enumerate((a, b)):
            put(e, cols, own(i), jnp.where(low, 0.0, key_edge(cols)), jnp.where(low, query_edge(cols), 0.0))
        put(e, c, second(a), jnp.where(low, key_edge(a), 0.0), jnp.where(low, 0.0, query_edge(b)))
        put(e, d, jnp.where(low, second(b), own(2)), key_edge(c))
        made = run_copies([(e.at[here ^ m], outs[m]) for m in range(groups)], sems)
        left_over = own(3)
        left_over = jnp.concatenate([left_over[:EDGE] + key_edge(d), left_over[EDGE:]], axis=0)
        v[...] = left_over.astype(BF16)
        wait_all(made)

    return pl.pallas_call(
        body,
        out_shape=[jax.ShapeDtypeStruct((share, 2 * width), BF16)] * groups + [jax.ShapeDtypeStruct((rows, half), BF16)],
        in_specs=in_vmem(8),
        out_specs=anywhere(groups) + [pl.BlockSpec(memory_space=pltpu.VMEM)],
        scratch_shapes=[pltpu.VMEM((groups, share, 2 * width), BF16), pltpu.SemaphoreType.DMA((groups,))],
        compiler_params=pltpu.CompilerParams(vmem_limit_bytes=VMEM_SMALL),
        cost_estimate=pl.CostEstimate(flops=0, bytes_accessed=16 * rows * width, transcendentals=0),
        name="finish_first",
    )(dw, la, lo, dy2, l2, out1, from_pair, from_swap)


def finish_second(dy1, swap2, out2, v, from_pair, from_swap, groups):
    rows, width = dy1.shape
    half = width // 2
    share = rows // groups

    def body(dy1, swap2, out2, v, dp, ds, *refs):
        outs, e, sems = refs[:groups], *refs[groups:]
        here, z = lax.axis_index("head"), lax.axis_index("ctx")
        low, middle = z < 2, (z == 1) | (z == 2)

        def put(cols, whole):
            for h in range(groups):
                e[h, :, cols] = whole[h * share : (h + 1) * share].astype(BF16)

        a, b = pl.ds(0, half), pl.ds(half, half)
        end = pl.ds(width + half, half)

        def total(cols):
            return dy1[:, cols].astype(F32) + jnp.where(middle, swap2[:, cols], out2[:, cols]).astype(F32)

        left = total(a)
        first = left[:EDGE] + jnp.where(z == 1, dp[:, b].astype(F32), 0.0)
        last = left[rows - EDGE :] + jnp.where(z == 2, dp[:, a].astype(F32), 0.0)
        put(a, jnp.concatenate([first, left[EDGE : rows - EDGE], last], axis=0))
        right = total(b)
        right = jnp.concatenate([right[:EDGE] + jnp.where(z == 1, dp[:, end].astype(F32), 0.0), right[EDGE:]], axis=0)
        put(b, jnp.where(low, right, v[...].astype(F32)))
        wait_all(run_copies([(e.at[here ^ m], outs[m]) for m in range(groups)], sems))

    return pl.pallas_call(
        body,
        out_shape=[jax.ShapeDtypeStruct((share, width), BF16)] * groups,
        in_specs=[pl.BlockSpec(memory_space=pltpu.VMEM)] * 6,
        out_specs=anywhere(groups),
        scratch_shapes=[pltpu.VMEM((groups, share, width), BF16), pltpu.SemaphoreType.DMA((groups,))],
        compiler_params=pltpu.CompilerParams(vmem_limit_bytes=VMEM_SMALL),
        cost_estimate=pl.CostEstimate(flops=0, bytes_accessed=9 * rows * width, transcendentals=0),
        name="finish_second",
    )(dy1, swap2, out2, v, from_pair, from_swap)


def unpack_early(parts):
    groups = len(parts)
    rows = parts[0].shape[0]
    width = parts[0].shape[1] // 2
    half = width // 2

    def body(*refs):
        dq, dk, dv, first, second, third, sems = refs[groups:]
        here, low = lax.axis_index("head"), lax.axis_index("ctx") < 2
        todo = []
        for m in range(groups):
            base = pl.multiple_of((here ^ m) * width, LANES)
            place = pl.multiple_of(base + jnp.where(low, 0, half), LANES)
            todo.append((refs[m].at[:, pl.ds(0, width)], first.at[:, pl.ds(base, width)]))
            todo.append((refs[m].at[:, pl.ds(width, half)], second.at[:, pl.ds(place, half)]))
            todo.append((refs[m].at[:, pl.ds(width + half, half)], third.at[:, pl.ds(base, half)]))
        wait_all(run_copies(todo, sems))

        @pl.when(low)
        def _():
            wait_all(run_copies([(first, dq), (second, dk), (third, dv)], sems))

        @pl.when(jnp.logical_not(low))
        def _():
            wait_all(run_copies([(first, dk), (second, dq), (third, dv)], sems))

    shape = jax.ShapeDtypeStruct((rows, groups * width), BF16)
    return pl.pallas_call(
        body,
        out_shape=[shape] * 3,
        in_specs=anywhere(groups),
        out_specs=anywhere(3),
        scratch_shapes=[pltpu.VMEM(shape.shape, BF16)] * 3 + [pltpu.SemaphoreType.DMA((3 * groups,))],
        cost_estimate=pl.CostEstimate(flops=0, bytes_accessed=10 * rows * groups * width, transcendentals=0),
        compiler_params=pltpu.CompilerParams(vmem_limit_bytes=VMEM_SMALL),
        name="unpack_early",
    )(*parts)


def unpack_late(parts, dq, dk, dv):
    groups = len(parts)
    rows, width = parts[0].shape
    half = width // 2

    def body(*refs):
        dq, dk, dv, sems = refs[groups + 3 :]
        here, low = lax.axis_index("head"), lax.axis_index("ctx") < 2

        def moves(far, near):
            todo = []
            for m in range(groups):
                base = pl.multiple_of((here ^ m) * width, LANES)
                todo.append((refs[m].at[:, pl.ds(0, half)], far.at[:, pl.ds(base + near, half)]))
                todo.append((refs[m].at[:, pl.ds(half, half)], dv.at[:, pl.ds(base + half, half)]))
            return todo

        @pl.when(low)
        def _():
            wait_all(run_copies(moves(dk, half), sems))

        @pl.when(jnp.logical_not(low))
        def _():
            wait_all(run_copies(moves(dq, 0), sems))

    shape = jax.ShapeDtypeStruct(dq.shape, BF16)
    return pl.pallas_call(
        body,
        out_shape=[shape] * 3,
        in_specs=in_vmem(groups) + anywhere(3),
        out_specs=anywhere(3),
        scratch_shapes=[pltpu.SemaphoreType.DMA((2 * groups,))],
        input_output_aliases={groups: 0, groups + 1: 1, groups + 2: 2},
        compiler_params=pltpu.CompilerParams(vmem_limit_bytes=VMEM_SMALL),
        cost_estimate=pl.CostEstimate(flops=0, bytes_accessed=8 * rows * groups * width, transcendentals=0),
        name="unpack_late",
    )(*parts, dq, dk, dv)


def after(array, other):
    return lax.optimization_barrier((array, other))[0]


def local_split(queries, keys_in, values_in, attn_out, out_grad, log_norm, span_id):
    groups = lax.axis_size("head")
    width = queries.shape[1] // groups

    def swapped(parts):
        return [parts[0]] + [
            lax.ppermute(parts[m], "head", [(i, i ^ m) for i in range(groups)]) for m in range(1, groups)
        ]

    x1, x2, x3 = pack(queries, keys_in, values_in, attn_out, out_grad, span_id.reshape(1, -1), groups, width)
    x1, x2 = swapped(x1), swapped(x2)
    y1 = join_first(x1, log_norm.T)
    y1, x2[1], x2[2] = lax.optimization_barrier((y1, x2[1], x2[2]))
    r1 = lax.ppermute(y1, "ctx", PAIRS)
    s1 = lax.ppermute(y1, "ctx", SWAP)
    x3 = swapped(x3)
    y2 = join(x2)
    y2, r1, s1, x3[:-1] = lax.optimization_barrier((y2, r1, s1, x3[:-1]))
    r2 = lax.ppermute(y2, "ctx", PAIRS)
    s2 = lax.ppermute(r1, "ctx", SWAP)
    w, from_pair, from_swap = join_last(x3, y1, y2)
    from_pair = lax.ppermute(from_pair, "ctx", PAIRS)
    from_swap = lax.ppermute(from_swap, "ctx", SWAP)
    pq, pk, lo, l3 = far_early(y1, y2, w, r1, s1)
    w, from_pair, from_swap = lax.optimization_barrier((w, from_pair, from_swap))
    swap1, out1, swap2, la, l2 = far_pairs(y1, y2, w, r1, r2, s1, s2, pq, pk)
    dw, dy1, dy2, to_pair, to_swap = near_pairs(y1, y2, w, after(from_pair, l2), from_swap)
    swap1 = lax.ppermute(swap1, "ctx", SWAP)
    out1 = lax.ppermute(out1, "ctx", PAIRS)
    to_pair = lax.ppermute(to_pair, "ctx", PAIRS)
    to_swap = lax.ppermute(to_swap, "ctx", SWAP)
    swap1, swap2, out1, to_pair, to_swap = lax.optimization_barrier((swap1, swap2, out1, to_pair, to_swap))
    swap2 = lax.ppermute(swap2, "ctx", SWAP)
    out2 = lax.ppermute((swap1.astype(F32) + l3.astype(F32)).astype(BF16), "ctx", PAIRS)
    *early, kept = finish_first(dw, la, lo, dy2, l2, out1, to_pair, to_swap, groups)
    early = swapped(early)
    late = swapped(finish_second(dy1, swap2, out2, kept, to_pair, to_swap, groups))
    return tuple(unpack_late(late, *unpack_early(early)))


def splits(tokens, blocks, head_width, heads):
    if blocks != 4 or heads % 2 or head_width != LANES or 6 * heads + 1 > LANES:
        return False
    block = tokens // blocks
    span = -(-tokens // SPANS)
    for offset in range(SPANS * span - tokens + 1):
        for end in range(block, tokens, block):
            start = (end - 1 + offset) // span * span - offset
            if min(end - start, start + span - end) > EDGE or max(end - start, span) > block:
                return False
    return block % EDGE == 0


def local(queries, keys_in, values_in, attn_out, out_grad, log_norm, span_id):
    blocks, groups = lax.axis_size("ctx"), lax.axis_size("head")
    heads = log_norm.shape[1]
    tokens = queries.shape[0] * blocks * groups
    plan = local_plain
    if groups & (groups - 1) == 0 and splits(tokens, blocks, queries.shape[1] // (heads * groups), heads):
        plan = local_split
    return plan(queries, keys_in, values_in, attn_out, out_grad, log_norm, span_id)


def solution(mesh):
    placed = (
        P(("clip", "ctx", "head"), None),
        P(("clip", "ctx", "head"), None),
        P(("clip", "ctx", "head"), None),
        P(("clip", "ctx", "head"), None),
        P(("clip", "ctx", "head"), None),
        P(("clip", "ctx"), "head"),
        P(("clip", "ctx", "head")),
    )
    return jax.shard_map(
        local,
        mesh=mesh,
        in_specs=placed,
        out_specs=(
            P(("clip", "ctx", "head"), None),
            P(("clip", "ctx", "head"), None),
            P(("clip", "ctx", "head"), None),
        ),
        check_vma=False,
    )
```
